32 devices in a mesh: lat: 8 (over z, x), lon: 4 (over y, core).
Axes of the slice: x: 2, y: 2, z: 4, core: 2. Of those that a mesh axis runs over, the one named last changes fastest.
Arguments:
- state: float32 [64, 1440, 256], P('lat', 'lon'), may hold values from -6 to 6
- filter_flag: int32 [64], P('lat'), may hold values from 0 to 1, as said below
- cutoff: int32 [64], P('lat'), may hold values from 2 to 179
Outputs:
- state_new: float32 [64, 1440, 256], P('lat', 'lon')
The draws below stay inside these ranges and needn't reach their ends.
Inputs may be any that keep to these rules, and one draw needn't show every extreme that they name: `filter_flag`: row j is flagged exactly when j < S or j >= 32 + S, for one S between 8 and 24.
All inputs are finite; a program needn't handle non-finite values.
Results may differ from the reference program's by a relative error of at most 0.000057.
Values sent between devices are 32-bit elements; how exact they have to be, the bound alone decides.
No kernel may reach another device: no remote copies, remote signals or barrier semaphores. Data moves between devices by JAX's collectives and lax.ppermute only.
A program may use at most 64 MiB of HBM per device.

```python
import math
import jax
import jax.numpy as jnp

NLON = 1440
LEV = 64
NLAT = 64


def draw_filter_flag(key, part):
    split = jax.random.randint(key, (), NLAT // 8, 3 * NLAT // 8 + 1)
    index = jnp.arange(NLAT)
    return ((index < split) | (index >= NLAT // 2 + split)).astype(jnp.int32)


def with_ends(values, stream_key, least, top_value):
    shape = values.shape
    spot = [jax.random.randint(jax.random.fold_in(stream_key, axis), (), 0, shape[axis]) for axis in range(len(shape))]
    values = values.at[tuple(spot)].set(least)
    longest = shape.index(max(shape))
    spot[longest] = (spot[longest] + 1) % shape[longest]
    return values.at[tuple(spot)].set(top_value)


def level_of(own_key, shape, pieces, least, top_value):
    factor_of = 1.0
    for axis_at, shards_of in pieces:
        heights = jax.random.uniform(jax.random.fold_in(jax.random.fold_in(own_key, 6), axis_at), (shards_of,), jnp.float32, least / len(pieces), top_value / len(pieces))
        factor_of = factor_of * jnp.repeat(jnp.exp(heights), shape[axis_at] // shards_of).reshape((-1,) + (1,) * (len(shape) - 1 - axis_at))
    return factor_of


def normal_values(own_key, dims, scale, limit, cuts=(), kind=jnp.bfloat16):
    gain = level_of(own_key, dims, cuts, -0.22, 0.18) if cuts else 1.0
    result = jax.random.normal(own_key, dims, jnp.float32) * scale * gain
    return jnp.minimum(jnp.maximum(result, -limit), limit).astype(kind)


def setup_inputs(seed: int = 0) -> dict:
    key_list = jax.random.split(jax.random.key(seed), 4)
    return {
        "state": normal_values(key_list[0], (NLAT, NLON, 4 * LEV), 1.0, 6.0, ((0, 8), (1, 4)), jnp.float32),
        "filter_flag": draw_filter_flag(jax.random.fold_in(key_list[3], 71), 0),
        "cutoff": with_ends(jax.random.randint(key_list[2], (NLAT,), 2, NLON // 8), jax.random.fold_in(key_list[2], 1), 2, (NLON // 8) - 1).astype(jnp.int32),
    }


WIND_COEF = 0.03
VERT_COEF = 0.2
PRESS_COEF = 0.03


def row_cosines(count):
    index = jnp.arange(count).astype(jnp.float32)
    return jnp.cos(-0.5 * math.pi + (index + 0.5) * math.pi / count)


def polar_filter(field, filter_flag, cutoff):
    width = field.shape[1]
    spectra = jnp.fft.rfft(field, axis=1)
    waves = jnp.arange(width // 2 + 1).astype(jnp.float32)
    ratio = cutoff.astype(jnp.float32)[:, None] / jnp.maximum(waves, 1.0)[None, :]
    damping = jnp.minimum(1.0, ratio * ratio)
    smooth = jnp.fft.irfft(spectra * damping[:, :, None], n=width, axis=1).astype(field.dtype)
    return jnp.where(filter_flag[:, None, None] == 1, smooth, field)


def level_diff(field):
    padded = jnp.pad(field, ((0, 0), (0, 0), (1, 1)))
    return 0.5 * (padded[:, :, 2:] - padded[:, :, :-2])


def reference(state, filter_flag, cutoff):
    levels = state.shape[2] // 4
    zonal_wind = state[:, :, :levels]
    merid_wind = state[:, :, levels:2 * levels]
    vert_wind = state[:, :, 2 * levels:3 * levels]
    pressure = state[:, :, 3 * levels:]
    nlat = state.shape[0]
    cos_rows = row_cosines(nlat)[:, None, None]
    grad_x = (jnp.roll(pressure, -1, 1) - jnp.roll(pressure, 1, 1)) / (2.0 * cos_rows)
    padded = jnp.pad(pressure, ((1, 1), (0, 0), (0, 0)))
    grad_y = 0.5 * (padded[2:] - padded[:-2])
    grad_z = level_diff(pressure)
    zonal_new = polar_filter(zonal_wind - WIND_COEF * grad_x, filter_flag, cutoff)
    merid_new = polar_filter(merid_wind - WIND_COEF * grad_y, filter_flag, cutoff)
    vert_new = vert_wind - VERT_COEF * grad_z
    div_x = (jnp.roll(zonal_new, -1, 1) - jnp.roll(zonal_new, 1, 1)) / (2.0 * cos_rows)
    flux = jnp.pad(merid_new * cos_rows, ((1, 1), (0, 0), (0, 0)))
    div_y = (flux[2:] - flux[:-2]) / (2.0 * cos_rows)
    div_z = level_diff(vert_new)
    press_mid = pressure - PRESS_COEF * (div_x + div_y + div_z)
    press_new = polar_filter(press_mid, filter_flag, cutoff)
    return jnp.concatenate([zonal_new, merid_new, vert_new, press_new], 2)
```

```python
import functools
import math

import jax
import jax.numpy as jnp
import numpy as np
from jax import lax
from jax.experimental import pallas as pl
from jax.experimental.pallas import tpu as pltpu
from jax.sharding import PartitionSpec as P

WIND_COEF = 0.03
VERT_COEF = 0.2
PRESS_COEF = 0.03
LANES = 128
VMEM_BYTES = 40 * 1024 * 1024
F32 = jnp.float32
BF16 = jnp.bfloat16


def split_np(table):
    high = table.astype(np.float32).astype(jnp.bfloat16)
    low = (table - high.astype(np.float64)).astype(np.float32).astype(jnp.bfloat16)
    return high, low


def round_up(value, step):
    return -(-value // step) * step


@functools.lru_cache(maxsize=None)
def spectral_plan(nlon):
    quarter = nlon // 4
    points = np.arange(quarter)
    waves0 = np.arange(0, nlon // 2 + 1, 4)
    waves2 = np.arange(2, nlon // 2 + 1, 4)
    waves1 = np.arange(1, nlon // 2 + 1, 2)
    size0 = round_up(len(waves0), 16)
    size2 = round_up(len(waves2), 16)
    size1 = round_up(len(waves1), 8)

    def trig(waves, size):
        angle = 2.0 * np.pi * ((waves[:, None] * points[None, :]) % nlon) / nlon
        cos_t, sin_t = np.zeros((2, size, quarter))
        cos_t[: len(waves)] = np.cos(angle)
        sin_t[: len(waves)] = np.sin(angle)
        return cos_t, sin_t

    def padded(values, size):
        out = np.zeros(size)
        out[: len(values)] = values
        return out

    def weights(waves, size):
        ends = (waves == 0) | (2 * waves == nlon)
        return padded(np.where(ends, 1.0, 2.0) / nlon, size)

    cos0, sin0 = trig(waves0, size0)
    cos2, sin2 = trig(waves2, size2)
    cos1, sin1 = trig(waves1, size1)
    turn = padded(np.where(waves1 % 4 == 1, 1.0, -1.0), size1)[:, None]
    fwd0 = np.concatenate([cos0, sin0], 0)
    fwd2 = np.concatenate([cos2, sin2], 0)
    fwd1 = np.block([[cos1, -turn * sin1], [sin1, turn * cos1]])
    inv0 = (fwd0 * np.tile(weights(waves0, size0), 2)[:, None]).T
    inv2 = (fwd2 * np.tile(weights(waves2, size2), 2)[:, None]).T
    inv1 = (fwd1 * np.tile(weights(waves1, size1), 2)[:, None]).T
    forward = [part for table in (fwd0, fwd2, fwd1) for part in split_np(table)]
    inverse = [part for table in (inv0, inv2, inv1) for part in split_np(table)]

    def columns(waves, size):
        inv_wave = padded(1.0 / np.maximum(waves, 1), size)
        delta = padded(np.sin(2.0 * np.pi * waves / nlon), size)
        return np.concatenate([inv_wave, inv_wave]), np.concatenate([delta, -delta])

    per_wave = [columns(w, s) for w, s in ((waves0, size0), (waves2, size2), (waves1, size1))]
    mode = np.stack([np.concatenate([c[0] for c in per_wave]), np.concatenate([c[1] for c in per_wave])], 1)
    mode = np.pad(mode.astype(np.float32), ((0, 0), (0, LANES - 2)))
    return forward, inverse, mode, (size0, size2, size1)


@functools.lru_cache(maxsize=None)
def row_cosines(nlat):
    index = np.arange(-1, nlat + 1).astype(np.float32)
    angle = np.float32(-0.5 * math.pi) + (index + np.float32(0.5)) * np.float32(math.pi) / np.float32(nlat)
    return np.cos(angle.astype(np.float64)).astype(np.float32)


def lane_ids(shape):
    return lax.broadcasted_iota(jnp.int32, shape, len(shape) - 1)


def level_diff_at(tile, start, levels, lanes):
    up = jnp.where(lanes == start + levels - 1, 0.0, pltpu.roll(tile, LANES - 1, 1))
    down = jnp.where(lanes == start, 0.0, pltpu.roll(tile, 1, 1))
    return 0.5 * (up - down)


def pack_row(refs, value, row, start, part, me, lanes):
    group = lanes // part == row
    for step, ref in enumerate(refs):
        shift = lax.rem(row * part - start - part * (me ^ step) + 2 * LANES, LANES)
        moved = pltpu.roll(value, shift, 1)
        width = ref.shape[1]
        if row == 0:
            ref[...] = moved[:, :width]
        else:
            ref[...] = jnp.where(group, moved, jnp.pad(ref[...], ((0, 0), (0, LANES - width))))[:, :width]


def press_kernel(levels, part, tile_ref, *refs):
    packs, (north_ref, south_ref, west_ref, east_ref) = refs[:-4], refs[-4:]
    rows, width, _ = tile_ref.shape
    me = lax.axis_index("lon")
    lanes = lane_ids((width, LANES))
    for row in range(rows):
        tile = tile_ref[row]
        press_low = pltpu.roll(tile, levels, 1)
        vert_new = tile - VERT_COEF * level_diff_at(press_low, 0, levels, lanes)
        div_z = level_diff_at(vert_new, 0, levels, lanes)
        value = press_low - PRESS_COEF * div_z
        pack_row(packs, value, row, 0, part, me, lanes)
        west_ref[row : row + 1] = tile[0:1]
        east_ref[row : row + 1] = tile[width - 1 : width]
    south_ref[...] = tile_ref[0]
    north_ref[...] = tile_ref[rows - 1]


def zonal_kernel(levels, part, cos_ref, wind_ref, tile_ref, west_ref, east_ref, *packs):
    rows, width, _ = tile_ref.shape
    me = lax.axis_index("lon")
    first = lax.axis_index("lat") * rows
    lanes = lane_ids((width, LANES))
    place = lax.broadcasted_iota(jnp.int32, (width, LANES), 0)
    for row in range(rows):
        press = tile_ref[row]
        after = jnp.where(place == width - 1, east_ref[row : row + 1], pltpu.roll(press, width - 1, 0))
        before = jnp.where(place == 0, west_ref[row : row + 1], pltpu.roll(press, 1, 0))
        scale = WIND_COEF / (2.0 * jnp.full((1, LANES), cos_ref[first + row + 1], F32))
        value = wind_ref[row] - pltpu.roll((after - before) * scale, levels, 1)
        pack_row(packs, value, row, 0, part, me, lanes)


def merid_kernel(levels, part, wind_ref, tile_ref, south_ref, north_ref, *packs):
    rows, width, _ = tile_ref.shape
    me = lax.axis_index("lon")
    lanes = lane_ids((width, LANES))
    for row in range(rows):
        above = north_ref[...] if row == rows - 1 else tile_ref[row + 1]
        below = south_ref[...] if row == 0 else tile_ref[row - 1]
        value = wind_ref[row] - (0.5 * WIND_COEF) * (above - below)
        pack_row(packs, value, row, levels, part, me, lanes)


def dot3(table_high, table_low, value):
    high = value.astype(BF16)
    low = (value - high.astype(F32)).astype(BF16)
    width = value.shape[1]
    dot = functools.partial(jnp.dot, preferred_element_type=F32)
    if width % LANES == 0:
        both = dot(table_high[...], jnp.concatenate([high, low], 1))
        both = both[:, :width] + both[:, width:]
    else:
        both = dot(table_high[...], high) + dot(table_high[...], low)
    return both + dot(table_low[...], high)


def turn_lanes(value, shift):
    width = value.shape[1]
    shift %= width
    if shift == 0:
        return value
    if width % LANES == 0:
        return pltpu.roll(value, shift, 1)
    return jnp.concatenate([value[:, width - shift :], value[:, : width - shift]], 1)


def forward_dft(quarters, tables, order):
    own, core, chip, far = [ref[...] for ref in quarters]
    if order:
        me = lax.axis_index("lon")
        odd = lax.rem(me, 2) == 1
        sign_y = jnp.where(me >= 2, -1.0, 1.0).astype(F32)
        sign_c = jnp.where(odd, -1.0, 1.0).astype(F32)
    sum0, sum1 = own + chip, core + far
    dif0, dif1 = own - chip, core - far
    total, other = sum0 + sum1, sum0 - sum1
    if order:
        other = other * sign_c
        dif0, dif1 = jnp.where(odd, dif1, dif0) * sign_y, jnp.where(odd, dif0, dif1) * sign_y
    return (
        dot3(tables[0], tables[1], total),
        dot3(tables[2], tables[3], other),
        dot3(tables[4], tables[5], jnp.concatenate([dif0, dif1], 0)),
    )


def inverse_dft(parts, tables, order, outs):
    even = dot3(tables[0], tables[1], parts[0])
    other = dot3(tables[2], tables[3], parts[1])
    both = dot3(tables[4], tables[5], parts[2])
    quarter = even.shape[0]
    dif0, dif1 = both[:quarter], both[quarter:]
    if order:
        me = lax.axis_index("lon")
        odd = lax.rem(me, 2) == 1
        sign_y = jnp.where(me >= 2, -1.0, 1.0).astype(F32)
        sign_c = jnp.where(odd, -1.0, 1.0).astype(F32)
        other = other * sign_c
        dif0, dif1 = jnp.where(odd, dif1, dif0) * sign_y, jnp.where(odd, dif0, dif1) * sign_y
    plus, minus = even + other, even - other
    outs[0][...] = plus + dif0
    outs[1][...] = minus + dif1
    outs[2][...] = plus - dif0
    outs[3][...] = minus - dif1


def lane_rows(pick, rows, part, width):
    group = lane_ids((1, width)) // part
    out = jnp.zeros((1, width), F32)
    for row in range(rows):
        out = jnp.where(group == row, pick(row), out)
    return out


def damping(flag_ref, cut_ref, mode, nlon, part):
    rows = flag_ref.shape[0]

    def pick(row):
        return jnp.where(flag_ref[row] == 1, cut_ref[row], nlon).astype(F32)

    width = rows * part
    ratio = lane_rows(pick, rows, part, width) * mode[:, 0:1]
    return jnp.minimum(1.0, ratio * ratio)


def spec_kernel(order, bounds, q0, q1, q2, q3, *refs):
    tables, spec_ref = refs[:6], refs[6]
    for bound, value in zip(bounds, forward_dft((q0, q1, q2, q3), tables, order)):
        spec_ref[bound[0] : bound[1]] = value


def wind_kernel(order, bounds, part, edges, flag_ref, cut_ref, mode_ref, q0, q1, q2, q3, *refs):
    forward, inverse, outs, spec_ref = refs[:6], refs[6:12], refs[12:16], refs[16]
    nlon = 4 * q0.shape[0]
    damp = damping(flag_ref, cut_ref, mode_ref[...], nlon, part)
    parts = forward_dft((q0, q1, q2, q3), forward, order)
    parts = [value * damp[b[0] : b[1]] for b, value in zip(bounds, parts)]
    for bound, value in zip(bounds, parts):
        spec_ref[bound[0] : bound[1]] = value
    inverse_dft(parts, inverse, order, outs)
    if edges:
        south_ref, north_ref = refs[17:]
        width = spec_ref.shape[1]
        count = width // part
        chunk = south_ref.shape[0]
        group = lane_ids((chunk, width)) // part
        for ref, source in ((south_ref, 0), (north_ref, count - 1)):
            for piece in range(count):
                lines = min(chunk, spec_ref.shape[0] - piece * chunk)
                value = spec_ref[piece * chunk : piece * chunk + lines]
                if lines < chunk:
                    value = jnp.concatenate([value, jnp.zeros((chunk - lines, width), F32)], 0)
                moved = turn_lanes(value, (piece - source) * part)
                if piece == 0:
                    ref[...] = moved
                else:
                    ref[...] = jnp.where(group == piece, moved, ref[...])


def final_press_kernel(
    order, bounds, part, flag_ref, cut_ref, cos_ref, mode_ref, spec_ref, zonal_ref, merid_ref, south_ref, north_ref, *refs
):
    inverse, outs = refs[:6], refs[6:10]
    rows = flag_ref.shape[0]
    width = spec_ref.shape[1]
    nlon = 4 * inverse[0].shape[0]
    first = lax.axis_index("lat") * rows
    chunk = south_ref.shape[0]

    mode = mode_ref[...]
    damp = damping(flag_ref, cut_ref, mode, nlon, part)
    cosine = lane_rows(lambda row: cos_ref[first + row + 1], rows, part, width)
    below = cos_ref[first]
    above = cos_ref[first + rows + 1]
    half_inv = 0.5 / cosine
    group = lane_ids((1, width)) // part

    def halo(ref, target):
        pieces = []
        for piece in range(rows):
            pieces.append(turn_lanes(ref[...], (target - piece) * part))
        return jnp.concatenate(pieces, 0)[: spec_ref.shape[0]]

    flux = merid_ref[...] * cosine
    north = jnp.where(group == rows - 1, halo(north_ref, rows - 1) * above, turn_lanes(flux, -part))
    south = jnp.where(group == 0, halo(south_ref, 0) * below, turn_lanes(flux, part))
    div_y = (north - south) * half_inv
    zonal = zonal_ref[...]
    slope = mode[:, 1:2] / cosine
    parts = []
    for bound in bounds:
        low, high = bound
        mid = (low + high) // 2
        swapped = jnp.concatenate([zonal[mid:high], zonal[low:mid]], 0)
        div = swapped * slope[low:high] + div_y[low:high]
        parts.append((spec_ref[low:high] - PRESS_COEF * div) * damp[low:high])
    inverse_dft(parts, inverse, order, outs)


def unpack_row(refs, row, start, part, me, lanes, base):
    out = base
    for step, ref in enumerate(refs):
        owner = me ^ step
        first = start + part * owner
        value = ref[...]
        if value.shape[1] < LANES:
            value = jnp.pad(value, ((0, 0), (0, LANES - value.shape[1])))
        moved = pltpu.roll(value, lax.rem(first - row * part + 2 * LANES, LANES), 1)
        out = jnp.where((lanes >= first) & (lanes < first + part), moved, out)
    return out


def winds_out_kernel(levels, part, count, *refs):
    zonal, merid, out_ref = refs[:count], refs[count : 2 * count], refs[2 * count]
    rows, width, _ = out_ref.shape
    me = lax.axis_index("lon")
    lanes = lane_ids((width, LANES))
    for row in range(rows):
        value = unpack_row(zonal, row, 0, part, me, lanes, jnp.zeros((width, LANES), F32))
        out_ref[row] = unpack_row(merid, row, levels, part, me, lanes, value)


def press_out_kernel(levels, part, count, _, tile_ref, *refs):
    press, out_ref = refs[:count], refs[count]
    rows, width, _ = out_ref.shape
    me = lax.axis_index("lon")
    lanes = lane_ids((width, LANES))
    for row in range(rows):
        tile = tile_ref[row]
        press_low = pltpu.roll(tile, levels, 1)
        vert_new = tile - VERT_COEF * level_diff_at(press_low, 0, levels, lanes)
        out_ref[row] = unpack_row(press, row, levels, part, me, lanes, vert_new)


def whole(shape):
    return pl.BlockSpec(shape, lambda step: (0,) * len(shape))


def tile_of(shape, index):
    return pl.BlockSpec((shape[0], shape[1], LANES), lambda step: (0, 0, index))


SMEM = pl.BlockSpec(memory_space=pltpu.SMEM)


def call(kernel, out_shape, in_specs, out_specs, cost, **more):
    flops, moved = cost
    return pl.pallas_call(
        kernel,
        grid=(1,),
        out_shape=out_shape,
        in_specs=in_specs,
        out_specs=out_specs,
        compiler_params=pltpu.CompilerParams(vmem_limit_bytes=VMEM_BYTES),
        cost_estimate=pl.CostEstimate(flops=flops, bytes_accessed=moved, transcendentals=0),
        **more,
    )


def f32(*shape):
    return jax.ShapeDtypeStruct(shape, F32)


def body(state, filter_flag, cutoff):
    rows, width, depth = state.shape
    levels = depth // 4
    count = lax.axis_size("lon")
    bands = lax.axis_size("lat")
    nlon = width * count
    part = levels // count
    packed = rows * part
    forward, inverse, mode, sizes = spectral_plan(nlon)
    cosines = jnp.asarray(row_cosines(rows * bands))
    forward = [jnp.asarray(t) for t in forward]
    inverse = [jnp.asarray(t) for t in inverse]
    mode = jnp.asarray(mode)
    bounds, at = [], 0
    for size in sizes:
        bounds.append((at, at + 2 * size))
        at += 2 * size
    spectrum = at
    order = count == 4
    table_specs = [whole(t.shape) for t in forward]
    inverse_specs = [whole(t.shape) for t in inverse]
    state_bytes = state.size * 4
    block = whole((width, packed))
    edge = whole((width, LANES))
    side = whole((rows, LANES))
    low_tile, high_tile = tile_of(state.shape, 0), tile_of(state.shape, 1)
    packs = [f32(width, packed)] * count
    quarter = whole((nlon // 4, packed))
    quarters = [f32(nlon // 4, packed)] * 4

    def exchange(blocks):
        out = [blocks[0]]
        for step in range(1, count):
            pairs = [(i, i ^ step) for i in range(count)]
            out.append(lax.ppermute(blocks[step], "lon", pairs))
        return out

    def to_quarters(blocks):
        if order:
            return blocks
        me = lax.axis_index("lon")
        ring = jnp.stack(blocks)[me ^ jnp.arange(count)].reshape(4, nlon // 4, packed)
        return [ring[i] for i in range(4)]

    def from_quarters(parts):
        if order:
            return parts
        me = lax.axis_index("lon")
        ring = jnp.stack(parts).reshape(count, width, packed)[me ^ jnp.arange(count)]
        return [ring[i] for i in range(count)]

    def lat_halo(to_north, to_south):
        up = [(i, i + 1) for i in range(bands - 1)]
        down = [(i + 1, i) for i in range(bands - 1)]
        return lax.ppermute(to_north, "lat", up), lax.ppermute(to_south, "lat", down)

    *press_packs, to_north, to_south, to_west, to_east = call(
        functools.partial(press_kernel, levels, part),
        packs + [f32(width, LANES)] * 2 + [f32(rows, LANES)] * 2,
        [high_tile],
        [block] * count + [edge] * 2 + [side] * 2,
        (20 * state.size, state_bytes),
    )(state)
    press_circle = exchange(press_packs)
    east = [(i, (i + 1) % count) for i in range(count)]
    west = [((i + 1) % count, i) for i in range(count)]
    from_west = lax.ppermute(to_east, "lon", east)
    from_east = lax.ppermute(to_west, "lon", west)
    from_south, from_north = lat_halo(to_north, to_south)

    zonal_packs = call(
        functools.partial(zonal_kernel, levels, part),
        packs,
        [SMEM, low_tile, high_tile, side, side],
        [block] * count,
        (20 * state.size, 2 * state_bytes),
    )(cosines, state, state, from_west, from_east)
    zonal_circle = exchange(zonal_packs)
    merid_packs = call(
        functools.partial(merid_kernel, levels, part),
        packs,
        [low_tile, high_tile, edge, edge],
        [block] * count,
        (20 * state.size, 2 * state_bytes),
    )(state, state, from_south, from_north)
    merid_circle = exchange(merid_packs)

    dft_cost = 6 * sum(t.size for t in forward[::2]) * packed
    table_bytes = sum(t.size * 2 for t in forward)
    press_spec = call(
        functools.partial(spec_kernel, order, bounds),
        f32(spectrum, packed),
        [quarter] * 4 + table_specs,
        whole((spectrum, packed)),
        (dft_cost, table_bytes + 2 * spectrum * packed * 4),
    )(*to_quarters(press_circle), *forward)

    chunk = round_up(-(-spectrum // rows), 8)

    def wind(circle, edges):
        return call(
            functools.partial(wind_kernel, order, bounds, part, edges),
            quarters + [f32(spectrum, packed)] + [f32(chunk, packed)] * (2 if edges else 0),
            [SMEM, SMEM, whole(mode.shape)] + [quarter] * 4 + table_specs + inverse_specs,
            [quarter] * 4 + [whole((spectrum, packed))] + [whole((chunk, packed))] * (2 if edges else 0),
            (2 * dft_cost, 2 * table_bytes + 4 * spectrum * packed * 4),
        )(filter_flag, cutoff, mode, *to_quarters(circle), *forward, *inverse)

    *zonal_parts, zonal_spec = wind(zonal_circle, False)
    zonal_back = exchange(from_quarters(zonal_parts))
    *merid_parts, merid_spec, spec_to_south, spec_to_north = wind(merid_circle, True)
    spec_south, spec_north = lat_halo(spec_to_north, spec_to_south)
    merid_back = exchange(from_quarters(merid_parts))

    press_parts = call(
        functools.partial(final_press_kernel, order, bounds, part),
        quarters,
        [SMEM] * 3 + [whole(mode.shape)] + [whole((spectrum, packed))] * 3 + [whole((chunk, packed))] * 2 + inverse_specs,
        [quarter] * 4,
        (dft_cost, table_bytes + 5 * spectrum * packed * 4),
    )(filter_flag, cutoff, cosines, mode, press_spec, zonal_spec, merid_spec, spec_south, spec_north, *inverse)
    press_back = exchange(from_quarters(press_parts))

    out = call(
        functools.partial(winds_out_kernel, levels, part, count),
        f32(*state.shape),
        [block] * (2 * count),
        low_tile,
        (20 * state.size, state_bytes),
    )(*zonal_back, *merid_back)
    return call(
        functools.partial(press_out_kernel, levels, part, count),
        f32(*state.shape),
        [pl.BlockSpec(memory_space=pl.ANY), high_tile] + [block] * count,
        high_tile,
        (20 * state.size, state_bytes),
        input_output_aliases={0: 0},
    )(out, state, *press_back)


def solution(mesh):
    return jax.shard_map(
        body,
        mesh=mesh,
        in_specs=(P("lat", "lon", None), P("lat"), P("lat")),
        out_specs=P("lat", "lon", None),
        check_vma=False,
    )
```

```python
import functools
import math

import jax
import jax.numpy as jnp
import numpy as np
from jax import lax
from jax.experimental import pallas as pl
from jax.experimental.pallas import tpu as pltpu
from jax.sharding import PartitionSpec as P

WIND_COEF = 0.03
VERT_COEF = 0.2
PRESS_COEF = 0.03
LANES = 128
VMEM_BYTES = 40 * 1024 * 1024
FIRST = 3
MERID = 2
ZONAL_SPEC = 4
F32 = jnp.float32
BF16 = jnp.bfloat16


def split_np(table):
    high = table.astype(np.float32).astype(jnp.bfloat16)
    low = (table - high.astype(np.float64)).astype(np.float32).astype(jnp.bfloat16)
    return high, low


def round_up(value, step):
    return -(-value // step) * step


@functools.lru_cache(maxsize=None)
def spectral_plan(nlon):
    quarter = nlon // 4
    points = np.arange(quarter)
    waves0 = np.arange(0, nlon // 2 + 1, 4)
    waves2 = np.arange(2, nlon // 2 + 1, 4)
    waves1 = np.arange(1, nlon // 2 + 1, 2)
    size0 = round_up(len(waves0), 16)
    size2 = round_up(len(waves2), 16)
    size1 = round_up(len(waves1), 8)

    def trig(waves, size):
        angle = 2.0 * np.pi * ((waves[:, None] * points[None, :]) % nlon) / nlon
        cos_t, sin_t = np.zeros((2, size, quarter))
        cos_t[: len(waves)] = np.cos(angle)
        sin_t[: len(waves)] = np.sin(angle)
        return cos_t, sin_t

    def padded(values, size):
        out = np.zeros(size)
        out[: len(values)] = values
        return out

    def weights(waves, size):
        ends = (waves == 0) | (2 * waves == nlon)
        return padded(np.where(ends, 1.0, 2.0) / nlon, size)

    cos0, sin0 = trig(waves0, size0)
    cos2, sin2 = trig(waves2, size2)
    cos1, sin1 = trig(waves1, size1)
    turn = padded(np.where(waves1 % 4 == 1, 1.0, -1.0), size1)[:, None]
    fwd0 = np.concatenate([cos0, sin0], 0)
    fwd2 = np.concatenate([cos2, sin2], 0)
    fwd1 = np.block([[cos1, -turn * sin1], [sin1, turn * cos1]])
    inv0 = (fwd0 * np.tile(weights(waves0, size0), 2)[:, None]).T
    inv2 = (fwd2 * np.tile(weights(waves2, size2), 2)[:, None]).T
    inv1 = (fwd1 * np.tile(weights(waves1, size1), 2)[:, None]).T
    forward = [part for table in (fwd0, fwd2, fwd1) for part in split_np(table)]
    inverse = [part for table in (inv0, inv2, inv1) for part in split_np(table)]

    def columns(waves, size):
        inv_wave = padded(1.0 / np.maximum(waves, 1), size)
        delta = padded(np.sin(2.0 * np.pi * waves / nlon), size)
        return np.concatenate([inv_wave, inv_wave]), np.concatenate([delta, -delta])

    per_wave = [columns(w, s) for w, s in ((waves0, size0), (waves2, size2), (waves1, size1))]
    mode = np.stack([np.concatenate([c[0] for c in per_wave]), np.concatenate([c[1] for c in per_wave])], 1)
    mode = np.pad(mode.astype(np.float32), ((0, 0), (0, LANES - 2)))
    return forward, inverse, mode, (size0, size2, size1)


def lane_ids(shape):
    return lax.broadcasted_iota(jnp.int32, shape, len(shape) - 1)


def select_groups(values, masks):
    out = values[0]
    for mask, value in zip(masks[1:], values[1:]):
        out = jnp.where(mask, value, out)
    return out


def group_masks(size, part):
    group = lane_ids((size, LANES)) // part
    return [group == g for g in range(LANES // part)]


def transpose_groups(tiles, masks, part, wanted):
    count = len(tiles)
    turned = []
    for shift in range(count):
        mixed = select_groups([tiles[(shift + g) % count] for g in range(count)], masks)
        turned.append(pltpu.roll(mixed, shift * part, 1) if shift else mixed)
    return [select_groups([turned[(h - g) % count] for h in range(count)], masks) for g in wanted]


def partner_order(blocks, me):
    odd, far = lax.rem(me, 2) == 1, me >= 2
    a, b, c, d = blocks
    a, b, c, d = jnp.where(odd, b, a), jnp.where(odd, a, b), jnp.where(odd, d, c), jnp.where(odd, c, d)
    return [jnp.where(far, c, a), jnp.where(far, d, b), jnp.where(far, a, c), jnp.where(far, b, d)]


def chunk_of(size):
    return next(c for c in (24, 40, 16, 8) if size % c == 0)


def cut_value(flag_ref, cut_ref, row, nlon):
    return jnp.where(flag_ref[row] == 1, cut_ref[row], nlon).astype(F32)


def row_cosine(row, count):
    return jnp.sin((row.astype(F32) + 0.5) * (math.pi / count))


def levels_table(levels):
    shape = (2 * levels, 2 * levels)
    source = lax.broadcasted_iota(jnp.int32, shape, 0)
    target = lax.broadcasted_iota(jnp.int32, shape, 1)
    step = source % levels - target % levels
    diff = jnp.where(step == 1, 1.0, jnp.where(step == -1, -1.0, 0.0))
    rim = (target % levels == 0) | (target % levels == levels - 1)
    twice = jnp.where(step == 0, jnp.where(rim, -1.0, -2.0), jnp.where(abs(step) == 2, 1.0, 0.0))
    from_press, to_press = source >= levels, target >= levels
    table = jnp.where(from_press, jnp.where(to_press, twice, diff), jnp.where(to_press, -10.0 * diff, 0.0))
    return table.astype(BF16)


def first_kernel(part, wind_ref, tile_ref, *refs):
    packs, (vert_ref, both_ref) = refs[:4], refs[4:]
    rows, width, _ = tile_ref.shape
    levels = LANES // 2
    nlat = rows * lax.axis_size("lat")
    me = lax.axis_index("lon")
    first = lax.axis_index("lat") * rows
    low = lane_ids((width, LANES)) < levels
    place = lax.broadcasted_iota(jnp.int32, (width, LANES), 0)
    gain = jnp.where(lane_ids((1, LANES)) < levels, -0.5 * VERT_COEF, 0.25 * PRESS_COEF * VERT_COEF)
    table = levels_table(levels)
    dot = functools.partial(jnp.dot, preferred_element_type=F32)
    for row in range(rows):
        tile = tile_ref[row]
        high = tile.astype(BF16)
        rest = (tile - high.astype(F32)).astype(BF16)
        mixed = tile + gain * (dot(high, table) + dot(rest, table))
        vert_ref[row] = mixed
        after = jnp.where(place == width - 1, 0.0, pltpu.roll(tile, width - 1, 0))
        before = jnp.where(place == 0, 0.0, pltpu.roll(tile, 1, 0))
        scale = WIND_COEF / (2.0 * row_cosine(jnp.full((1, LANES), first + row), nlat))
        zonal = wind_ref[row] - pltpu.roll((after - before) * scale, levels, 1)
        both_ref[row] = jnp.where(low, zonal, mixed)

    size = chunk_of(width)
    masks = group_masks(size, part)

    def pack(step, carry):
        start = pl.multiple_of(step * size, 8)
        lines = pl.ds(start, size)
        blocks = transpose_groups([both_ref[row, lines] for row in range(rows)], masks, part, range(8))
        for ref, value in zip(packs, partner_order(blocks[4:], me)):
            ref[lines] = value
        for ref, value in zip(packs, partner_order(blocks[:4], me)):
            ref[pl.ds(start + width, size)] = value
        return carry

    lax.fori_loop(0, width // size, pack, 0)
    line = lax.broadcasted_iota(jnp.int32, (8, LANES), 0)
    sides = []
    for row in range(rows):
        side = jnp.where(line == 0, tile_ref[row, 0:8], 0.0)
        sides.append(jnp.where(line == 7, tile_ref[row, width - 8 : width], side))
    blocks = transpose_groups(sides, group_masks(8, part), part, range(4, 8))
    for ref, value in zip(packs, partner_order(blocks, me)):
        ref[2 * width :] = value


def rim_kernel(flag_ref, cut_ref, wind_ref, tile_ref, _, north_ref, south_ref):
    rows, width, _ = tile_ref.shape
    levels = LANES // 2
    nlon = width * lax.axis_size("lon")
    low = lane_ids((width, LANES)) < levels
    half = 0.5 * WIND_COEF
    last = rows - 1
    rim = wind_ref[last] + half * tile_ref[last - 1]
    north_ref[:width] = jnp.where(low, pltpu.roll(rim, levels, 1), tile_ref[last])
    rim = wind_ref[0] - half * tile_ref[1]
    south_ref[:width] = jnp.where(low, pltpu.roll(rim, levels, 1), tile_ref[0])
    north_ref[width:] = jnp.full((8, LANES), cut_value(flag_ref, cut_ref, last, nlon), F32)
    south_ref[width:] = jnp.full((8, LANES), cut_value(flag_ref, cut_ref, 0, nlon), F32)


def merid_kernel(part, wind_ref, tile_ref, south_ref, north_ref, *refs):
    outs, (merid_ref, rim_ref) = refs[:4], refs[4:]
    rows, width, _ = tile_ref.shape
    levels = LANES // 2
    me = lax.axis_index("lon")
    half = 0.5 * WIND_COEF
    for row in range(rows):
        above = north_ref[:width] if row == rows - 1 else tile_ref[row + 1]
        below = south_ref[:width] if row == 0 else tile_ref[row - 1]
        merid_ref[row] = wind_ref[row] - half * (above - below)
    lines = rim_ref.shape[1] // 4
    rim_ref[0, :width] = south_ref[:width] - half * pltpu.roll(tile_ref[0], levels, 1)
    rim_ref[1, :width] = north_ref[:width] + half * pltpu.roll(tile_ref[rows - 1], levels, 1)
    rim_ref[:, width:] = jnp.zeros((2, 4 * lines - width, LANES), F32)

    size = chunk_of(width)
    masks = group_masks(size, part)

    def pack(step, carry):
        where = pl.ds(pl.multiple_of(step * size, 8), size)
        blocks = transpose_groups([merid_ref[row, where] for row in range(rows)], masks, part, range(4, 8))
        for ref, value in zip(outs, partner_order(blocks, me)):
            ref[where] = value
        return carry

    lax.fori_loop(0, width // size, pack, 0)
    size = chunk_of(lines)
    masks = group_masks(size, part)
    for at in range(0, lines, size):
        tiles = [rim_ref[g % 2, g // 2 * lines + at : g // 2 * lines + at + size] for g in range(8)]
        blocks = transpose_groups(tiles, masks, part, range(4))
        for ref, value in zip(outs, partner_order(blocks, me)):
            ref[width + at : width + at + size] = value


def dot3(table_high, table_low, value):
    high = value.astype(BF16)
    low = (value - high.astype(F32)).astype(BF16)
    width = value.shape[1]
    dot = functools.partial(jnp.dot, preferred_element_type=F32)
    both = dot(table_high[...], jnp.concatenate([high, low], 1))
    return both[:, :width] + both[:, width:] + dot(table_low[...], high)


def by_place(me, dif0, dif1):
    odd = lax.rem(me, 2) == 1
    sign = jnp.where(me >= 2, -1.0, 1.0).astype(F32)
    return jnp.where(odd, dif1, dif0) * sign, jnp.where(odd, dif0, dif1) * sign


def parity_sign(me):
    return jnp.where(lax.rem(me, 2) == 1, -1.0, 1.0).astype(F32)


def forward_dft(quarters, tables):
    me = lax.axis_index("lon")
    own, core, chip, far = quarters
    sum0, sum1 = own + chip, core + far
    dif0, dif1 = by_place(me, own - chip, core - far)
    return (
        dot3(tables[0], tables[1], sum0 + sum1),
        dot3(tables[2], tables[3], (sum0 - sum1) * parity_sign(me)),
        dot3(tables[4], tables[5], jnp.concatenate([dif0, dif1], 0)),
    )


def inverse_dft(parts, tables, outs):
    me = lax.axis_index("lon")
    even = dot3(tables[0], tables[1], parts[0])
    other = dot3(tables[2], tables[3], parts[1]) * parity_sign(me)
    both = dot3(tables[4], tables[5], parts[2])
    quarter = even.shape[0]
    dif0, dif1 = by_place(me, both[:quarter], both[quarter:])
    plus, minus = even + other, even - other
    outs[0][...] = plus + dif0
    outs[1][...] = minus + dif1
    outs[2][...] = plus - dif0
    outs[3][...] = minus - dif1


def lane_rows(pick, rows, part):
    group = lane_ids((1, LANES)) // part
    out = jnp.zeros((1, LANES), F32)
    for row in range(rows):
        out = jnp.where(group == row, pick(row), out)
    return out


def lane_cut(flag_ref, cut_ref, nlon, part):
    rows = flag_ref.shape[0]
    return lane_rows(lambda row: cut_value(flag_ref, cut_ref, row, nlon), rows, part)


def lane_cosine(shift, rows, part):
    row = lane_ids((1, LANES)) // part + lax.axis_index("lat") * rows + shift
    return row_cosine(row, rows * lax.axis_size("lat"))


def damping(cut, inv_wave):
    ratio = cut * inv_wave
    return jnp.minimum(1.0, ratio * ratio)


def zonal_spec_kernel(bounds, part, flag_ref, cut_ref, mode_ref, q0, q1, q2, q3, *refs):
    forward, inverse, outs, (press_ref, spec_ref) = refs[:6], refs[6:12], refs[12:16], refs[16:]
    rows = flag_ref.shape[0]
    width = outs[0].shape[0]
    me = lax.axis_index("lon")
    quarters = (q0, q1, q2, q3)
    scale = WIND_COEF / (2.0 * lane_cosine(0, rows, part))
    line = lax.broadcasted_iota(jnp.int32, (8, LANES), 0)
    sides = partner_order([q[2 * width :] for q in quarters], me)
    starts = [jnp.where(line == 0, scale * pltpu.roll(sides[(q + 3) % 4], 1, 0), 0.0) for q in range(4)]
    ends = [jnp.where(line == 7, scale * pltpu.roll(sides[(q + 1) % 4], 7, 0), 0.0) for q in range(4)]
    starts, ends = partner_order(starts, me), partner_order(ends, me)
    fields = []
    for q, start, end in zip(quarters, starts, ends):
        middle = q[width + 8 : 2 * width - 8]
        zonal = jnp.concatenate([q[width : width + 8] + start, middle, q[2 * width - 8 : 2 * width] - end], 0)
        fields.append(jnp.concatenate([q[:width], zonal], 1))
    damp = damping(lane_cut(flag_ref, cut_ref, 4 * width, part), mode_ref[:, 0:1])
    parts = []
    for (low, high), value in zip(bounds, forward_dft(fields, forward)):
        press_ref[low:high] = value[:, :LANES]
        parts.append(value[:, LANES:] * damp[low:high])
        spec_ref[low:high] = parts[-1]
    inverse_dft(parts, inverse, outs)


def merid_spec_kernel(bounds, part, flag_ref, cut_ref, mode_ref, south_ref, north_ref, q0, q1, q2, q3, *refs):
    forward, inverse, outs, (spec_ref, rim_ref) = refs[:6], refs[6:12], refs[12:16], refs[16:]
    width = outs[0].shape[0]
    fields = []
    for q in (q0, q1, q2, q3):
        value = q[width:]
        pieces = [pltpu.roll(value, LANES - 2 * part * g, 1) if g else value for g in range(4)]
        fields.append(jnp.concatenate([q[:width], jnp.concatenate(pieces, 0)[:width]], 1))
    group = lane_ids((1, LANES)) // part
    rim_cut = jnp.where(group == 0, south_ref[0:1], jnp.where(group == 1, north_ref[0:1], 0.0))
    inv_wave = mode_ref[:, 0:1]
    damp = damping(lane_cut(flag_ref, cut_ref, 4 * width, part), inv_wave)
    rim_damp = damping(rim_cut, inv_wave)
    parts = []
    for (low, high), value in zip(bounds, forward_dft(fields, forward)):
        rim_ref[low:high] = value[:, LANES:] * rim_damp[low:high]
        parts.append(value[:, :LANES] * damp[low:high])
        spec_ref[low:high] = parts[-1]
    inverse_dft(parts, inverse, outs)


def press_back_kernel(bounds, part, flag_ref, cut_ref, mode_ref, spec_ref, zonal_ref, merid_ref, rim_ref, *refs):
    inverse, outs = refs[:6], refs[6:10]
    rows = flag_ref.shape[0]
    nlon = 4 * inverse[0].shape[0]
    band = lax.axis_index("lat")
    mode = mode_ref[...]
    damp = damping(lane_cut(flag_ref, cut_ref, nlon, part), mode[:, 0:1])
    cosine = lane_cosine(0, rows, part)
    below = jnp.where(band == 0, 0.0, lane_cosine(-1, rows, part))
    above = jnp.where(band == lax.axis_size("lat") - 1, 0.0, lane_cosine(1, rows, part))
    half_inv = 0.5 / cosine
    group = lane_ids((1, LANES)) // part
    flux = merid_ref[...] * cosine
    rim = rim_ref[...]
    north = jnp.where(group == rows - 1, pltpu.roll(rim, (rows - 2) * part, 1) * above, pltpu.roll(flux, LANES - part, 1))
    south = jnp.where(group == 0, rim * below, pltpu.roll(flux, part, 1))
    div_y = (north - south) * half_inv
    zonal = zonal_ref[...]
    slope = mode[:, 1:2] / cosine
    parts = []
    for low, high in bounds:
        mid = (low + high) // 2
        swapped = jnp.concatenate([zonal[mid:high], zonal[low:mid]], 0)
        div = swapped * slope[low:high] + div_y[low:high]
        parts.append((spec_ref[low:high] - PRESS_COEF * div) * damp[low:high])
    inverse_dft(parts, inverse, outs)


def winds_out_kernel(part, *refs):
    blocks, out_ref = refs[:8], refs[8]
    rows, width, _ = out_ref.shape
    me = lax.axis_index("lon")
    size = chunk_of(width)
    masks = group_masks(size, part)

    def unpack(step, carry):
        lines = pl.ds(pl.multiple_of(step * size, 8), size)
        values = [ref[lines] for ref in blocks]
        values = partner_order(values[:4], me) + partner_order(values[4:], me)
        for row, value in enumerate(transpose_groups(values, masks, part, range(rows))):
            out_ref[row, lines] = value
        return carry

    lax.fori_loop(0, width // size, unpack, 0)


def press_out_kernel(part, _, tile_ref, *refs):
    blocks, out_ref = refs[:4], refs[4]
    rows, width, _ = out_ref.shape
    me = lax.axis_index("lon")
    size = chunk_of(width)
    masks = group_masks(size, part)
    low = lane_ids((size, LANES)) < LANES // 2

    def unpack(step, carry):
        lines = pl.ds(pl.multiple_of(step * size, 8), size)
        values = partner_order([ref[lines] for ref in blocks], me)
        for row, value in enumerate(transpose_groups(values + values, masks, part, range(rows))):
            out_ref[row, lines] = jnp.where(low, tile_ref[row, lines], value)
        return carry

    lax.fori_loop(0, width // size, unpack, 0)


def whole(shape):
    return pl.BlockSpec(shape, lambda step: (0,) * len(shape))


def tile_of(shape, index):
    return pl.BlockSpec((shape[0], shape[1], LANES), lambda step: (0, 0, index))


SMEM = pl.BlockSpec(memory_space=pltpu.SMEM)
ANY = pl.BlockSpec(memory_space=pl.ANY)


def call(kernel, out_shape, in_specs, out_specs, cost=1, grid=(1,), **more):
    return pl.pallas_call(
        kernel,
        grid=grid,
        out_shape=out_shape,
        in_specs=in_specs,
        out_specs=out_specs,
        compiler_params=pltpu.CompilerParams(vmem_limit_bytes=VMEM_BYTES),
        cost_estimate=pl.CostEstimate(flops=0, bytes_accessed=int(cost * 3.69e6), transcendentals=0),
        **more,
    )


def f32(*shape):
    return jax.ShapeDtypeStruct(shape, F32)


def exchange(blocks):
    pairs = [[(i, i ^ step) for i in range(4)] for step in range(4)]
    return [blocks[0]] + [lax.ppermute(blocks[step], "lon", pairs[step]) for step in range(1, 4)]


def packed_body(state, filter_flag, cutoff):
    rows, width, depth = state.shape
    levels = depth // 4
    bands = lax.axis_size("lat")
    nlon = 4 * width
    part = levels // 4
    forward, inverse, mode, sizes = spectral_plan(nlon)
    forward = [jnp.asarray(t) for t in forward]
    inverse = [jnp.asarray(t) for t in inverse]
    mode = jnp.asarray(mode)
    bounds, at = [], 0
    for size in sizes:
        bounds.append((at, at + 2 * size))
        at += 2 * size
    table_specs = [whole(t.shape) for t in forward] + [whole(t.shape) for t in inverse]
    block, spectrum = (width, LANES), (at, LANES)
    sided = (width + 8, LANES)
    rimmed = (width + round_up(-(-width // 4), 8), LANES)
    double = (2 * width + 8, LANES)
    full = (rows, width, LANES)
    low_tile, high_tile = tile_of(state.shape, 0), tile_of(state.shape, 1)

    *packs, vert = call(
        functools.partial(first_kernel, part),
        [f32(*double)] * 4 + [f32(*full)],
        [low_tile, high_tile],
        [whole(double)] * 4 + [whole(full)],
        cost=FIRST,
        scratch_shapes=[pltpu.VMEM(full, F32)],
    )(state, state)
    circle = exchange(packs)
    to_north, to_south = call(
        rim_kernel,
        [f32(*sided)] * 2,
        [SMEM] * 2 + [low_tile, high_tile, ANY],
        [whole(sided)] * 2,
    )(filter_flag, cutoff, state, state, vert)
    from_south = lax.ppermute(to_north, "lat", [(i, i + 1) for i in range(bands - 1)])
    from_north = lax.ppermute(to_south, "lat", [(i + 1, i) for i in range(bands - 1)])

    merid_packs = call(
        functools.partial(merid_kernel, part),
        [f32(*rimmed)] * 4,
        [low_tile, high_tile, whole(sided), whole(sided)],
        [whole(rimmed)] * 4,
        cost=MERID,
        scratch_shapes=[pltpu.VMEM(full, F32), pltpu.VMEM((2, 4 * (rimmed[0] - width), LANES), F32)],
    )(state, state, from_south, from_north)
    merid_circle = exchange(merid_packs)

    *zonal_parts, press_spec, zonal_spec = call(
        functools.partial(zonal_spec_kernel, bounds, part),
        [f32(*block)] * 4 + [f32(*spectrum)] * 2,
        [SMEM] * 2 + [whole(mode.shape)] + [whole(double)] * 4 + table_specs,
        [whole(block)] * 4 + [whole(spectrum)] * 2,
        cost=ZONAL_SPEC,
    )(filter_flag, cutoff, mode, *circle, *forward, *inverse)
    zonal_back = exchange(zonal_parts)

    last_lines = pl.BlockSpec((8, LANES), lambda step: (width // 8, 0))
    *merid_parts, merid_spec, rim_spec = call(
        functools.partial(merid_spec_kernel, bounds, part),
        [f32(*block)] * 4 + [f32(*spectrum)] * 2,
        [SMEM] * 2 + [whole(mode.shape), last_lines, last_lines] + [whole(rimmed)] * 4 + table_specs,
        [whole(block)] * 4 + [whole(spectrum)] * 2,
    )(filter_flag, cutoff, mode, from_south, from_north, *merid_circle, *forward, *inverse)
    merid_back = exchange(merid_parts)

    press_parts = call(
        functools.partial(press_back_kernel, bounds, part),
        [f32(*block)] * 4,
        [SMEM] * 2 + [whole(mode.shape)] + [whole(spectrum)] * 4 + table_specs[6:],
        [whole(block)] * 4,
    )(filter_flag, cutoff, mode, press_spec, zonal_spec, merid_spec, rim_spec, *inverse)
    press_back = exchange(press_parts)

    steps = next(s for s in (3, 5, 1) if width % (8 * s) == 0)
    piece = pl.BlockSpec((width // steps, LANES), lambda step: (step, 0))

    def slab(index):
        return pl.BlockSpec((rows, width // steps, LANES), lambda step: (0, step, index))

    out = call(
        functools.partial(winds_out_kernel, part),
        f32(*state.shape),
        [piece] * 8,
        slab(0),
        grid=(steps,),
    )(*zonal_back, *merid_back)
    return call(
        functools.partial(press_out_kernel, part),
        f32(*state.shape),
        [ANY, slab(0)] + [piece] * 4,
        slab(1),
        grid=(steps,),
        input_output_aliases={0: 0},
    )(out, vert, *press_back)


def padded_2(block, sides, width, periodic):
    for axis, dim in sides:
        count = lax.axis_size(axis)
        forward = [(i, i + 1) for i in range(count - 1)]
        if periodic:
            forward.append((count - 1, 0))
        backward = [(target, source) for source, target in forward]
        low = lax.ppermute(
            lax.slice_in_dim(block, block.shape[dim] - width, None, axis=dim), axis, forward
        )
        high = lax.ppermute(lax.slice_in_dim(block, 0, width, axis=dim), axis, backward)
        block = jnp.concatenate([low, block, high], axis=dim)
    return block


def dft_tables(width):
    points = jnp.arange(width, dtype=jnp.int32)
    waves = jnp.arange(width // 2 + 1, dtype=jnp.int32)
    phase = points[:, None] * waves[None, :] % width
    angle = phase.astype(jnp.float32) * (2.0 * math.pi / width)
    weights = jnp.where((waves == 0) | (waves * 2 == width), 1.0, 2.0).astype(jnp.float32) / width
    return (jnp.cos(angle), jnp.sin(angle), weights)


def rims(stack):
    wide = padded_2(stack, (("lon", 1),), 1, True)
    return padded_2(wide, (("lat", 0),), 1, False)


def level_diff(field):
    padded = jnp.pad(field, ((0, 0), (0, 0), (1, 1)))
    return 0.5 * (padded[:, :, 2:] - padded[:, :, :-2])


def damped(block, cut_vec, tables):
    cos_table, sin_table, weights = tables
    highest = lax.Precision.HIGHEST
    wave_vals = jnp.arange(cos_table.shape[1]).astype(jnp.float32)
    ratio = cut_vec[:, None] / jnp.maximum(wave_vals, 1.0)[None, :]
    damping = (jnp.minimum(1.0, ratio * ratio) * weights[None, :])[:, None, :]
    real_part = jnp.einsum("rnq,nk->rqk", block, cos_table, precision=highest)
    imag_part = jnp.einsum("rnq,nk->rqk", block, sin_table, precision=highest)
    restored = jnp.einsum("rqk,nk->rnq", real_part * damping, cos_table, precision=highest)
    return restored + jnp.einsum("rqk,nk->rnq", imag_part * damping, sin_table, precision=highest)


def circle_local(fields, cut_rows, tables):
    return damped(fields, cut_rows, tables)


def polar(fields, row_flag, cut_rows, tables, apply):
    smooth = apply(fields, cut_rows, tables)
    return jnp.where(row_flag[:, None, None], smooth, fields)


def plain_body(state, filter_flag, cutoff):
    rows, width, depth = state.shape
    levels = depth // 4
    zonal_wind = state[:, :, :levels]
    merid_wind = state[:, :, levels : 2 * levels]
    vert_wind = state[:, :, 2 * levels : 3 * levels]
    pressure = state[:, :, 3 * levels :]
    nlat = rows * lax.axis_size("lat")
    nlon = width * lax.axis_size("lon")
    offset = lax.axis_index("lat") * rows
    row_ids = (offset + jnp.arange(-1, rows + 1)).astype(jnp.float32)
    cos_ext = jnp.cos(-0.5 * math.pi + (row_ids + 0.5) * math.pi / nlat)
    cos_mid = cos_ext[1:-1][:, None, None]
    tables = dft_tables(nlon)
    row_flag = filter_flag == 1
    cut_rows = cutoff.astype(jnp.float32)
    padded = rims(pressure)
    grad_x = (padded[1:-1, 2:] - padded[1:-1, :-2]) / (2.0 * cos_mid)
    grad_y = 0.5 * (padded[2:, 1:-1] - padded[:-2, 1:-1])
    grad_z = level_diff(pressure)
    zonal_pre = zonal_wind - WIND_COEF * grad_x
    merid_pre = merid_wind - WIND_COEF * grad_y
    vert_new = vert_wind - VERT_COEF * grad_z
    div_z = level_diff(vert_new)
    outgoing = jnp.stack([zonal_pre, merid_pre, pressure, div_z], 3).reshape(
        rows, width, 4 * levels
    )
    circles = lax.all_to_all(outgoing, "lon", split_axis=2, concat_axis=1, tiled=True)
    part_levels = circles.shape[2] // 4
    circles = circles.reshape(rows, nlon, part_levels, 4)
    winds_c = jnp.concatenate([circles[:, :, :, 0], circles[:, :, :, 1]], 2)
    press_c = circles[:, :, :, 2]
    div_z_c = circles[:, :, :, 3]
    winds_c = polar(winds_c, row_flag, cut_rows, tables, circle_local)
    zonal_c = winds_c[:, :, :part_levels]
    merid_c = winds_c[:, :, part_levels:]
    div_x = (jnp.roll(zonal_c, -1, 1) - jnp.roll(zonal_c, 1, 1)) / (2.0 * cos_mid)
    flux = padded_2(merid_c * cos_mid, (("lat", 0),), 1, False)
    div_y = (flux[2:] - flux[:-2]) / (2.0 * cos_mid)
    press_mid = press_c - PRESS_COEF * (div_x + div_y + div_z_c)
    press_c = polar(press_mid, row_flag, cut_rows, tables, circle_local)
    back = jnp.stack([zonal_c, merid_c, press_c], 3).reshape(rows, nlon, 3 * part_levels)
    patches = lax.all_to_all(back, "lon", split_axis=1, concat_axis=2, tiled=True).reshape(
        rows, width, levels, 3
    )
    return jnp.concatenate(
        [patches[:, :, :, 0], patches[:, :, :, 1], vert_new, patches[:, :, :, 2]], 2
    )


def body(state, filter_flag, cutoff):
    rows, width, depth = state.shape
    levels = depth // 4
    lanes_fit = rows == 8 and 2 * levels == LANES and width % 8 == 0
    if lax.axis_size("lon") == 4 and lanes_fit:
        return packed_body(state, filter_flag, cutoff)
    return plain_body(state, filter_flag, cutoff)


def solution(mesh):
    return jax.shard_map(
        body,
        mesh=mesh,
        in_specs=(P("lat", "lon", None), P("lat"), P("lat")),
        out_specs=P("lat", "lon", None),
        check_vma=False,
    )
```

```python
import functools
import math

import jax
import jax.numpy as jnp
import numpy as np
from jax import lax
from jax.experimental import pallas as pl
from jax.experimental.pallas import tpu as pltpu
from jax.sharding import PartitionSpec as P

WIND_COEF = 0.03
VERT_COEF = 0.2
PRESS_COEF = 0.03
LANES = 128
VMEM_BYTES = 40 * 1024 * 1024
F32 = jnp.float32
BF16 = jnp.bfloat16


def split_np(table):
    high = table.astype(np.float32).astype(jnp.bfloat16)
    low = (table - high.astype(np.float64)).astype(np.float32).astype(jnp.bfloat16)
    return high, low


def round_up(value, step):
    return -(-value // step) * step


@functools.lru_cache(maxsize=None)
def spectral_plan(nlon):
    quarter = nlon // 4
    points = np.arange(quarter)
    waves0 = np.arange(0, nlon // 2 + 1, 4)
    waves2 = np.arange(2, nlon // 2 + 1, 4)
    waves1 = np.arange(1, nlon // 2 + 1, 2)
    size0 = round_up(len(waves0), 16)
    size2 = round_up(len(waves2), 16)
    size1 = round_up(len(waves1), 8)

    def trig(waves, size):
        angle = 2.0 * np.pi * ((waves[:, None] * points[None, :]) % nlon) / nlon
        cos_t, sin_t = np.zeros((2, size, quarter))
        cos_t[: len(waves)] = np.cos(angle)
        sin_t[: len(waves)] = np.sin(angle)
        return cos_t, sin_t

    def padded(values, size):
        out = np.zeros(size)
        out[: len(values)] = values
        return out

    def weights(waves, size):
        ends = (waves == 0) | (2 * waves == nlon)
        return padded(np.where(ends, 1.0, 2.0) / nlon, size)

    cos0, sin0 = trig(waves0, size0)
    cos2, sin2 = trig(waves2, size2)
    cos1, sin1 = trig(waves1, size1)
    turn = padded(np.where(waves1 % 4 == 1, 1.0, -1.0), size1)[:, None]
    fwd0 = np.concatenate([cos0, sin0], 0)
    fwd2 = np.concatenate([cos2, sin2], 0)
    fwd1 = np.block([[cos1, -turn * sin1], [sin1, turn * cos1]])
    inv0 = (fwd0 * np.tile(weights(waves0, size0), 2)[:, None]).T
    inv2 = (fwd2 * np.tile(weights(waves2, size2), 2)[:, None]).T
    inv1 = (fwd1 * np.tile(weights(waves1, size1), 2)[:, None]).T
    forward = [part for table in (fwd0, fwd2, fwd1) for part in split_np(table)]
    inverse = [part for table in (inv0, inv2, inv1) for part in split_np(table)]

    def columns(waves, size):
        inv_wave = padded(1.0 / np.maximum(waves, 1), size)
        delta = padded(np.sin(2.0 * np.pi * waves / nlon), size)
        return np.concatenate([inv_wave, inv_wave]), np.concatenate([delta, -delta])

    per_wave = [columns(w, s) for w, s in ((waves0, size0), (waves2, size2), (waves1, size1))]
    mode = np.stack([np.concatenate([c[0] for c in per_wave]), np.concatenate([c[1] for c in per_wave])], 1)
    mode = np.pad(mode.astype(np.float32), ((0, 0), (0, LANES - 2)))
    return forward, inverse, mode, (size0, size2, size1)


def lane_ids(shape):
    return lax.broadcasted_iota(jnp.int32, shape, len(shape) - 1)


def select_groups(values, masks):
    out = values[0]
    for mask, value in zip(masks[1:], values[1:]):
        out = jnp.where(mask, value, out)
    return out


def group_masks(size, part):
    group = lane_ids((size, LANES)) // part
    return [group == g for g in range(LANES // part)]


def transpose_groups(tiles, masks, part, wanted):
    count = len(tiles)
    turned = []
    for shift in range(count):
        mixed = select_groups([tiles[(shift + g) % count] for g in range(count)], masks)
        turned.append(pltpu.roll(mixed, shift * part, 1) if shift else mixed)
    return [select_groups([turned[(h - g) % count] for h in range(count)], masks) for g in wanted]


def partner_order(blocks, me):
    odd, far = lax.rem(me, 2) == 1, me >= 2
    a, b, c, d = blocks
    a, b, c, d = jnp.where(odd, b, a), jnp.where(odd, a, b), jnp.where(odd, d, c), jnp.where(odd, c, d)
    return [jnp.where(far, c, a), jnp.where(far, d, b), jnp.where(far, a, c), jnp.where(far, b, d)]


def chunk_of(size):
    return next(c for c in (24, 40, 16, 8) if size % c == 0)


def cut_value(flag_ref, cut_ref, row, nlon):
    return jnp.where(flag_ref[row] == 1, cut_ref[row], nlon).astype(F32)


def row_cosine(row, count):
    return jnp.sin((row.astype(F32) + 0.5) * (math.pi / count))


def levels_table(levels):
    shape = (2 * levels, 2 * levels)
    source = lax.broadcasted_iota(jnp.int32, shape, 0)
    target = lax.broadcasted_iota(jnp.int32, shape, 1)
    step = source % levels - target % levels
    diff = jnp.where(step == 1, 1.0, jnp.where(step == -1, -1.0, 0.0))
    rim = (target % levels == 0) | (target % levels == levels - 1)
    twice = jnp.where(step == 0, jnp.where(rim, -1.0, -2.0), jnp.where(abs(step) == 2, 1.0, 0.0))
    from_press, to_press = source >= levels, target >= levels
    table = jnp.where(from_press, jnp.where(to_press, twice, diff), jnp.where(to_press, -10.0 * diff, 0.0))
    return table.astype(BF16)


def each_chunk(size, step, work, **loop):
    def turn(index, carry):
        work(pl.multiple_of(index * step, 8))
        return carry

    lax.fori_loop(0, size // step, turn, 0, **loop)


def put(refs, start, values):
    for ref, value in zip(refs, values):
        ref[pl.ds(start, value.shape[0])] = value


def merid_row(wind_ref, tile_ref, row, lines):
    half = 0.5 * WIND_COEF
    value = wind_ref[row, lines]
    if row < tile_ref.shape[0] - 1:
        value = value - half * tile_ref[row + 1, lines]
    return value + half * tile_ref[row - 1, lines] if row else value


def zonal_kernel(part, wind_ref, tile_ref, *refs):
    packs, zonal_ref = refs[:4], refs[4]
    rows, width, _ = tile_ref.shape
    last = rows - 1
    levels = LANES // 2
    nlat = rows * lax.axis_size("lat")
    me = lax.axis_index("lon")
    first = lax.axis_index("lat") * rows
    place = lax.broadcasted_iota(jnp.int32, (width, LANES), 0)
    for row in range(rows):
        tile = tile_ref[row]
        after = jnp.where(place == width - 1, 0.0, pltpu.roll(tile, width - 1, 0))
        before = jnp.where(place == 0, 0.0, pltpu.roll(tile, 1, 0))
        scale = WIND_COEF / (2.0 * row_cosine(jnp.full((1, LANES), first + row), nlat))
        zonal_ref[row] = wind_ref[row] - pltpu.roll((after - before) * scale, levels, 1)

    size = chunk_of(width)
    masks = group_masks(size, part)

    def pack(start):
        lines = pl.ds(start, size)
        blocks = transpose_groups([zonal_ref[row, lines] for row in range(rows)], masks, part, range(4))
        put(packs, start, partner_order(blocks, me))

    each_chunk(width, size, pack)
    line = lax.broadcasted_iota(jnp.int32, (8, LANES), 0)
    sides = []
    for row in range(rows):
        side = jnp.where(line == 0, tile_ref[row, 0:8], 0.0)
        sides.append(jnp.where(line == 7, tile_ref[row, width - 8 : width], side))
    masks8 = group_masks(8, part)
    put(packs, width, partner_order(transpose_groups(sides, masks8, part, range(4, 8)), me))

    head = rim_lines(width)

    def pack_rim(start):
        tiles = []
        for begin in (start, jnp.minimum(start + head, width - 8)):
            lines = pl.ds(pl.multiple_of(begin, 8), 8)
            for row in (0, last):
                tiles += [merid_row(wind_ref, tile_ref, row, lines), tile_ref[row, lines]]
        put(packs, width + 8 + start, partner_order(transpose_groups(tiles, masks8, part, range(4, 8)), me))

    each_chunk(head, 8, pack_rim, unroll=True)


def rim_lines(width):
    return round_up(-(-width // 2), 8)


def fold_lines(width):
    return round_up(-(-width * 3 // 4), 8)


def press_kernel(part, wind_ref, tile_ref, *refs):
    packs, vert_ref = refs[:4], refs[4]
    rows, width, _ = tile_ref.shape
    levels = LANES // 2
    me = lax.axis_index("lon")
    masks8 = group_masks(8, part)
    head = fold_lines(width)
    tail = width - head

    def pack_merid(start, pair, fold=None):
        lines = pl.ds(start, 8)
        folded = pl.ds(start - pair * tail + head if fold is None else fold, 8)
        tiles = [merid_row(wind_ref, tile_ref, row, lines) for row in range(1, rows - 1)]
        one = merid_row(wind_ref, tile_ref, 2 * pair + 1, folded)
        two = merid_row(wind_ref, tile_ref, 2 * pair + 2, folded)
        blocks = transpose_groups([one] + tiles + [two], masks8, part, range(4, 8))
        put(packs, start, partner_order(blocks, me))

    for pair in range(3):
        each_chunk(tail, 8, lambda start: pack_merid(pl.multiple_of(start + pair * tail, 8), pair), unroll=True)
    for start in range(3 * tail, head, 8):
        pack_merid(start, 2, start)

    gain = jnp.where(lane_ids((1, LANES)) < levels, -0.5 * VERT_COEF, 0.25 * PRESS_COEF * VERT_COEF)
    table = levels_table(levels)
    dot = functools.partial(jnp.dot, preferred_element_type=F32)
    for row in range(rows):
        tile = tile_ref[row]
        high = tile.astype(BF16)
        rest = (tile - high.astype(F32)).astype(BF16)
        vert_ref[row] = tile + gain * (dot(high, table) + dot(rest, table))

    size = chunk_of(width)
    masks = group_masks(size, part)

    def pack(start):
        lines = pl.ds(start, size)
        blocks = transpose_groups([vert_ref[row, lines] for row in range(rows)], masks, part, range(4, 8))
        put(packs, pl.multiple_of(start + head, 8), partner_order(blocks, me))

    each_chunk(width, size, pack)


def turn_groups(value, groups, part):
    shift = groups * part % LANES
    return pltpu.roll(value, shift, 1) if shift else value


def rim_kernel(part, skip, flag_ref, cut_ref, *refs):
    blocks, north_ref, south_ref = refs[:4], refs[4], refs[5]
    lines = blocks[0].shape[0] - skip
    first = lane_ids((lines, LANES)) // part % 4 < 2
    for half in range(2):
        one, two = blocks[2 * half][skip:], blocks[2 * half + 1][skip:]
        where = slice(half * lines, half * lines + lines)
        south_ref[where] = jnp.where(first, one, turn_groups(two, 2, part))
        north_ref[where] = jnp.where(first, turn_groups(two, -2, part), one)
    last = flag_ref.shape[0] - 1
    nlon = (skip - 8) * 4
    north_ref[2 * lines :] = jnp.full((8, LANES), cut_value(flag_ref, cut_ref, last, nlon), F32)
    south_ref[2 * lines :] = jnp.full((8, LANES), cut_value(flag_ref, cut_ref, 0, nlon), F32)


def edge_spec_kernel(bounds, part, skip, flag_ref, cut_ref, mode_ref, south_ref, north_ref, *refs):
    blocks, forward, spec_ref = refs[:4], refs[4:10], refs[10]
    lines = blocks[0].shape[0] - skip
    width = skip - 8
    half = 0.5 * WIND_COEF
    item = lane_ids((lines, LANES)) // part % 4
    fields = []
    for quarter, block in enumerate(blocks):
        where = slice(quarter // 2 * lines, quarter // 2 * lines + lines)
        own, south, north = block[skip:], south_ref[where], north_ref[where]
        at = 0 if quarter % 2 else 2
        merid_s, press_s = turn_groups(south, 1 - at, part), turn_groups(south, -1 - at, part)
        merid_n, press_n = turn_groups(north, 1 + at, part), turn_groups(north, at - 1, part)
        inner = own + half * jnp.where(item == 0, press_s, -press_n)
        outer = jnp.where(item == 1, merid_s - half * own, merid_n + half * own)
        value = jnp.where(item % 2 == 0, inner, outer)
        fields.append(jnp.concatenate([value, turn_groups(value, -4, part)], 0)[:width])
    rows = flag_ref.shape[0]
    group = lane_ids((1, LANES)) // part
    cut = jnp.where(group == 0, cut_value(flag_ref, cut_ref, 0, 4 * width), cut_value(flag_ref, cut_ref, rows - 1, 4 * width))
    cut = jnp.where(group == 1, south_ref[2 * lines : 2 * lines + 1], cut)
    cut = jnp.where(group == 3, north_ref[2 * lines : 2 * lines + 1], cut)
    damp = damping(cut, mode_ref[:, 0:1])
    for (low, high), value in zip(bounds, forward_dft(fields, forward)):
        spec_ref[low:high] = value * damp[low:high]


def merid_spec_kernel(bounds, part, flag_ref, cut_ref, mode_ref, edge_ref, _, *refs):
    blocks, forward, inverse, outs, spec_ref = refs[:4], refs[4:10], refs[10:16], refs[16:20], refs[20]
    rows = flag_ref.shape[0]
    width = outs[0].shape[0]
    head = fold_lines(width)
    tail = width - head
    group = lane_ids((tail, LANES)) // part
    fields = []
    for block in blocks:
        out = None
        for pair in range(3):
            value = block[pair * tail : pair * tail + tail]
            one, two = turn_groups(value, 2 * pair + 1, part), turn_groups(value, 2 * pair + 3, part)
            both = jnp.where(group == 2 * pair + 1, one, two)
            out = both if pair == 0 else jnp.where(group > 2 * pair, both, out)
        fields.append(jnp.concatenate([block[:head], out], 0))
    damp = damping(lane_cut(flag_ref, cut_ref, 4 * width, part), mode_ref[:, 0:1])
    group = lane_ids((1, LANES)) // part
    parts = []
    for (low, high), value in zip(bounds, forward_dft(fields, forward)):
        edge = edge_ref[low:high]
        value = jnp.where(group == 0, edge, value * damp[low:high])
        parts.append(jnp.where(group == rows - 1, turn_groups(edge, rows - 3, part), value))
        spec_ref[low:high] = parts[-1]
    inverse_dft(parts, inverse, outs)


def dot3(table_high, table_low, value):
    high = value.astype(BF16)
    low = (value - high.astype(F32)).astype(BF16)
    width = value.shape[1]
    dot = functools.partial(jnp.dot, preferred_element_type=F32)
    both = dot(table_high[...], jnp.concatenate([high, low], 1))
    return both[:, :width] + both[:, width:] + dot(table_low[...], high)


def by_place(me, dif0, dif1):
    odd = lax.rem(me, 2) == 1
    sign = jnp.where(me >= 2, -1.0, 1.0).astype(F32)
    return jnp.where(odd, dif1, dif0) * sign, jnp.where(odd, dif0, dif1) * sign


def parity_sign(me):
    return jnp.where(lax.rem(me, 2) == 1, -1.0, 1.0).astype(F32)


def forward_dft(quarters, tables):
    me = lax.axis_index("lon")
    own, core, chip, far = quarters
    sum0, sum1 = own + chip, core + far
    dif0, dif1 = by_place(me, own - chip, core - far)
    return (
        dot3(tables[0], tables[1], sum0 + sum1),
        dot3(tables[2], tables[3], (sum0 - sum1) * parity_sign(me)),
        dot3(tables[4], tables[5], jnp.concatenate([dif0, dif1], 0)),
    )


def inverse_dft(parts, tables, outs):
    me = lax.axis_index("lon")
    even = dot3(tables[0], tables[1], parts[0])
    other = dot3(tables[2], tables[3], parts[1]) * parity_sign(me)
    both = dot3(tables[4], tables[5], parts[2])
    quarter = even.shape[0]
    dif0, dif1 = by_place(me, both[:quarter], both[quarter:])
    plus, minus = even + other, even - other
    outs[0][...] = plus + dif0
    outs[1][...] = minus + dif1
    outs[2][...] = plus - dif0
    outs[3][...] = minus - dif1


def lane_rows(pick, rows, part):
    group = lane_ids((1, LANES)) // part
    out = jnp.zeros((1, LANES), F32)
    for row in range(rows):
        out = jnp.where(group == row, pick(row), out)
    return out


def lane_cut(flag_ref, cut_ref, nlon, part):
    rows = flag_ref.shape[0]
    return lane_rows(lambda row: cut_value(flag_ref, cut_ref, row, nlon), rows, part)


def lane_cosine(shift, rows, part):
    row = lane_ids((1, LANES)) // part + lax.axis_index("lat") * rows + shift
    return row_cosine(row, rows * lax.axis_size("lat"))


def damping(cut, inv_wave):
    ratio = cut * inv_wave
    return jnp.minimum(1.0, ratio * ratio)


def zonal_spec_kernel(bounds, part, flag_ref, cut_ref, mode_ref, q0, q1, q2, q3, *refs):
    forward, inverse, outs, spec_ref = refs[:6], refs[6:12], refs[12:16], refs[16]
    rows = flag_ref.shape[0]
    width = outs[0].shape[0]
    me = lax.axis_index("lon")
    quarters = (q0, q1, q2, q3)
    scale = WIND_COEF / (2.0 * lane_cosine(0, rows, part))
    line = lax.broadcasted_iota(jnp.int32, (8, LANES), 0)
    sides = partner_order([q[width : width + 8] for q in quarters], me)
    starts = [jnp.where(line == 0, scale * pltpu.roll(sides[(q + 3) % 4], 1, 0), 0.0) for q in range(4)]
    ends = [jnp.where(line == 7, scale * pltpu.roll(sides[(q + 1) % 4], 7, 0), 0.0) for q in range(4)]
    starts, ends = partner_order(starts, me), partner_order(ends, me)
    fields = [
        jnp.concatenate([q[0:8] + start, q[8 : width - 8], q[width - 8 : width] - end], 0)
        for q, start, end in zip(quarters, starts, ends)
    ]
    damp = damping(lane_cut(flag_ref, cut_ref, 4 * width, part), mode_ref[:, 0:1])
    parts = [value * damp[b[0] : b[1]] for b, value in zip(bounds, forward_dft(fields, forward))]
    for (low, high), value in zip(bounds, parts):
        spec_ref[low:high] = value
    inverse_dft(parts, inverse, outs)


def press_back_kernel(bounds, part, flag_ref, cut_ref, mode_ref, zonal_ref, merid_ref, edge_ref, *refs):
    quarters, forward, inverse, outs = refs[:4], refs[4:10], refs[10:16], refs[16:]
    skip = quarters[0].shape[0] - outs[0].shape[0]
    rows = flag_ref.shape[0]
    nlon = 4 * inverse[0].shape[0]
    band = lax.axis_index("lat")
    mode = mode_ref[...]
    damp = damping(lane_cut(flag_ref, cut_ref, nlon, part), mode[:, 0:1])
    cosine = lane_cosine(0, rows, part)
    below = jnp.where(band == 0, 0.0, lane_cosine(-1, rows, part))
    above = jnp.where(band == lax.axis_size("lat") - 1, 0.0, lane_cosine(1, rows, part))
    half_inv = 0.5 / cosine
    group = lane_ids((1, LANES)) // part
    flux = merid_ref[...] * cosine
    edge = edge_ref[...]
    north = jnp.where(group == rows - 1, turn_groups(edge, rows - 4, part) * above, turn_groups(flux, -1, part))
    south = jnp.where(group == 0, turn_groups(edge, -1, part) * below, turn_groups(flux, 1, part))
    div_y = (north - south) * half_inv
    zonal = zonal_ref[...]
    slope = mode[:, 1:2] / cosine
    parts = []
    for (low, high), press in zip(bounds, forward_dft([q[skip:] for q in quarters], forward)):
        mid = (low + high) // 2
        swapped = jnp.concatenate([zonal[mid:high], zonal[low:mid]], 0)
        div = swapped * slope[low:high] + div_y[low:high]
        parts.append((press - PRESS_COEF * div) * damp[low:high])
    inverse_dft(parts, inverse, outs)


def winds_out_kernel(part, *refs):
    blocks, out_ref = refs[:8], refs[8]
    rows, width, _ = out_ref.shape
    me = lax.axis_index("lon")
    size = chunk_of(width)
    masks = group_masks(size, part)

    def unpack(step, carry):
        lines = pl.ds(pl.multiple_of(step * size, 8), size)
        values = [ref[lines] for ref in blocks]
        values = partner_order(values[:4], me) + partner_order(values[4:], me)
        for row, value in enumerate(transpose_groups(values, masks, part, range(rows))):
            out_ref[row, lines] = value
        return carry

    lax.fori_loop(0, width // size, unpack, 0)


def press_out_kernel(part, _, tile_ref, *refs):
    blocks, out_ref = refs[:4], refs[4]
    rows, width, _ = out_ref.shape
    me = lax.axis_index("lon")
    size = chunk_of(width)
    masks = group_masks(size, part)
    low = lane_ids((size, LANES)) < LANES // 2

    def unpack(step, carry):
        lines = pl.ds(pl.multiple_of(step * size, 8), size)
        values = partner_order([ref[lines] for ref in blocks], me)
        for row, value in enumerate(transpose_groups(values + values, masks, part, range(rows))):
            out_ref[row, lines] = jnp.where(low, tile_ref[row, lines], value)
        return carry

    lax.fori_loop(0, width // size, unpack, 0)


def whole(shape):
    return pl.BlockSpec(shape, lambda step: (0,) * len(shape))


def tile_of(shape, index):
    return pl.BlockSpec((shape[0], shape[1], LANES), lambda step: (0, 0, index))


SMEM = pl.BlockSpec(memory_space=pltpu.SMEM)
ANY = pl.BlockSpec(memory_space=pl.ANY)


def call(kernel, out_shape, in_specs, out_specs, cost=2, grid=(1,), **more):
    return pl.pallas_call(
        kernel,
        grid=grid,
        out_shape=out_shape,
        in_specs=in_specs,
        out_specs=out_specs,
        compiler_params=pltpu.CompilerParams(vmem_limit_bytes=VMEM_BYTES),
        cost_estimate=pl.CostEstimate(flops=0, bytes_accessed=int(cost * 3.69e6), transcendentals=0),
        **more,
    )


def f32(*shape):
    return jax.ShapeDtypeStruct(shape, F32)


def exchange(blocks):
    pairs = [[(i, i ^ step) for i in range(4)] for step in range(4)]
    return [blocks[0]] + [lax.ppermute(blocks[step], "lon", pairs[step]) for step in range(1, 4)]


def packed_body(state, filter_flag, cutoff):
    rows, width, depth = state.shape
    levels = depth // 4
    bands = lax.axis_size("lat")
    nlon = 4 * width
    part = levels // 4
    forward, inverse, mode, sizes = spectral_plan(nlon)
    forward = [jnp.asarray(t) for t in forward]
    inverse = [jnp.asarray(t) for t in inverse]
    mode = jnp.asarray(mode)
    bounds, at = [], 0
    for size in sizes:
        bounds.append((at, at + 2 * size))
        at += 2 * size
    table_specs = [whole(t.shape) for t in forward] + [whole(t.shape) for t in inverse]
    block, spectrum, full = (width, LANES), (at, LANES), (rows, width, LANES)
    skip = width + 8
    first = (skip + rim_lines(width), LANES)
    second = (fold_lines(width) + width, LANES)
    rims = (2 * rim_lines(width) + 8, LANES)
    low_tile, high_tile = tile_of(state.shape, 0), tile_of(state.shape, 1)

    first_circle = exchange(
        call(
            functools.partial(zonal_kernel, part),
            [f32(*first)] * 4,
            [low_tile, high_tile],
            [whole(first)] * 4,
            scratch_shapes=[pltpu.VMEM(full, F32)],
        )(state, state)
    )
    *packs, vert = call(
        functools.partial(press_kernel, part),
        [f32(*second)] * 4 + [f32(*full)],
        [low_tile, high_tile],
        [whole(second)] * 4 + [whole(full)],
    )(state, state)
    second_circle = exchange(packs)

    to_north, to_south = call(
        functools.partial(rim_kernel, part, skip),
        [f32(*rims)] * 2,
        [SMEM] * 2 + [whole(first)] * 4,
        [whole(rims)] * 2,
    )(filter_flag, cutoff, *first_circle)
    from_south = lax.ppermute(to_north, "lat", [(i, i + 1) for i in range(bands - 1)])
    from_north = lax.ppermute(to_south, "lat", [(i + 1, i) for i in range(bands - 1)])

    *zonal_parts, zonal_spec = call(
        functools.partial(zonal_spec_kernel, bounds, part),
        [f32(*block)] * 4 + [f32(*spectrum)],
        [SMEM] * 2 + [whole(mode.shape)] + [whole(first)] * 4 + table_specs,
        [whole(block)] * 4 + [whole(spectrum)],
    )(filter_flag, cutoff, mode, *first_circle, *forward, *inverse)
    zonal_back = exchange(zonal_parts)
    edge_spec = call(
        functools.partial(edge_spec_kernel, bounds, part, skip),
        f32(*spectrum),
        [SMEM] * 2 + [whole(mode.shape)] + [whole(rims)] * 2 + [whole(first)] * 4 + table_specs[:6],
        whole(spectrum),
    )(filter_flag, cutoff, mode, from_south, from_north, *first_circle, *forward)

    *merid_parts, merid_spec = call(
        functools.partial(merid_spec_kernel, bounds, part),
        [f32(*block)] * 4 + [f32(*spectrum)],
        [SMEM] * 2 + [whole(mode.shape), whole(spectrum), ANY] + [whole(second)] * 4 + table_specs,
        [whole(block)] * 4 + [whole(spectrum)],
    )(filter_flag, cutoff, mode, edge_spec, zonal_spec, *second_circle, *forward, *inverse)
    merid_back = exchange(merid_parts)

    press_parts = call(
        functools.partial(press_back_kernel, bounds, part),
        [f32(*block)] * 4,
        [SMEM] * 2 + [whole(mode.shape)] + [whole(spectrum)] * 3 + [whole(second)] * 4 + table_specs,
        [whole(block)] * 4,
    )(filter_flag, cutoff, mode, zonal_spec, merid_spec, edge_spec, *second_circle, *forward, *inverse)
    press_back = exchange(press_parts)

    steps = next(s for s in (3, 5, 1) if width % (8 * s) == 0)
    piece = pl.BlockSpec((width // steps, LANES), lambda step: (step, 0))

    def slab(index):
        return pl.BlockSpec((rows, width // steps, LANES), lambda step: (0, step, index))

    out = call(
        functools.partial(winds_out_kernel, part),
        f32(*state.shape),
        [piece] * 8,
        slab(0),
        grid=(steps,),
    )(*zonal_back, *merid_back)
    return call(
        functools.partial(press_out_kernel, part),
        f32(*state.shape),
        [ANY, slab(0)] + [piece] * 4,
        slab(1),
        grid=(steps,),
        input_output_aliases={0: 0},
    )(out, vert, *press_back)


def padded_2(block, sides, width, periodic):
    for axis, dim in sides:
        count = lax.axis_size(axis)
        forward = [(i, i + 1) for i in range(count - 1)]
        if periodic:
            forward.append((count - 1, 0))
        backward = [(target, source) for source, target in forward]
        low = lax.ppermute(
            lax.slice_in_dim(block, block.shape[dim] - width, None, axis=dim), axis, forward
        )
        high = lax.ppermute(lax.slice_in_dim(block, 0, width, axis=dim), axis, backward)
        block = jnp.concatenate([low, block, high], axis=dim)
    return block


def dft_tables(width):
    points = jnp.arange(width, dtype=jnp.int32)
    waves = jnp.arange(width // 2 + 1, dtype=jnp.int32)
    phase = points[:, None] * waves[None, :] % width
    angle = phase.astype(jnp.float32) * (2.0 * math.pi / width)
    weights = jnp.where((waves == 0) | (waves * 2 == width), 1.0, 2.0).astype(jnp.float32) / width
    return (jnp.cos(angle), jnp.sin(angle), weights)


def rims(stack):
    wide = padded_2(stack, (("lon", 1),), 1, True)
    return padded_2(wide, (("lat", 0),), 1, False)


def level_diff(field):
    padded = jnp.pad(field, ((0, 0), (0, 0), (1, 1)))
    return 0.5 * (padded[:, :, 2:] - padded[:, :, :-2])


def damped(block, cut_vec, tables):
    cos_table, sin_table, weights = tables
    highest = lax.Precision.HIGHEST
    wave_vals = jnp.arange(cos_table.shape[1]).astype(jnp.float32)
    ratio = cut_vec[:, None] / jnp.maximum(wave_vals, 1.0)[None, :]
    damping = (jnp.minimum(1.0, ratio * ratio) * weights[None, :])[:, None, :]
    real_part = jnp.einsum("rnq,nk->rqk", block, cos_table, precision=highest)
    imag_part = jnp.einsum("rnq,nk->rqk", block, sin_table, precision=highest)
    restored = jnp.einsum("rqk,nk->rnq", real_part * damping, cos_table, precision=highest)
    return restored + jnp.einsum("rqk,nk->rnq", imag_part * damping, sin_table, precision=highest)


def circle_local(fields, cut_rows, tables):
    return damped(fields, cut_rows, tables)


def polar(fields, row_flag, cut_rows, tables, apply):
    smooth = apply(fields, cut_rows, tables)
    return jnp.where(row_flag[:, None, None], smooth, fields)


def plain_body(state, filter_flag, cutoff):
    rows, width, depth = state.shape
    levels = depth // 4
    zonal_wind = state[:, :, :levels]
    merid_wind = state[:, :, levels : 2 * levels]
    vert_wind = state[:, :, 2 * levels : 3 * levels]
    pressure = state[:, :, 3 * levels :]
    nlat = rows * lax.axis_size("lat")
    nlon = width * lax.axis_size("lon")
    offset = lax.axis_index("lat") * rows
    row_ids = (offset + jnp.arange(-1, rows + 1)).astype(jnp.float32)
    cos_ext = jnp.cos(-0.5 * math.pi + (row_ids + 0.5) * math.pi / nlat)
    cos_mid = cos_ext[1:-1][:, None, None]
    tables = dft_tables(nlon)
    row_flag = filter_flag == 1
    cut_rows = cutoff.astype(jnp.float32)
    padded = rims(pressure)
    grad_x = (padded[1:-1, 2:] - padded[1:-1, :-2]) / (2.0 * cos_mid)
    grad_y = 0.5 * (padded[2:, 1:-1] - padded[:-2, 1:-1])
    grad_z = level_diff(pressure)
    zonal_pre = zonal_wind - WIND_COEF * grad_x
    merid_pre = merid_wind - WIND_COEF * grad_y
    vert_new = vert_wind - VERT_COEF * grad_z
    div_z = level_diff(vert_new)
    outgoing = jnp.stack([zonal_pre, merid_pre, pressure, div_z], 3).reshape(
        rows, width, 4 * levels
    )
    circles = lax.all_to_all(outgoing, "lon", split_axis=2, concat_axis=1, tiled=True)
    part_levels = circles.shape[2] // 4
    circles = circles.reshape(rows, nlon, part_levels, 4)
    winds_c = jnp.concatenate([circles[:, :, :, 0], circles[:, :, :, 1]], 2)
    press_c = circles[:, :, :, 2]
    div_z_c = circles[:, :, :, 3]
    winds_c = polar(winds_c, row_flag, cut_rows, tables, circle_local)
    zonal_c = winds_c[:, :, :part_levels]
    merid_c = winds_c[:, :, part_levels:]
    div_x = (jnp.roll(zonal_c, -1, 1) - jnp.roll(zonal_c, 1, 1)) / (2.0 * cos_mid)
    flux = padded_2(merid_c * cos_mid, (("lat", 0),), 1, False)
    div_y = (flux[2:] - flux[:-2]) / (2.0 * cos_mid)
    press_mid = press_c - PRESS_COEF * (div_x + div_y + div_z_c)
    press_c = polar(press_mid, row_flag, cut_rows, tables, circle_local)
    back = jnp.stack([zonal_c, merid_c, press_c], 3).reshape(rows, nlon, 3 * part_levels)
    patches = lax.all_to_all(back, "lon", split_axis=1, concat_axis=2, tiled=True).reshape(
        rows, width, levels, 3
    )
    return jnp.concatenate(
        [patches[:, :, :, 0], patches[:, :, :, 1], vert_new, patches[:, :, :, 2]], 2
    )


def body(state, filter_flag, cutoff):
    rows, width, depth = state.shape
    levels = depth // 4
    lanes_fit = rows == 8 and 2 * levels == LANES and width % 8 == 0
    if lax.axis_size("lon") == 4 and lanes_fit:
        return packed_body(state, filter_flag, cutoff)
    return plain_body(state, filter_flag, cutoff)


def solution(mesh):
    return jax.shard_map(
        body,
        mesh=mesh,
        in_specs=(P("lat", "lon", None), P("lat"), P("lat")),
        out_specs=P("lat", "lon", None),
        check_vma=False,
    )
```

```python
import functools
import math

import jax
import jax.numpy as jnp
import numpy as np
from jax import lax
from jax.experimental import pallas as pl
from jax.experimental.pallas import tpu as pltpu
from jax.sharding import PartitionSpec as P

WIND_COEF = 0.03
VERT_COEF = 0.2
PRESS_COEF = 0.03
LANES = 128
VMEM_BYTES = 40 * 1024 * 1024
F32 = jnp.float32
BF16 = jnp.bfloat16


def split_np(table):
    high = table.astype(np.float32).astype(jnp.bfloat16)
    low = (table - high.astype(np.float64)).astype(np.float32).astype(jnp.bfloat16)
    return high, low


def round_up(value, step):
    return -(-value // step) * step


@functools.lru_cache(maxsize=None)
def spectral_plan(nlon):
    quarter = nlon // 4
    points = np.arange(quarter)
    waves0 = np.arange(0, nlon // 2 + 1, 4)
    waves2 = np.arange(2, nlon // 2 + 1, 4)
    waves1 = np.arange(1, nlon // 2 + 1, 2)
    size0 = round_up(len(waves0), 16)
    size2 = round_up(len(waves2), 16)
    size1 = round_up(len(waves1), 8)

    def trig(waves, size):
        angle = 2.0 * np.pi * ((waves[:, None] * points[None, :]) % nlon) / nlon
        cos_t, sin_t = np.zeros((2, size, quarter))
        cos_t[: len(waves)] = np.cos(angle)
        sin_t[: len(waves)] = np.sin(angle)
        return cos_t, sin_t

    def padded(values, size):
        out = np.zeros(size)
        out[: len(values)] = values
        return out

    def weights(waves, size):
        ends = (waves == 0) | (2 * waves == nlon)
        return padded(np.where(ends, 1.0, 2.0) / nlon, size)

    cos0, sin0 = trig(waves0, size0)
    cos2, sin2 = trig(waves2, size2)
    cos1, sin1 = trig(waves1, size1)
    turn = padded(np.where(waves1 % 4 == 1, 1.0, -1.0), size1)[:, None]
    fwd0 = np.concatenate([cos0, sin0], 0)
    fwd2 = np.concatenate([cos2, sin2], 0)
    fwd1 = np.block([[cos1, -turn * sin1], [sin1, turn * cos1]])
    inv0 = (fwd0 * np.tile(weights(waves0, size0), 2)[:, None]).T
    inv2 = (fwd2 * np.tile(weights(waves2, size2), 2)[:, None]).T
    inv1 = (fwd1 * np.tile(weights(waves1, size1), 2)[:, None]).T
    forward = [part for table in (fwd0, fwd2, fwd1) for part in split_np(table)]
    inverse = [part for table in (inv0, inv2, inv1) for part in split_np(table)]

    def columns(waves, size):
        inv_wave = padded(1.0 / np.maximum(waves, 1), size)
        delta = padded(np.sin(2.0 * np.pi * waves / nlon), size)
        return np.concatenate([inv_wave, inv_wave]), np.concatenate([delta, -delta])

    per_wave = [columns(w, s) for w, s in ((waves0, size0), (waves2, size2), (waves1, size1))]
    mode = np.stack([np.concatenate([c[0] for c in per_wave]), np.concatenate([c[1] for c in per_wave])], 1)
    mode = np.pad(mode.astype(np.float32), ((0, 0), (0, LANES - 2)))
    return forward, inverse, mode, (size0, size2, size1)


def lane_ids(shape):
    return lax.broadcasted_iota(jnp.int32, shape, len(shape) - 1)


def select_groups(values, masks):
    out = None
    for mask, value in zip(masks, values):
        if value is not None:
            out = value if out is None else jnp.where(mask, value, out)
    return out


def group_masks(size, part):
    group = lane_ids((size, LANES)) // part
    return [group == g for g in range(LANES // part)]


def transpose_groups(tiles, masks, part, wanted):
    count = len(tiles)
    turned = []
    for shift in range(count):
        mixed = select_groups([tiles[(shift + g) % count] if g in wanted else None for g in range(count)], masks)
        turned.append(pltpu.roll(mixed, shift * part, 1) if shift else mixed)
    return [select_groups([turned[(h - g) % count] for h in range(count)], masks) for g in wanted]


def gather_groups(blocks, masks, part):
    count = len(masks)
    turned = []
    for shift in range(count):
        mixed = [None] * count
        for g, block in enumerate(blocks):
            mixed[(4 + g - shift) % count] = block
        mixed = select_groups(mixed, masks)
        turned.append(pltpu.roll(mixed, shift * part, 1) if shift else mixed)
    return [select_groups([None] * 4 + [turned[(4 + g - row) % count] for g in range(4)], masks) for row in range(count)]


def partner_order(blocks, me):
    odd, far = lax.rem(me, 2) == 1, me >= 2
    a, b, c, d = blocks
    a, b, c, d = jnp.where(odd, b, a), jnp.where(odd, a, b), jnp.where(odd, d, c), jnp.where(odd, c, d)
    return [jnp.where(far, c, a), jnp.where(far, d, b), jnp.where(far, a, c), jnp.where(far, b, d)]


def chunk_of(size):
    return next(c for c in (24, 40, 16, 8) if size % c == 0)


def cut_value(flag_ref, cut_ref, row, nlon):
    return jnp.where(flag_ref[row] == 1, cut_ref[row], nlon).astype(F32)


def row_cosine(row, count):
    return jnp.sin((row.astype(F32) + 0.5) * (math.pi / count))


def levels_table(levels):
    shape = (2 * levels, 2 * levels)
    source = lax.broadcasted_iota(jnp.int32, shape, 0)
    target = lax.broadcasted_iota(jnp.int32, shape, 1)
    step = source % levels - target % levels
    diff = jnp.where(step == 1, 1.0, jnp.where(step == -1, -1.0, 0.0))
    rim = (target % levels == 0) | (target % levels == levels - 1)
    twice = jnp.where(step == 0, jnp.where(rim, -1.0, -2.0), jnp.where(abs(step) == 2, 1.0, 0.0))
    from_press, to_press = source >= levels, target >= levels
    table = jnp.where(from_press, jnp.where(to_press, twice, diff), jnp.where(to_press, -10.0 * diff, 0.0))
    return table.astype(BF16)


def each_chunk(size, step, work):
    def turn(index, carry):
        work(pl.multiple_of(index * step, 8))
        return carry

    lax.fori_loop(0, size // step, turn, 0, unroll=True)


def put(refs, start, values):
    for ref, value in zip(refs, values):
        ref[pl.ds(start, value.shape[0])] = value


def merid_row(wind_ref, tile_ref, row, lines):
    half = 0.5 * WIND_COEF
    value = wind_ref[row, lines]
    if row < tile_ref.shape[0] - 1:
        value = value - half * tile_ref[row + 1, lines]
    return value + half * tile_ref[row - 1, lines] if row else value


def zonal_kernel(part, wind_ref, tile_ref, *refs):
    packs, zonal_ref = refs[:4], refs[4]
    rows, width, _ = tile_ref.shape
    last = rows - 1
    levels = LANES // 2
    nlat = rows * lax.axis_size("lat")
    me = lax.axis_index("lon")
    first = lax.axis_index("lat") * rows
    place = lax.broadcasted_iota(jnp.int32, (width, LANES), 0)
    for row in range(rows):
        tile = tile_ref[row]
        after = jnp.where(place == width - 1, 0.0, pltpu.roll(tile, width - 1, 0))
        before = jnp.where(place == 0, 0.0, pltpu.roll(tile, 1, 0))
        scale = WIND_COEF / (2.0 * row_cosine(jnp.full((1, LANES), first + row), nlat))
        zonal_ref[row] = wind_ref[row] - pltpu.roll((after - before) * scale, levels, 1)

    size = chunk_of(width)
    masks = group_masks(size, part)

    def pack(start):
        lines = pl.ds(start, size)
        blocks = transpose_groups([zonal_ref[row, lines] for row in range(rows)], masks, part, range(4))
        put(packs, start, partner_order(blocks, me))

    each_chunk(width, size, pack)
    line = lax.broadcasted_iota(jnp.int32, (8, LANES), 0)
    sides = []
    for row in range(rows):
        side = jnp.where(line == 0, tile_ref[row, 0:8], 0.0)
        sides.append(jnp.where(line == 7, tile_ref[row, width - 8 : width], side))
    masks8 = group_masks(8, part)
    put(packs, width, partner_order(transpose_groups(sides, masks8, part, range(4, 8)), me))

    head = rim_lines(width)

    def pack_rim(start):
        tiles = []
        for begin in (start, jnp.minimum(start + head, width - 8)):
            lines = pl.ds(pl.multiple_of(begin, 8), 8)
            for row in (0, last):
                tiles += [merid_row(wind_ref, tile_ref, row, lines), tile_ref[row, lines]]
        put(packs, width + 8 + start, partner_order(transpose_groups(tiles, masks8, part, range(4, 8)), me))

    each_chunk(head, 8, pack_rim)


def rim_lines(width):
    return round_up(-(-width // 2), 8)


def fold_lines(width):
    return round_up(-(-width * 3 // 4), 8)


def press_kernel(part, wind_ref, tile_ref, *refs):
    packs, vert_ref = refs[:4], refs[4]
    rows, width, _ = tile_ref.shape
    levels = LANES // 2
    me = lax.axis_index("lon")
    masks8 = group_masks(8, part)
    head = fold_lines(width)
    tail = width - head

    def pack_merid(start, pair, fold=None):
        lines = pl.ds(start, 8)
        folded = pl.ds(start - pair * tail + head if fold is None else fold, 8)
        tiles = [merid_row(wind_ref, tile_ref, row, lines) for row in range(1, rows - 1)]
        one = merid_row(wind_ref, tile_ref, 2 * pair + 1, folded)
        two = merid_row(wind_ref, tile_ref, 2 * pair + 2, folded)
        blocks = transpose_groups([one] + tiles + [two], masks8, part, range(4, 8))
        put(packs, start, partner_order(blocks, me))

    for pair in range(3):
        each_chunk(tail, 8, lambda start: pack_merid(pl.multiple_of(start + pair * tail, 8), pair))
    for start in range(3 * tail, head, 8):
        pack_merid(start, 2, start)

    gain = jnp.where(lane_ids((1, LANES)) < levels, -0.5 * VERT_COEF, 0.25 * PRESS_COEF * VERT_COEF)
    table = levels_table(levels)
    dot = functools.partial(jnp.dot, preferred_element_type=F32)
    for row in range(rows):
        tile = tile_ref[row]
        high = tile.astype(BF16)
        rest = (tile - high.astype(F32)).astype(BF16)
        vert_ref[row] = tile + gain * (dot(high, table) + dot(rest, table))

    size = chunk_of(width)
    masks = group_masks(size, part)

    def pack(start):
        lines = pl.ds(start, size)
        blocks = transpose_groups([vert_ref[row, lines] for row in range(rows)], masks, part, range(4, 8))
        put(packs, pl.multiple_of(start + head, 8), partner_order(blocks, me))

    each_chunk(width, size, pack)


def turn_groups(value, groups, part):
    shift = groups * part % LANES
    return pltpu.roll(value, shift, 1) if shift else value


def rim_kernel(part, skip, flag_ref, cut_ref, *refs):
    blocks, north_ref, south_ref = refs[:4], refs[4], refs[5]
    lines = blocks[0].shape[0] - skip
    first = lane_ids((lines, LANES)) // part % 4 < 2
    for half in range(2):
        one, two = blocks[2 * half][skip:], blocks[2 * half + 1][skip:]
        where = slice(half * lines, half * lines + lines)
        south_ref[where] = jnp.where(first, one, turn_groups(two, 2, part))
        north_ref[where] = jnp.where(first, turn_groups(two, -2, part), one)
    last = flag_ref.shape[0] - 1
    nlon = (skip - 8) * 4
    north_ref[2 * lines :] = jnp.full((8, LANES), cut_value(flag_ref, cut_ref, last, nlon), F32)
    south_ref[2 * lines :] = jnp.full((8, LANES), cut_value(flag_ref, cut_ref, 0, nlon), F32)


def edge_spec_kernel(bounds, part, skip, flag_ref, cut_ref, mode_ref, south_ref, north_ref, *refs):
    blocks, forward, spec_ref = refs[:4], refs[4:10], refs[10]
    lines = blocks[0].shape[0] - skip
    width = skip - 8
    half = 0.5 * WIND_COEF
    item = lane_ids((lines, LANES)) // part % 4
    fields = []
    for quarter, block in enumerate(blocks):
        where = slice(quarter // 2 * lines, quarter // 2 * lines + lines)
        own, south, north = block[skip:], south_ref[where], north_ref[where]
        at = 0 if quarter % 2 else 2
        merid_s, press_s = turn_groups(south, 1 - at, part), turn_groups(south, -1 - at, part)
        merid_n, press_n = turn_groups(north, 1 + at, part), turn_groups(north, at - 1, part)
        inner = own + half * jnp.where(item == 0, press_s, -press_n)
        outer = jnp.where(item == 1, merid_s - half * own, merid_n + half * own)
        value = jnp.where(item % 2 == 0, inner, outer)
        fields.append(jnp.concatenate([value, turn_groups(value, -4, part)], 0)[:width])
    rows = flag_ref.shape[0]
    group = lane_ids((1, LANES)) // part
    cut = jnp.where(group == 0, cut_value(flag_ref, cut_ref, 0, 4 * width), cut_value(flag_ref, cut_ref, rows - 1, 4 * width))
    cut = jnp.where(group == 1, south_ref[2 * lines : 2 * lines + 1], cut)
    cut = jnp.where(group == 3, north_ref[2 * lines : 2 * lines + 1], cut)
    damp = damping(cut, mode_ref[:, 0:1])
    for (low, high), value in zip(bounds, forward_dft(fields, forward)):
        spec_ref[low:high] = value * damp[low:high]


def merid_spec_kernel(bounds, part, flag_ref, cut_ref, mode_ref, edge_ref, _, *refs):
    blocks, forward, inverse, outs, spec_ref = refs[:4], refs[4:10], refs[10:16], refs[16:20], refs[20]
    rows = flag_ref.shape[0]
    width = outs[0].shape[0]
    head = fold_lines(width)
    tail = width - head
    group = lane_ids((tail, LANES)) // part
    fields = []
    for block in blocks:
        out = None
        for pair in range(3):
            value = block[pair * tail : pair * tail + tail]
            one, two = turn_groups(value, 2 * pair + 1, part), turn_groups(value, 2 * pair + 3, part)
            both = jnp.where(group == 2 * pair + 1, one, two)
            out = both if pair == 0 else jnp.where(group > 2 * pair, both, out)
        fields.append(jnp.concatenate([block[:head], out], 0))
    damp = damping(lane_cut(flag_ref, cut_ref, 4 * width, part), mode_ref[:, 0:1])
    group = lane_ids((1, LANES)) // part
    parts = []
    for (low, high), value in zip(bounds, forward_dft(fields, forward)):
        edge = edge_ref[low:high]
        value = jnp.where(group == 0, edge, value * damp[low:high])
        parts.append(jnp.where(group == rows - 1, turn_groups(edge, rows - 3, part), value))
        spec_ref[low:high] = parts[-1]
    inverse_dft(parts, inverse, outs)


def dot3(table_high, table_low, value):
    high = value.astype(BF16)
    low = (value - high.astype(F32)).astype(BF16)
    width = value.shape[1]
    dot = functools.partial(jnp.dot, preferred_element_type=F32)
    both = dot(table_high[...], jnp.concatenate([high, low], 1))
    return both[:, :width] + both[:, width:] + dot(table_low[...], high)


def by_place(me, dif0, dif1):
    odd = lax.rem(me, 2) == 1
    sign = jnp.where(me >= 2, -1.0, 1.0).astype(F32)
    return jnp.where(odd, dif1, dif0) * sign, jnp.where(odd, dif0, dif1) * sign


def parity_sign(me):
    return jnp.where(lax.rem(me, 2) == 1, -1.0, 1.0).astype(F32)


def forward_dft(quarters, tables):
    me = lax.axis_index("lon")
    own, core, chip, far = quarters
    sum0, sum1 = own + chip, core + far
    dif0, dif1 = by_place(me, own - chip, core - far)
    return (
        dot3(tables[0], tables[1], sum0 + sum1),
        dot3(tables[2], tables[3], (sum0 - sum1) * parity_sign(me)),
        dot3(tables[4], tables[5], jnp.concatenate([dif0, dif1], 0)),
    )


def inverse_dft(parts, tables, outs):
    me = lax.axis_index("lon")
    even = dot3(tables[0], tables[1], parts[0])
    other = dot3(tables[2], tables[3], parts[1]) * parity_sign(me)
    both = dot3(tables[4], tables[5], parts[2])
    quarter = even.shape[0]
    dif0, dif1 = by_place(me, both[:quarter], both[quarter:])
    plus, minus = even + other, even - other
    outs[0][...] = plus + dif0
    outs[1][...] = minus + dif1
    outs[2][...] = plus - dif0
    outs[3][...] = minus - dif1


def lane_rows(pick, rows, part):
    group = lane_ids((1, LANES)) // part
    out = jnp.zeros((1, LANES), F32)
    for row in range(rows):
        out = jnp.where(group == row, pick(row), out)
    return out


def lane_cut(flag_ref, cut_ref, nlon, part):
    rows = flag_ref.shape[0]
    return lane_rows(lambda row: cut_value(flag_ref, cut_ref, row, nlon), rows, part)


def lane_cosine(shift, rows, part):
    row = lane_ids((1, LANES)) // part + lax.axis_index("lat") * rows + shift
    return row_cosine(row, rows * lax.axis_size("lat"))


def damping(cut, inv_wave):
    ratio = cut * inv_wave
    return jnp.minimum(1.0, ratio * ratio)


def zonal_spec_kernel(bounds, part, flag_ref, cut_ref, mode_ref, _, q0, q1, q2, q3, *refs):
    forward, inverse, outs, spec_ref = refs[:6], refs[6:12], refs[12:16], refs[16]
    rows = flag_ref.shape[0]
    width = outs[0].shape[0]
    me = lax.axis_index("lon")
    quarters = (q0, q1, q2, q3)
    scale = WIND_COEF / (2.0 * lane_cosine(0, rows, part))
    line = lax.broadcasted_iota(jnp.int32, (8, LANES), 0)
    sides = partner_order([q[width : width + 8] for q in quarters], me)
    starts = [jnp.where(line == 0, scale * pltpu.roll(sides[(q + 3) % 4], 1, 0), 0.0) for q in range(4)]
    ends = [jnp.where(line == 7, scale * pltpu.roll(sides[(q + 1) % 4], 7, 0), 0.0) for q in range(4)]
    starts, ends = partner_order(starts, me), partner_order(ends, me)
    fields = [
        jnp.concatenate([q[0:8] + start, q[8 : width - 8], q[width - 8 : width] - end], 0)
        for q, start, end in zip(quarters, starts, ends)
    ]
    damp = damping(lane_cut(flag_ref, cut_ref, 4 * width, part), mode_ref[:, 0:1])
    parts = [value * damp[b[0] : b[1]] for b, value in zip(bounds, forward_dft(fields, forward))]
    for (low, high), value in zip(bounds, parts):
        spec_ref[low:high] = value
    inverse_dft(parts, inverse, outs)


def press_back_kernel(bounds, part, flag_ref, cut_ref, mode_ref, zonal_ref, merid_ref, edge_ref, *refs):
    quarters, forward, inverse, outs = refs[:4], refs[4:10], refs[10:16], refs[16:]
    skip = quarters[0].shape[0] - outs[0].shape[0]
    rows = flag_ref.shape[0]
    nlon = 4 * inverse[0].shape[0]
    band = lax.axis_index("lat")
    mode = mode_ref[...]
    damp = damping(lane_cut(flag_ref, cut_ref, nlon, part), mode[:, 0:1])
    cosine = lane_cosine(0, rows, part)
    below = jnp.where(band == 0, 0.0, lane_cosine(-1, rows, part))
    above = jnp.where(band == lax.axis_size("lat") - 1, 0.0, lane_cosine(1, rows, part))
    half_inv = 0.5 / cosine
    group = lane_ids((1, LANES)) // part
    flux = merid_ref[...] * cosine
    edge = edge_ref[...]
    north = jnp.where(group == rows - 1, turn_groups(edge, rows - 4, part) * above, turn_groups(flux, -1, part))
    south = jnp.where(group == 0, turn_groups(edge, -1, part) * below, turn_groups(flux, 1, part))
    div_y = (north - south) * half_inv
    zonal = zonal_ref[...]
    slope = mode[:, 1:2] / cosine
    parts = []
    for (low, high), press in zip(bounds, forward_dft([q[skip:] for q in quarters], forward)):
        mid = (low + high) // 2
        swapped = jnp.concatenate([zonal[mid:high], zonal[low:mid]], 0)
        div = swapped * slope[low:high] + div_y[low:high]
        parts.append((press - PRESS_COEF * div) * damp[low:high])
    inverse_dft(parts, inverse, outs)


def winds_out_kernel(part, *refs):
    blocks, out_ref = refs[:8], refs[8]
    rows, width, _ = out_ref.shape
    me = lax.axis_index("lon")
    size = chunk_of(width)
    masks = group_masks(size, part)

    def unpack(start):
        lines = pl.ds(start, size)
        values = [ref[lines] for ref in blocks]
        values = partner_order(values[:4], me) + partner_order(values[4:], me)
        for row, value in enumerate(transpose_groups(values, masks, part, range(rows))):
            out_ref[row, lines] = value

    each_chunk(width, size, unpack)


def press_out_kernel(part, _, tile_ref, *refs):
    blocks, out_hbm, tile_out, sems = refs[:4], refs[4], refs[5], refs[6]
    rows, width, _ = tile_ref.shape
    me = lax.axis_index("lon")
    size = chunk_of(width)
    masks = group_masks(size, part)
    low = lane_ids((size, LANES)) < LANES // 2
    count = sems.shape[0]
    copies = []
    for piece in range(count):
        begin, end = piece * width // count, (piece + 1) * width // count

        def unpack(start):
            lines = pl.ds(start + begin, size)
            values = partner_order([ref[lines] for ref in blocks], me)
            for row, value in enumerate(gather_groups(values, masks, part)):
                tile_out[row, lines] = jnp.where(low, tile_ref[row, lines], value)

        each_chunk(end - begin, size, unpack)
        copy = pltpu.make_async_copy(tile_out.at[:, begin:end], out_hbm.at[:, begin:end, LANES:], sems.at[piece])
        copy.start()
        copies.append(copy)
    for copy in copies:
        copy.wait()


def whole(shape):
    return pl.BlockSpec(shape, lambda step: (0,) * len(shape))


def tile_of(shape, index):
    return pl.BlockSpec((shape[0], shape[1], LANES), lambda step: (0, 0, index))


SMEM = pl.BlockSpec(memory_space=pltpu.SMEM)
ANY = pl.BlockSpec(memory_space=pl.ANY)


def call(kernel, out_shape, in_specs, out_specs, cost=2, grid=(1,), **more):
    return pl.pallas_call(
        kernel,
        grid=grid,
        out_shape=out_shape,
        in_specs=in_specs,
        out_specs=out_specs,
        compiler_params=pltpu.CompilerParams(vmem_limit_bytes=VMEM_BYTES),
        cost_estimate=pl.CostEstimate(flops=0, bytes_accessed=int(cost * 3.69e6), transcendentals=0),
        **more,
    )


def f32(*shape):
    return jax.ShapeDtypeStruct(shape, F32)


def exchange(blocks):
    pairs = [[(i, i ^ step) for i in range(4)] for step in range(4)]
    chip, far, core = (lax.ppermute(blocks[step], "lon", pairs[step]) for step in (2, 3, 1))
    return [blocks[0], core, chip, far]


def packed_body(state, filter_flag, cutoff):
    rows, width, depth = state.shape
    levels = depth // 4
    bands = lax.axis_size("lat")
    nlon = 4 * width
    part = levels // 4
    forward, inverse, mode, sizes = spectral_plan(nlon)
    forward = [jnp.asarray(t) for t in forward]
    inverse = [jnp.asarray(t) for t in inverse]
    mode = jnp.asarray(mode)
    bounds, at = [], 0
    for size in sizes:
        bounds.append((at, at + 2 * size))
        at += 2 * size
    table_specs = [whole(t.shape) for t in forward] + [whole(t.shape) for t in inverse]
    block, spectrum, full = (width, LANES), (at, LANES), (rows, width, LANES)
    skip = width + 8
    first = (skip + rim_lines(width), LANES)
    second = (fold_lines(width) + width, LANES)
    rims = (2 * rim_lines(width) + 8, LANES)
    low_tile, high_tile = tile_of(state.shape, 0), tile_of(state.shape, 1)

    first_circle = exchange(
        call(
            functools.partial(zonal_kernel, part),
            [f32(*first)] * 4,
            [low_tile, high_tile],
            [whole(first)] * 4,
            scratch_shapes=[pltpu.VMEM(full, F32)],
        )(state, state)
    )
    *packs, vert = call(
        functools.partial(press_kernel, part),
        [f32(*second)] * 4 + [f32(*full)],
        [low_tile, high_tile],
        [whole(second)] * 4 + [whole(full)],
    )(state, state)
    second_circle = exchange(packs)

    to_north, to_south = call(
        functools.partial(rim_kernel, part, skip),
        [f32(*rims)] * 2,
        [SMEM] * 2 + [whole(first)] * 4,
        [whole(rims)] * 2,
    )(filter_flag, cutoff, *first_circle)
    from_south = lax.ppermute(to_north, "lat", [(i, i + 1) for i in range(bands - 1)])
    from_north = lax.ppermute(to_south, "lat", [(i + 1, i) for i in range(bands - 1)])

    *zonal_parts, zonal_spec = call(
        functools.partial(zonal_spec_kernel, bounds, part),
        [f32(*block)] * 4 + [f32(*spectrum)],
        [SMEM] * 2 + [whole(mode.shape), ANY] + [whole(first)] * 4 + table_specs,
        [whole(block)] * 4 + [whole(spectrum)],
    )(filter_flag, cutoff, mode, second_circle[1], *first_circle, *forward, *inverse)
    zonal_back = exchange(zonal_parts)
    edge_spec = call(
        functools.partial(edge_spec_kernel, bounds, part, skip),
        f32(*spectrum),
        [SMEM] * 2 + [whole(mode.shape)] + [whole(rims)] * 2 + [whole(first)] * 4 + table_specs[:6],
        whole(spectrum),
    )(filter_flag, cutoff, mode, from_south, from_north, *first_circle, *forward)

    *merid_parts, merid_spec = call(
        functools.partial(merid_spec_kernel, bounds, part),
        [f32(*block)] * 4 + [f32(*spectrum)],
        [SMEM] * 2 + [whole(mode.shape), whole(spectrum), ANY] + [whole(second)] * 4 + table_specs,
        [whole(block)] * 4 + [whole(spectrum)],
    )(filter_flag, cutoff, mode, edge_spec, zonal_spec, *second_circle, *forward, *inverse)
    merid_back = exchange(merid_parts)

    press_parts = call(
        functools.partial(press_back_kernel, bounds, part),
        [f32(*block)] * 4,
        [SMEM] * 2 + [whole(mode.shape)] + [whole(spectrum)] * 3 + [whole(second)] * 4 + table_specs,
        [whole(block)] * 4,
    )(filter_flag, cutoff, mode, zonal_spec, merid_spec, edge_spec, *second_circle, *forward, *inverse)
    press_back = exchange(press_parts)

    out = call(
        functools.partial(winds_out_kernel, part),
        f32(*state.shape),
        [whole(block)] * 8,
        low_tile,
    )(*zonal_back, *merid_back)
    pieces = next(n for n in (3, 5, 1) if width % (n * chunk_of(width)) == 0)
    return call(
        functools.partial(press_out_kernel, part),
        f32(*state.shape),
        [ANY, whole(full)] + [whole(block)] * 4,
        ANY,
        scratch_shapes=[pltpu.VMEM(full, F32), pltpu.SemaphoreType.DMA((pieces,))],
        input_output_aliases={0: 0},
    )(out, vert, *press_back)


def padded_2(block, sides, width, periodic):
    for axis, dim in sides:
        count = lax.axis_size(axis)
        forward = [(i, i + 1) for i in range(count - 1)]
        if periodic:
            forward.append((count - 1, 0))
        backward = [(target, source) for source, target in forward]
        low = lax.ppermute(
            lax.slice_in_dim(block, block.shape[dim] - width, None, axis=dim), axis, forward
        )
        high = lax.ppermute(lax.slice_in_dim(block, 0, width, axis=dim), axis, backward)
        block = jnp.concatenate([low, block, high], axis=dim)
    return block


def dft_tables(width):
    points = jnp.arange(width, dtype=jnp.int32)
    waves = jnp.arange(width // 2 + 1, dtype=jnp.int32)
    phase = points[:, None] * waves[None, :] % width
    angle = phase.astype(jnp.float32) * (2.0 * math.pi / width)
    weights = jnp.where((waves == 0) | (waves * 2 == width), 1.0, 2.0).astype(jnp.float32) / width
    return (jnp.cos(angle), jnp.sin(angle), weights)


def rims(stack):
    wide = padded_2(stack, (("lon", 1),), 1, True)
    return padded_2(wide, (("lat", 0),), 1, False)


def level_diff(field):
    padded = jnp.pad(field, ((0, 0), (0, 0), (1, 1)))
    return 0.5 * (padded[:, :, 2:] - padded[:, :, :-2])


def damped(block, cut_vec, tables):
    cos_table, sin_table, weights = tables
    highest = lax.Precision.HIGHEST
    wave_vals = jnp.arange(cos_table.shape[1]).astype(jnp.float32)
    ratio = cut_vec[:, None] / jnp.maximum(wave_vals, 1.0)[None, :]
    damping = (jnp.minimum(1.0, ratio * ratio) * weights[None, :])[:, None, :]
    real_part = jnp.einsum("rnq,nk->rqk", block, cos_table, precision=highest)
    imag_part = jnp.einsum("rnq,nk->rqk", block, sin_table, precision=highest)
    restored = jnp.einsum("rqk,nk->rnq", real_part * damping, cos_table, precision=highest)
    return restored + jnp.einsum("rqk,nk->rnq", imag_part * damping, sin_table, precision=highest)


def circle_local(fields, cut_rows, tables):
    return damped(fields, cut_rows, tables)


def polar(fields, row_flag, cut_rows, tables, apply):
    smooth = apply(fields, cut_rows, tables)
    return jnp.where(row_flag[:, None, None], smooth, fields)


def plain_body(state, filter_flag, cutoff):
    rows, width, depth = state.shape
    levels = depth // 4
    zonal_wind = state[:, :, :levels]
    merid_wind = state[:, :, levels : 2 * levels]
    vert_wind = state[:, :, 2 * levels : 3 * levels]
    pressure = state[:, :, 3 * levels :]
    nlat = rows * lax.axis_size("lat")
    nlon = width * lax.axis_size("lon")
    offset = lax.axis_index("lat") * rows
    row_ids = (offset + jnp.arange(-1, rows + 1)).astype(jnp.float32)
    cos_ext = jnp.cos(-0.5 * math.pi + (row_ids + 0.5) * math.pi / nlat)
    cos_mid = cos_ext[1:-1][:, None, None]
    tables = dft_tables(nlon)
    row_flag = filter_flag == 1
    cut_rows = cutoff.astype(jnp.float32)
    padded = rims(pressure)
    grad_x = (padded[1:-1, 2:] - padded[1:-1, :-2]) / (2.0 * cos_mid)
    grad_y = 0.5 * (padded[2:, 1:-1] - padded[:-2, 1:-1])
    grad_z = level_diff(pressure)
    zonal_pre = zonal_wind - WIND_COEF * grad_x
    merid_pre = merid_wind - WIND_COEF * grad_y
    vert_new = vert_wind - VERT_COEF * grad_z
    div_z = level_diff(vert_new)
    outgoing = jnp.stack([zonal_pre, merid_pre, pressure, div_z], 3).reshape(
        rows, width, 4 * levels
    )
    circles = lax.all_to_all(outgoing, "lon", split_axis=2, concat_axis=1, tiled=True)
    part_levels = circles.shape[2] // 4
    circles = circles.reshape(rows, nlon, part_levels, 4)
    winds_c = jnp.concatenate([circles[:, :, :, 0], circles[:, :, :, 1]], 2)
    press_c = circles[:, :, :, 2]
    div_z_c = circles[:, :, :, 3]
    winds_c = polar(winds_c, row_flag, cut_rows, tables, circle_local)
    zonal_c = winds_c[:, :, :part_levels]
    merid_c = winds_c[:, :, part_levels:]
    div_x = (jnp.roll(zonal_c, -1, 1) - jnp.roll(zonal_c, 1, 1)) / (2.0 * cos_mid)
    flux = padded_2(merid_c * cos_mid, (("lat", 0),), 1, False)
    div_y = (flux[2:] - flux[:-2]) / (2.0 * cos_mid)
    press_mid = press_c - PRESS_COEF * (div_x + div_y + div_z_c)
    press_c = polar(press_mid, row_flag, cut_rows, tables, circle_local)
    back = jnp.stack([zonal_c, merid_c, press_c], 3).reshape(rows, nlon, 3 * part_levels)
    patches = lax.all_to_all(back, "lon", split_axis=1, concat_axis=2, tiled=True).reshape(
        rows, width, levels, 3
    )
    return jnp.concatenate(
        [patches[:, :, :, 0], patches[:, :, :, 1], vert_new, patches[:, :, :, 2]], 2
    )


def body(state, filter_flag, cutoff):
    rows, width, depth = state.shape
    levels = depth // 4
    lanes_fit = rows == 8 and 2 * levels == LANES and width % 8 == 0
    if lax.axis_size("lon") == 4 and lanes_fit:
        return packed_body(state, filter_flag, cutoff)
    return plain_body(state, filter_flag, cutoff)


def solution(mesh):
    return jax.shard_map(
        body,
        mesh=mesh,
        in_specs=(P("lat", "lon", None), P("lat"), P("lat")),
        out_specs=P("lat", "lon", None),
        check_vma=False,
    )
```

```python
import functools
import math

import jax
import jax.numpy as jnp
import numpy as np
from jax import lax
from jax.experimental import pallas as pl
from jax.experimental.pallas import tpu as pltpu
from jax.sharding import PartitionSpec as P

WIND_COEF = 0.03
VERT_COEF = 0.2
PRESS_COEF = 0.03
LANES = 128
VMEM_BYTES = 40 * 1024 * 1024
F32 = jnp.float32
BF16 = jnp.bfloat16


def split_np(table):
    high = table.astype(np.float32).astype(jnp.bfloat16)
    low = (table - high.astype(np.float64)).astype(np.float32).astype(jnp.bfloat16)
    return high, low


def round_up(value, step):
    return -(-value // step) * step


@functools.lru_cache(maxsize=None)
def spectral_plan(nlon):
    quarter = nlon // 4
    points = np.arange(quarter)
    waves0 = np.arange(0, nlon // 2 + 1, 4)
    waves2 = np.arange(2, nlon // 2 + 1, 4)
    waves1 = np.arange(1, nlon // 2 + 1, 2)
    size0 = round_up(len(waves0), 16)
    size2 = round_up(len(waves2), 16)
    size1 = round_up(len(waves1), 8)

    def trig(waves, size):
        angle = 2.0 * np.pi * ((waves[:, None] * points[None, :]) % nlon) / nlon
        cos_t, sin_t = np.zeros((2, size, quarter))
        cos_t[: len(waves)] = np.cos(angle)
        sin_t[: len(waves)] = np.sin(angle)
        return cos_t, sin_t

    def padded(values, size):
        out = np.zeros(size)
        out[: len(values)] = values
        return out

    def weights(waves, size):
        ends = (waves == 0) | (2 * waves == nlon)
        return padded(np.where(ends, 1.0, 2.0) / nlon, size)

    cos0, sin0 = trig(waves0, size0)
    cos2, sin2 = trig(waves2, size2)
    cos1, sin1 = trig(waves1, size1)
    turn = padded(np.where(waves1 % 4 == 1, 1.0, -1.0), size1)[:, None]
    fwd0 = np.concatenate([cos0, sin0], 0)
    fwd2 = np.concatenate([cos2, sin2], 0)
    fwd1 = np.block([[cos1, -turn * sin1], [sin1, turn * cos1]])
    inv0 = (fwd0 * np.tile(weights(waves0, size0), 2)[:, None]).T
    inv2 = (fwd2 * np.tile(weights(waves2, size2), 2)[:, None]).T
    inv1 = (fwd1 * np.tile(weights(waves1, size1), 2)[:, None]).T
    forward = [part for table in (fwd0, fwd2, fwd1) for part in split_np(table)]
    inverse = [part for table in (inv0, inv2, inv1) for part in split_np(table)]

    def columns(waves, size):
        inv_wave = padded(1.0 / np.maximum(waves, 1), size)
        delta = padded(np.sin(2.0 * np.pi * waves / nlon), size)
        return np.concatenate([inv_wave, inv_wave]), np.concatenate([delta, -delta])

    per_wave = [columns(w, s) for w, s in ((waves0, size0), (waves2, size2), (waves1, size1))]
    mode = np.stack([np.concatenate([c[0] for c in per_wave]), np.concatenate([c[1] for c in per_wave])], 1)
    mode = np.pad(mode.astype(np.float32), ((0, 0), (0, LANES - 2)))
    return forward, inverse, mode, (size0, size2, size1)


def lane_ids(shape):
    return lax.broadcasted_iota(jnp.int32, shape, len(shape) - 1)


def select_groups(values, masks):
    out = None
    for mask, value in zip(masks, values):
        if value is not None:
            out = value if out is None else jnp.where(mask, value, out)
    return out


def group_masks(size, part):
    group = lane_ids((size, LANES)) // part
    return [group == g for g in range(LANES // part)]


def transpose_groups(tiles, masks, part, wanted):
    count = len(tiles)
    turned = []
    for shift in range(count):
        mixed = select_groups([tiles[(shift + g) % count] if g in wanted else None for g in range(count)], masks)
        turned.append(pltpu.roll(mixed, shift * part, 1) if shift else mixed)
    return [select_groups([turned[(h - g) % count] for h in range(count)], masks) for g in wanted]


def gather_groups(blocks, masks, part):
    count = len(masks)
    turned = []
    for shift in range(count):
        mixed = [None] * count
        for g, block in enumerate(blocks):
            mixed[(4 + g - shift) % count] = block
        mixed = select_groups(mixed, masks)
        turned.append(pltpu.roll(mixed, shift * part, 1) if shift else mixed)
    return [select_groups([None] * 4 + [turned[(4 + g - row) % count] for g in range(4)], masks) for row in range(count)]


def partner_order(blocks, me):
    odd, far = lax.rem(me, 2) == 1, me >= 2
    a, b, c, d = blocks
    a, b, c, d = jnp.where(odd, b, a), jnp.where(odd, a, b), jnp.where(odd, d, c), jnp.where(odd, c, d)
    return [jnp.where(far, c, a), jnp.where(far, d, b), jnp.where(far, a, c), jnp.where(far, b, d)]


def chunk_of(size):
    return next(c for c in (24, 40, 16, 8) if size % c == 0)


def cut_value(flag_ref, cut_ref, row, nlon):
    return jnp.where(flag_ref[row] == 1, cut_ref[row], nlon).astype(F32)


def row_cosine(row, count):
    return jnp.sin((row.astype(F32) + 0.5) * (math.pi / count))


def levels_table(levels):
    shape = (2 * levels, 2 * levels)
    source = lax.broadcasted_iota(jnp.int32, shape, 0)
    target = lax.broadcasted_iota(jnp.int32, shape, 1)
    step = source % levels - target % levels
    diff = jnp.where(step == 1, 1.0, jnp.where(step == -1, -1.0, 0.0))
    rim = (target % levels == 0) | (target % levels == levels - 1)
    twice = jnp.where(step == 0, jnp.where(rim, -1.0, -2.0), jnp.where(abs(step) == 2, 1.0, 0.0))
    from_press, to_press = source >= levels, target >= levels
    table = jnp.where(from_press, jnp.where(to_press, twice, diff), jnp.where(to_press, -10.0 * diff, 0.0))
    return table.astype(BF16)


def each_chunk(size, step, work):
    def turn(index, carry):
        work(pl.multiple_of(index * step, 8))
        return carry

    lax.fori_loop(0, size // step, turn, 0, unroll=True)


def natural(refs):
    own, chip, far, core = refs
    return [own, core, chip, far]


def put(refs, start, values):
    for ref, value in zip(refs, values):
        ref[pl.ds(start, value.shape[0])] = value


def merid_row(wind_ref, tile_ref, row, lines):
    half = 0.5 * WIND_COEF
    value = wind_ref[row, lines]
    if row < tile_ref.shape[0] - 1:
        value = value - half * tile_ref[row + 1, lines]
    return value + half * tile_ref[row - 1, lines] if row else value


def zonal_kernel(part, wind_ref, tile_ref, *refs):
    packs, zonal_ref = refs[:4], refs[4]
    rows, width, _ = tile_ref.shape
    last = rows - 1
    levels = LANES // 2
    nlat = rows * lax.axis_size("lat")
    me = lax.axis_index("lon")
    first = lax.axis_index("lat") * rows
    place = lax.broadcasted_iota(jnp.int32, (width, LANES), 0)
    for row in range(rows):
        tile = tile_ref[row]
        after = jnp.where(place == width - 1, 0.0, pltpu.roll(tile, width - 1, 0))
        before = jnp.where(place == 0, 0.0, pltpu.roll(tile, 1, 0))
        scale = WIND_COEF / (2.0 * row_cosine(jnp.full((1, LANES), first + row), nlat))
        zonal_ref[row] = wind_ref[row] - pltpu.roll((after - before) * scale, levels, 1)

    size = chunk_of(width)
    masks = group_masks(size, part)

    def pack(start):
        lines = pl.ds(start, size)
        blocks = transpose_groups([zonal_ref[row, lines] for row in range(rows)], masks, part, range(4))
        put(packs, start, partner_order(blocks, me))

    each_chunk(width, size, pack)
    line = lax.broadcasted_iota(jnp.int32, (8, LANES), 0)
    sides = []
    for row in range(rows):
        side = jnp.where(line == 0, tile_ref[row, 0:8], 0.0)
        sides.append(jnp.where(line == 7, tile_ref[row, width - 8 : width], side))
    masks8 = group_masks(8, part)
    put(packs, width, partner_order(transpose_groups(sides, masks8, part, range(4, 8)), me))

    head = rim_lines(width)

    def pack_rim(start):
        tiles = []
        for begin in (start, jnp.minimum(start + head, width - 8)):
            lines = pl.ds(pl.multiple_of(begin, 8), 8)
            for row in (0, last):
                tiles += [merid_row(wind_ref, tile_ref, row, lines), tile_ref[row, lines]]
        put(packs, width + 8 + start, partner_order(transpose_groups(tiles, masks8, part, range(4, 8)), me))

    each_chunk(head, 8, pack_rim)


def rim_lines(width):
    return round_up(-(-width // 2), 8)


def fold_lines(width):
    return round_up(-(-width * 3 // 4), 8)


def press_kernel(part, wind_ref, tile_ref, *refs):
    packs, vert_ref = refs[:4], refs[4]
    rows, width, _ = tile_ref.shape
    levels = LANES // 2
    me = lax.axis_index("lon")
    masks8 = group_masks(8, part)
    head = fold_lines(width)
    tail = width - head

    def pack_merid(start, pair, fold=None):
        lines = pl.ds(start, 8)
        folded = pl.ds(start - pair * tail + head if fold is None else fold, 8)
        tiles = [merid_row(wind_ref, tile_ref, row, lines) for row in range(1, rows - 1)]
        one = merid_row(wind_ref, tile_ref, 2 * pair + 1, folded)
        two = merid_row(wind_ref, tile_ref, 2 * pair + 2, folded)
        blocks = transpose_groups([one] + tiles + [two], masks8, part, range(4, 8))
        put(packs, start, partner_order(blocks, me))

    for pair in range(3):
        each_chunk(tail, 8, lambda start: pack_merid(pl.multiple_of(start + pair * tail, 8), pair))
    for start in range(3 * tail, head, 8):
        pack_merid(start, 2, start)

    gain = jnp.where(lane_ids((1, LANES)) < levels, -0.5 * VERT_COEF, 0.25 * PRESS_COEF * VERT_COEF)
    table = levels_table(levels)
    dot = functools.partial(jnp.dot, preferred_element_type=F32)
    for row in range(rows):
        tile = tile_ref[row]
        high = tile.astype(BF16)
        rest = (tile - high.astype(F32)).astype(BF16)
        vert_ref[row] = tile + gain * (dot(high, table) + dot(rest, table))

    size = chunk_of(width)
    masks = group_masks(size, part)

    def pack(start):
        lines = pl.ds(start, size)
        blocks = transpose_groups([vert_ref[row, lines] for row in range(rows)], masks, part, range(4, 8))
        put(packs, pl.multiple_of(start + head, 8), partner_order(blocks, me))

    each_chunk(width, size, pack)


def turn_groups(value, groups, part):
    shift = groups * part % LANES
    return pltpu.roll(value, shift, 1) if shift else value


def rim_kernel(part, skip, flag_ref, cut_ref, *refs):
    blocks, north_ref, south_ref = natural(refs[:4]), refs[4], refs[5]
    lines = blocks[0].shape[0] - skip
    first = lane_ids((lines, LANES)) // part % 4 < 2
    for half in range(2):
        one, two = blocks[2 * half][skip:], blocks[2 * half + 1][skip:]
        where = slice(half * lines, half * lines + lines)
        south_ref[where] = jnp.where(first, one, turn_groups(two, 2, part))
        north_ref[where] = jnp.where(first, turn_groups(two, -2, part), one)
    last = flag_ref.shape[0] - 1
    nlon = (skip - 8) * 4
    north_ref[2 * lines :] = jnp.full((8, LANES), cut_value(flag_ref, cut_ref, last, nlon), F32)
    south_ref[2 * lines :] = jnp.full((8, LANES), cut_value(flag_ref, cut_ref, 0, nlon), F32)


def edge_spec_kernel(bounds, part, skip, flag_ref, cut_ref, mode_ref, south_ref, north_ref, *refs):
    blocks, forward, spec_ref = natural(refs[:4]), refs[4:10], refs[10]
    lines = blocks[0].shape[0] - skip
    width = skip - 8
    half = 0.5 * WIND_COEF
    item = lane_ids((lines, LANES)) // part % 4
    fields = []
    for quarter, block in enumerate(blocks):
        where = slice(quarter // 2 * lines, quarter // 2 * lines + lines)
        own, south, north = block[skip:], south_ref[where], north_ref[where]
        at = 0 if quarter % 2 else 2
        merid_s, press_s = turn_groups(south, 1 - at, part), turn_groups(south, -1 - at, part)
        merid_n, press_n = turn_groups(north, 1 + at, part), turn_groups(north, at - 1, part)
        inner = own + half * jnp.where(item == 0, press_s, -press_n)
        outer = jnp.where(item == 1, merid_s - half * own, merid_n + half * own)
        value = jnp.where(item % 2 == 0, inner, outer)
        fields.append(jnp.concatenate([value, turn_groups(value, -4, part)], 0)[:width])
    rows = flag_ref.shape[0]
    group = lane_ids((1, LANES)) // part
    cut = jnp.where(group == 0, cut_value(flag_ref, cut_ref, 0, 4 * width), cut_value(flag_ref, cut_ref, rows - 1, 4 * width))
    cut = jnp.where(group == 1, south_ref[2 * lines : 2 * lines + 1], cut)
    cut = jnp.where(group == 3, north_ref[2 * lines : 2 * lines + 1], cut)
    damp = damping(cut, mode_ref[:, 0:1])
    for (low, high), value in zip(bounds, forward_dft(fields, forward)):
        spec_ref[low:high] = value * damp[low:high]


def merid_spec_kernel(bounds, part, flag_ref, cut_ref, mode_ref, edge_ref, _, *refs):
    blocks, forward, inverse, outs, spec_ref = natural(refs[:4]), refs[4:10], refs[10:16], refs[16:20], refs[20]
    rows = flag_ref.shape[0]
    width = outs[0].shape[0]
    head = fold_lines(width)
    tail = width - head
    group = lane_ids((tail, LANES)) // part
    fields = []
    for block in blocks:
        out = None
        for pair in range(3):
            value = block[pair * tail : pair * tail + tail]
            one, two = turn_groups(value, 2 * pair + 1, part), turn_groups(value, 2 * pair + 3, part)
            both = jnp.where(group == 2 * pair + 1, one, two)
            out = both if pair == 0 else jnp.where(group > 2 * pair, both, out)
        fields.append(jnp.concatenate([block[:head], out], 0))
    damp = damping(lane_cut(flag_ref, cut_ref, 4 * width, part), mode_ref[:, 0:1])
    group = lane_ids((1, LANES)) // part
    parts = []
    for (low, high), value in zip(bounds, forward_dft(fields, forward)):
        edge = edge_ref[low:high]
        value = jnp.where(group == 0, edge, value * damp[low:high])
        parts.append(jnp.where(group == rows - 1, turn_groups(edge, rows - 3, part), value))
        spec_ref[low:high] = parts[-1]
    inverse_dft(parts, inverse, outs)


def dot3(table_high, table_low, value):
    high = value.astype(BF16)
    low = (value - high.astype(F32)).astype(BF16)
    width = value.shape[1]
    dot = functools.partial(jnp.dot, preferred_element_type=F32)
    both = dot(table_high[...], jnp.concatenate([high, low], 1))
    return both[:, :width] + both[:, width:] + dot(table_low[...], high)


def by_place(me, dif0, dif1):
    odd = lax.rem(me, 2) == 1
    sign = jnp.where(me >= 2, -1.0, 1.0).astype(F32)
    return jnp.where(odd, dif1, dif0) * sign, jnp.where(odd, dif0, dif1) * sign


def parity_sign(me):
    return jnp.where(lax.rem(me, 2) == 1, -1.0, 1.0).astype(F32)


def forward_dft(quarters, tables):
    me = lax.axis_index("lon")
    own, core, chip, far = quarters
    sum0, sum1 = own + chip, core + far
    dif0, dif1 = by_place(me, own - chip, core - far)
    return (
        dot3(tables[0], tables[1], sum0 + sum1),
        dot3(tables[2], tables[3], (sum0 - sum1) * parity_sign(me)),
        dot3(tables[4], tables[5], jnp.concatenate([dif0, dif1], 0)),
    )


def inverse_dft(parts, tables, outs):
    me = lax.axis_index("lon")
    even = dot3(tables[0], tables[1], parts[0])
    other = dot3(tables[2], tables[3], parts[1]) * parity_sign(me)
    both = dot3(tables[4], tables[5], parts[2])
    quarter = even.shape[0]
    dif0, dif1 = by_place(me, both[:quarter], both[quarter:])
    plus, minus = even + other, even - other
    outs[0][...] = plus + dif0
    outs[1][...] = minus + dif1
    outs[2][...] = plus - dif0
    outs[3][...] = minus - dif1


def lane_rows(pick, rows, part):
    group = lane_ids((1, LANES)) // part
    out = jnp.zeros((1, LANES), F32)
    for row in range(rows):
        out = jnp.where(group == row, pick(row), out)
    return out


def lane_cut(flag_ref, cut_ref, nlon, part):
    rows = flag_ref.shape[0]
    return lane_rows(lambda row: cut_value(flag_ref, cut_ref, row, nlon), rows, part)


def lane_cosine(shift, rows, part):
    row = lane_ids((1, LANES)) // part + lax.axis_index("lat") * rows + shift
    return row_cosine(row, rows * lax.axis_size("lat"))


def damping(cut, inv_wave):
    ratio = cut * inv_wave
    return jnp.minimum(1.0, ratio * ratio)


def zonal_spec_kernel(bounds, part, flag_ref, cut_ref, mode_ref, _, q0, q2, q3, q1, *refs):
    forward, inverse, outs, spec_ref = refs[:6], refs[6:12], refs[12:16], refs[16]
    rows = flag_ref.shape[0]
    width = outs[0].shape[0]
    me = lax.axis_index("lon")
    quarters = (q0, q1, q2, q3)
    scale = WIND_COEF / (2.0 * lane_cosine(0, rows, part))
    line = lax.broadcasted_iota(jnp.int32, (8, LANES), 0)
    sides = partner_order([q[width : width + 8] for q in quarters], me)
    starts = [jnp.where(line == 0, scale * pltpu.roll(sides[(q + 3) % 4], 1, 0), 0.0) for q in range(4)]
    ends = [jnp.where(line == 7, scale * pltpu.roll(sides[(q + 1) % 4], 7, 0), 0.0) for q in range(4)]
    starts, ends = partner_order(starts, me), partner_order(ends, me)
    fields = [
        jnp.concatenate([q[0:8] + start, q[8 : width - 8], q[width - 8 : width] - end], 0)
        for q, start, end in zip(quarters, starts, ends)
    ]
    damp = damping(lane_cut(flag_ref, cut_ref, 4 * width, part), mode_ref[:, 0:1])
    parts = [value * damp[b[0] : b[1]] for b, value in zip(bounds, forward_dft(fields, forward))]
    for (low, high), value in zip(bounds, parts):
        spec_ref[low:high] = value
    inverse_dft(parts, inverse, outs)


def press_back_kernel(bounds, part, flag_ref, cut_ref, mode_ref, zonal_ref, merid_ref, edge_ref, *refs):
    quarters, forward, inverse, outs = natural(refs[:4]), refs[4:10], refs[10:16], refs[16:]
    skip = quarters[0].shape[0] - outs[0].shape[0]
    rows = flag_ref.shape[0]
    nlon = 4 * inverse[0].shape[0]
    band = lax.axis_index("lat")
    mode = mode_ref[...]
    damp = damping(lane_cut(flag_ref, cut_ref, nlon, part), mode[:, 0:1])
    cosine = lane_cosine(0, rows, part)
    below = jnp.where(band == 0, 0.0, lane_cosine(-1, rows, part))
    above = jnp.where(band == lax.axis_size("lat") - 1, 0.0, lane_cosine(1, rows, part))
    half_inv = 0.5 / cosine
    group = lane_ids((1, LANES)) // part
    flux = merid_ref[...] * cosine
    edge = edge_ref[...]
    north = jnp.where(group == rows - 1, turn_groups(edge, rows - 4, part) * above, turn_groups(flux, -1, part))
    south = jnp.where(group == 0, turn_groups(edge, -1, part) * below, turn_groups(flux, 1, part))
    div_y = (north - south) * half_inv
    zonal = zonal_ref[...]
    slope = mode[:, 1:2] / cosine
    parts = []
    for (low, high), press in zip(bounds, forward_dft([q[skip:] for q in quarters], forward)):
        mid = (low + high) // 2
        swapped = jnp.concatenate([zonal[mid:high], zonal[low:mid]], 0)
        div = swapped * slope[low:high] + div_y[low:high]
        parts.append((press - PRESS_COEF * div) * damp[low:high])
    inverse_dft(parts, inverse, outs)


def winds_out_kernel(part, *refs):
    blocks, out_ref = natural(refs[:4]) + natural(refs[4:8]), refs[8]
    rows, width, _ = out_ref.shape
    me = lax.axis_index("lon")
    size = chunk_of(width)
    masks = group_masks(size, part)

    def unpack(start):
        lines = pl.ds(start, size)
        values = [ref[lines] for ref in blocks]
        values = partner_order(values[:4], me) + partner_order(values[4:], me)
        for row, value in enumerate(transpose_groups(values, masks, part, range(rows))):
            out_ref[row, lines] = value

    each_chunk(width, size, unpack)


def press_out_kernel(part, _, tile_ref, *refs):
    blocks, out_hbm, tile_out, sems = natural(refs[:4]), refs[4], refs[5], refs[6]
    rows, width, _ = tile_ref.shape
    me = lax.axis_index("lon")
    size = chunk_of(width)
    masks = group_masks(size, part)
    low = lane_ids((size, LANES)) < LANES // 2
    count = sems.shape[0]
    copies = []
    for piece in range(count):
        begin, end = piece * width // count, (piece + 1) * width // count

        def unpack(start):
            lines = pl.ds(start + begin, size)
            values = partner_order([ref[lines] for ref in blocks], me)
            for row, value in enumerate(gather_groups(values, masks, part)):
                tile_out[row, lines] = jnp.where(low, tile_ref[row, lines], value)

        each_chunk(end - begin, size, unpack)
        copy = pltpu.make_async_copy(tile_out.at[:, begin:end], out_hbm.at[:, begin:end, LANES:], sems.at[piece])
        copy.start()
        copies.append(copy)
    for copy in copies:
        copy.wait()


def whole(shape):
    return pl.BlockSpec(shape, lambda step: (0,) * len(shape))


def tile_of(shape, index):
    return pl.BlockSpec((shape[0], shape[1], LANES), lambda step: (0, 0, index))


SMEM = pl.BlockSpec(memory_space=pltpu.SMEM)
ANY = pl.BlockSpec(memory_space=pl.ANY)


def call(kernel, out_shape, in_specs, out_specs, cost=2, grid=(1,), **more):
    return pl.pallas_call(
        kernel,
        grid=grid,
        out_shape=out_shape,
        in_specs=in_specs,
        out_specs=out_specs,
        compiler_params=pltpu.CompilerParams(vmem_limit_bytes=VMEM_BYTES),
        cost_estimate=pl.CostEstimate(flops=0, bytes_accessed=int(cost * 3.69e6), transcendentals=0),
        **more,
    )


def f32(*shape):
    return jax.ShapeDtypeStruct(shape, F32)


def exchange(blocks):
    pairs = [[(i, i ^ step) for i in range(4)] for step in range(4)]
    return [blocks[0]] + [lax.ppermute(blocks[step], "lon", pairs[step]) for step in (2, 3, 1)]


def packed_body(state, filter_flag, cutoff):
    rows, width, depth = state.shape
    levels = depth // 4
    bands = lax.axis_size("lat")
    nlon = 4 * width
    part = levels // 4
    forward, inverse, mode, sizes = spectral_plan(nlon)
    forward = [jnp.asarray(t) for t in forward]
    inverse = [jnp.asarray(t) for t in inverse]
    mode = jnp.asarray(mode)
    bounds, at = [], 0
    for size in sizes:
        bounds.append((at, at + 2 * size))
        at += 2 * size
    table_specs = [whole(t.shape) for t in forward] + [whole(t.shape) for t in inverse]
    block, spectrum, full = (width, LANES), (at, LANES), (rows, width, LANES)
    skip = width + 8
    first = (skip + rim_lines(width), LANES)
    second = (fold_lines(width) + width, LANES)
    rims = (2 * rim_lines(width) + 8, LANES)
    low_tile, high_tile = tile_of(state.shape, 0), tile_of(state.shape, 1)

    first_circle = exchange(
        call(
            functools.partial(zonal_kernel, part),
            [f32(*first)] * 4,
            [low_tile, high_tile],
            [whole(first)] * 4,
            scratch_shapes=[pltpu.VMEM(full, F32)],
        )(state, state)
    )
    *packs, vert = call(
        functools.partial(press_kernel, part),
        [f32(*second)] * 4 + [f32(*full)],
        [low_tile, high_tile],
        [whole(second)] * 4 + [whole(full)],
    )(state, state)
    second_circle = exchange(packs)

    to_north, to_south = call(
        functools.partial(rim_kernel, part, skip),
        [f32(*rims)] * 2,
        [SMEM] * 2 + [whole(first)] * 4,
        [whole(rims)] * 2,
    )(filter_flag, cutoff, *first_circle)
    from_south = lax.ppermute(to_north, "lat", [(i, i + 1) for i in range(bands - 1)])
    from_north = lax.ppermute(to_south, "lat", [(i + 1, i) for i in range(bands - 1)])

    *zonal_parts, zonal_spec = call(
        functools.partial(zonal_spec_kernel, bounds, part),
        [f32(*block)] * 4 + [f32(*spectrum)],
        [SMEM] * 2 + [whole(mode.shape), ANY] + [whole(first)] * 4 + table_specs,
        [whole(block)] * 4 + [whole(spectrum)],
    )(filter_flag, cutoff, mode, second_circle[3], *first_circle, *forward, *inverse)
    zonal_back = exchange(zonal_parts)
    edge_spec = call(
        functools.partial(edge_spec_kernel, bounds, part, skip),
        f32(*spectrum),
        [SMEM] * 2 + [whole(mode.shape)] + [whole(rims)] * 2 + [whole(first)] * 4 + table_specs[:6],
        whole(spectrum),
    )(filter_flag, cutoff, mode, from_south, from_north, *first_circle, *forward)

    *merid_parts, merid_spec = call(
        functools.partial(merid_spec_kernel, bounds, part),
        [f32(*block)] * 4 + [f32(*spectrum)],
        [SMEM] * 2 + [whole(mode.shape), whole(spectrum), ANY] + [whole(second)] * 4 + table_specs,
        [whole(block)] * 4 + [whole(spectrum)],
    )(filter_flag, cutoff, mode, edge_spec, zonal_spec, *second_circle, *forward, *inverse)
    merid_back = exchange(merid_parts)

    press_parts = call(
        functools.partial(press_back_kernel, bounds, part),
        [f32(*block)] * 4,
        [SMEM] * 2 + [whole(mode.shape)] + [whole(spectrum)] * 3 + [whole(second)] * 4 + table_specs,
        [whole(block)] * 4,
    )(filter_flag, cutoff, mode, zonal_spec, merid_spec, edge_spec, *second_circle, *forward, *inverse)
    press_back = exchange(press_parts)

    out = call(
        functools.partial(winds_out_kernel, part),
        f32(*state.shape),
        [whole(block)] * 8,
        low_tile,
    )(*zonal_back, *merid_back)
    pieces = next(n for n in (3, 5, 1) if width % (n * chunk_of(width)) == 0)
    return call(
        functools.partial(press_out_kernel, part),
        f32(*state.shape),
        [ANY, whole(full)] + [whole(block)] * 4,
        ANY,
        scratch_shapes=[pltpu.VMEM(full, F32), pltpu.SemaphoreType.DMA((pieces,))],
        input_output_aliases={0: 0},
    )(out, vert, *press_back)


def padded_2(block, sides, width, periodic):
    for axis, dim in sides:
        count = lax.axis_size(axis)
        forward = [(i, i + 1) for i in range(count - 1)]
        if periodic:
            forward.append((count - 1, 0))
        backward = [(target, source) for source, target in forward]
        low = lax.ppermute(
            lax.slice_in_dim(block, block.shape[dim] - width, None, axis=dim), axis, forward
        )
        high = lax.ppermute(lax.slice_in_dim(block, 0, width, axis=dim), axis, backward)
        block = jnp.concatenate([low, block, high], axis=dim)
    return block


def dft_tables(width):
    points = jnp.arange(width, dtype=jnp.int32)
    waves = jnp.arange(width // 2 + 1, dtype=jnp.int32)
    phase = points[:, None] * waves[None, :] % width
    angle = phase.astype(jnp.float32) * (2.0 * math.pi / width)
    weights = jnp.where((waves == 0) | (waves * 2 == width), 1.0, 2.0).astype(jnp.float32) / width
    return (jnp.cos(angle), jnp.sin(angle), weights)


def rims(stack):
    wide = padded_2(stack, (("lon", 1),), 1, True)
    return padded_2(wide, (("lat", 0),), 1, False)


def level_diff(field):
    padded = jnp.pad(field, ((0, 0), (0, 0), (1, 1)))
    return 0.5 * (padded[:, :, 2:] - padded[:, :, :-2])


def damped(block, cut_vec, tables):
    cos_table, sin_table, weights = tables
    highest = lax.Precision.HIGHEST
    wave_vals = jnp.arange(cos_table.shape[1]).astype(jnp.float32)
    ratio = cut_vec[:, None] / jnp.maximum(wave_vals, 1.0)[None, :]
    damping = (jnp.minimum(1.0, ratio * ratio) * weights[None, :])[:, None, :]
    real_part = jnp.einsum("rnq,nk->rqk", block, cos_table, precision=highest)
    imag_part = jnp.einsum("rnq,nk->rqk", block, sin_table, precision=highest)
    restored = jnp.einsum("rqk,nk->rnq", real_part * damping, cos_table, precision=highest)
    return restored + jnp.einsum("rqk,nk->rnq", imag_part * damping, sin_table, precision=highest)


def circle_local(fields, cut_rows, tables):
    return damped(fields, cut_rows, tables)


def polar(fields, row_flag, cut_rows, tables, apply):
    smooth = apply(fields, cut_rows, tables)
    return jnp.where(row_flag[:, None, None], smooth, fields)


def plain_body(state, filter_flag, cutoff):
    rows, width, depth = state.shape
    levels = depth // 4
    zonal_wind = state[:, :, :levels]
    merid_wind = state[:, :, levels : 2 * levels]
    vert_wind = state[:, :, 2 * levels : 3 * levels]
    pressure = state[:, :, 3 * levels :]
    nlat = rows * lax.axis_size("lat")
    nlon = width * lax.axis_size("lon")
    offset = lax.axis_index("lat") * rows
    row_ids = (offset + jnp.arange(-1, rows + 1)).astype(jnp.float32)
    cos_ext = jnp.cos(-0.5 * math.pi + (row_ids + 0.5) * math.pi / nlat)
    cos_mid = cos_ext[1:-1][:, None, None]
    tables = dft_tables(nlon)
    row_flag = filter_flag == 1
    cut_rows = cutoff.astype(jnp.float32)
    padded = rims(pressure)
    grad_x = (padded[1:-1, 2:] - padded[1:-1, :-2]) / (2.0 * cos_mid)
    grad_y = 0.5 * (padded[2:, 1:-1] - padded[:-2, 1:-1])
    grad_z = level_diff(pressure)
    zonal_pre = zonal_wind - WIND_COEF * grad_x
    merid_pre = merid_wind - WIND_COEF * grad_y
    vert_new = vert_wind - VERT_COEF * grad_z
    div_z = level_diff(vert_new)
    outgoing = jnp.stack([zonal_pre, merid_pre, pressure, div_z], 3).reshape(
        rows, width, 4 * levels
    )
    circles = lax.all_to_all(outgoing, "lon", split_axis=2, concat_axis=1, tiled=True)
    part_levels = circles.shape[2] // 4
    circles = circles.reshape(rows, nlon, part_levels, 4)
    winds_c = jnp.concatenate([circles[:, :, :, 0], circles[:, :, :, 1]], 2)
    press_c = circles[:, :, :, 2]
    div_z_c = circles[:, :, :, 3]
    winds_c = polar(winds_c, row_flag, cut_rows, tables, circle_local)
    zonal_c = winds_c[:, :, :part_levels]
    merid_c = winds_c[:, :, part_levels:]
    div_x = (jnp.roll(zonal_c, -1, 1) - jnp.roll(zonal_c, 1, 1)) / (2.0 * cos_mid)
    flux = padded_2(merid_c * cos_mid, (("lat", 0),), 1, False)
    div_y = (flux[2:] - flux[:-2]) / (2.0 * cos_mid)
    press_mid = press_c - PRESS_COEF * (div_x + div_y + div_z_c)
    press_c = polar(press_mid, row_flag, cut_rows, tables, circle_local)
    back = jnp.stack([zonal_c, merid_c, press_c], 3).reshape(rows, nlon, 3 * part_levels)
    patches = lax.all_to_all(back, "lon", split_axis=1, concat_axis=2, tiled=True).reshape(
        rows, width, levels, 3
    )
    return jnp.concatenate(
        [patches[:, :, :, 0], patches[:, :, :, 1], vert_new, patches[:, :, :, 2]], 2
    )


def body(state, filter_flag, cutoff):
    rows, width, depth = state.shape
    levels = depth // 4
    lanes_fit = rows == 8 and 2 * levels == LANES and width % 8 == 0
    if lax.axis_size("lon") == 4 and lanes_fit:
        return packed_body(state, filter_flag, cutoff)
    return plain_body(state, filter_flag, cutoff)


def solution(mesh):
    return jax.shard_map(
        body,
        mesh=mesh,
        in_specs=(P("lat", "lon", None), P("lat"), P("lat")),
        out_specs=P("lat", "lon", None),
        check_vma=False,
    )
```

```python
import functools
import math

import jax
import jax.numpy as jnp
import numpy as np
from jax import lax
from jax.experimental import pallas as pl
from jax.experimental.pallas import tpu as pltpu
from jax.sharding import PartitionSpec as P

WIND_COEF = 0.03
VERT_COEF = 0.2
PRESS_COEF = 0.03
LANES = 128
VMEM_BYTES = 40 * 1024 * 1024
F32 = jnp.float32
BF16 = jnp.bfloat16


def split_np(table):
    high = table.astype(np.float32).astype(jnp.bfloat16)
    low = (table - high.astype(np.float64)).astype(np.float32).astype(jnp.bfloat16)
    return high, low


def round_up(value, step):
    return -(-value // step) * step


@functools.lru_cache(maxsize=None)
def spectral_plan(nlon):
    quarter = nlon // 4
    points = np.arange(quarter)
    waves0 = np.arange(0, nlon // 2 + 1, 4)
    waves2 = np.arange(2, nlon // 2 + 1, 4)
    waves1 = np.arange(1, nlon // 2 + 1, 2)
    size0 = round_up(len(waves0), 16)
    size2 = round_up(len(waves2), 16)
    size1 = round_up(len(waves1), 8)

    def trig(waves, size):
        angle = 2.0 * np.pi * ((waves[:, None] * points[None, :]) % nlon) / nlon
        cos_t, sin_t = np.zeros((2, size, quarter))
        cos_t[: len(waves)] = np.cos(angle)
        sin_t[: len(waves)] = np.sin(angle)
        return cos_t, sin_t

    def padded(values, size):
        out = np.zeros(size)
        out[: len(values)] = values
        return out

    def weights(waves, size):
        ends = (waves == 0) | (2 * waves == nlon)
        return padded(np.where(ends, 1.0, 2.0) / nlon, size)

    cos0, sin0 = trig(waves0, size0)
    cos2, sin2 = trig(waves2, size2)
    cos1, sin1 = trig(waves1, size1)
    turn = padded(np.where(waves1 % 4 == 1, 1.0, -1.0), size1)[:, None]
    fwd0 = np.concatenate([cos0, sin0], 0)
    fwd2 = np.concatenate([cos2, sin2], 0)
    fwd1 = np.block([[cos1, -turn * sin1], [sin1, turn * cos1]])
    inv0 = (fwd0 * np.tile(weights(waves0, size0), 2)[:, None]).T
    inv2 = (fwd2 * np.tile(weights(waves2, size2), 2)[:, None]).T
    inv1 = (fwd1 * np.tile(weights(waves1, size1), 2)[:, None]).T
    forward = [part for table in (fwd0, fwd2, fwd1) for part in split_np(table)]
    inverse = [part for table in (inv0, inv2, inv1) for part in split_np(table)]

    def columns(waves, size):
        inv_wave = padded(1.0 / np.maximum(waves, 1), size)
        delta = padded(np.sin(2.0 * np.pi * waves / nlon), size)
        return np.concatenate([inv_wave, inv_wave]), np.concatenate([delta, -delta])

    per_wave = [columns(w, s) for w, s in ((waves0, size0), (waves2, size2), (waves1, size1))]
    mode = np.stack([np.concatenate([c[0] for c in per_wave]), np.concatenate([c[1] for c in per_wave])], 1)
    mode = np.pad(mode.astype(np.float32), ((0, 0), (0, LANES - 2)))
    return forward, inverse, mode, (size0, size2, size1)


def lane_ids(shape):
    return lax.broadcasted_iota(jnp.int32, shape, len(shape) - 1)


def select_groups(values, masks):
    out = None
    for mask, value in zip(masks, values):
        if value is not None:
            out = value if out is None else jnp.where(mask, value, out)
    return out


def group_masks(size, part):
    group = lane_ids((size, LANES)) // part
    return [group == g for g in range(LANES // part)]


def transpose_groups(tiles, masks, part, wanted):
    count = len(tiles)
    turned = []
    for shift in range(count):
        mixed = select_groups([tiles[(shift + g) % count] if g in wanted else None for g in range(count)], masks)
        turned.append(pltpu.roll(mixed, shift * part, 1) if shift else mixed)
    return [select_groups([turned[(h - g) % count] for h in range(count)], masks) for g in wanted]


def gather_groups(blocks, masks, part):
    count = len(masks)
    turned = []
    for shift in range(count):
        mixed = [None] * count
        for g, block in enumerate(blocks):
            mixed[(4 + g - shift) % count] = block
        mixed = select_groups(mixed, masks)
        turned.append(pltpu.roll(mixed, shift * part, 1) if shift else mixed)
    return [select_groups([None] * 4 + [turned[(4 + g - row) % count] for g in range(4)], masks) for row in range(count)]


def partner_order(blocks, me):
    odd, far = lax.rem(me, 2) == 1, me >= 2
    a, b, c, d = blocks
    a, b, c, d = jnp.where(odd, b, a), jnp.where(odd, a, b), jnp.where(odd, d, c), jnp.where(odd, c, d)
    return [jnp.where(far, c, a), jnp.where(far, d, b), jnp.where(far, a, c), jnp.where(far, b, d)]


def chunk_of(size):
    return next(c for c in (24, 40, 16, 8) if size % c == 0)


def cut_value(flag_ref, cut_ref, row, nlon):
    return jnp.where(flag_ref[row] == 1, cut_ref[row], nlon).astype(F32)


def row_cosine(row, count):
    return jnp.sin((row.astype(F32) + 0.5) * (math.pi / count))


def levels_table(levels):
    shape = (2 * levels, 2 * levels)
    source = lax.broadcasted_iota(jnp.int32, shape, 0)
    target = lax.broadcasted_iota(jnp.int32, shape, 1)
    step = source % levels - target % levels
    diff = jnp.where(step == 1, 1.0, jnp.where(step == -1, -1.0, 0.0))
    rim = (target % levels == 0) | (target % levels == levels - 1)
    twice = jnp.where(step == 0, jnp.where(rim, -1.0, -2.0), jnp.where(abs(step) == 2, 1.0, 0.0))
    from_press, to_press = source >= levels, target >= levels
    table = jnp.where(from_press, jnp.where(to_press, twice, diff), jnp.where(to_press, -10.0 * diff, 0.0))
    return table.astype(BF16)


def each_chunk(size, step, work):
    def turn(index, carry):
        work(pl.multiple_of(index * step, 8))
        return carry

    lax.fori_loop(0, size // step, turn, 0, unroll=True)


def natural(refs):
    own, chip, far, core = refs
    return [own, core, chip, far]


def put(refs, start, values):
    for ref, value in zip(refs, values):
        ref[pl.ds(start, value.shape[0])] = value


def merid_row(wind_ref, tile_ref, row, lines):
    half = 0.5 * WIND_COEF
    value = wind_ref[row, lines]
    if row < tile_ref.shape[0] - 1:
        value = value - half * tile_ref[row + 1, lines]
    return value + half * tile_ref[row - 1, lines] if row else value


def zonal_kernel(part, wind_ref, tile_ref, *refs):
    packs, zonal_ref = refs[:4], refs[4]
    rows, width, _ = tile_ref.shape
    last = rows - 1
    levels = LANES // 2
    nlat = rows * lax.axis_size("lat")
    me = lax.axis_index("lon")
    first = lax.axis_index("lat") * rows
    place = lax.broadcasted_iota(jnp.int32, (width, LANES), 0)
    for row in range(rows):
        tile = tile_ref[row]
        after = jnp.where(place == width - 1, 0.0, pltpu.roll(tile, width - 1, 0))
        before = jnp.where(place == 0, 0.0, pltpu.roll(tile, 1, 0))
        scale = WIND_COEF / (2.0 * row_cosine(jnp.full((1, LANES), first + row), nlat))
        zonal_ref[row] = wind_ref[row] - pltpu.roll((after - before) * scale, levels, 1)

    size = chunk_of(width)
    masks = group_masks(size, part)

    def pack(start):
        lines = pl.ds(start, size)
        blocks = transpose_groups([zonal_ref[row, lines] for row in range(rows)], masks, part, range(4))
        put(packs, start, partner_order(blocks, me))

    each_chunk(width, size, pack)
    line = lax.broadcasted_iota(jnp.int32, (8, LANES), 0)
    sides = []
    for row in range(rows):
        side = jnp.where(line == 0, tile_ref[row, 0:8], 0.0)
        sides.append(jnp.where(line == 7, tile_ref[row, width - 8 : width], side))
    masks8 = group_masks(8, part)
    put(packs, width, partner_order(transpose_groups(sides, masks8, part, range(4, 8)), me))

    head = rim_lines(width)

    def pack_rim(start):
        tiles = []
        for begin in (start, jnp.minimum(start + head, width - 8)):
            lines = pl.ds(pl.multiple_of(begin, 8), 8)
            for row in (0, last):
                tiles += [merid_row(wind_ref, tile_ref, row, lines), tile_ref[row, lines]]
        put(packs, width + 8 + start, partner_order(transpose_groups(tiles, masks8, part, range(4, 8)), me))

    each_chunk(head, 8, pack_rim)


def rim_lines(width):
    return round_up(-(-width // 2), 8)


def fold_lines(width):
    return round_up(-(-width * 3 // 4), 8)


def press_kernel(part, wind_ref, tile_ref, _, *refs):
    packs, vert_ref = refs[:4], refs[4]
    rows, width, _ = tile_ref.shape
    levels = LANES // 2
    me = lax.axis_index("lon")
    masks8 = group_masks(8, part)
    head = fold_lines(width)
    tail = width - head

    def pack_merid(start, pair, fold=None):
        lines = pl.ds(start, 8)
        folded = pl.ds(start - pair * tail + head if fold is None else fold, 8)
        tiles = [merid_row(wind_ref, tile_ref, row, lines) for row in range(1, rows - 1)]
        one = merid_row(wind_ref, tile_ref, 2 * pair + 1, folded)
        two = merid_row(wind_ref, tile_ref, 2 * pair + 2, folded)
        blocks = transpose_groups([one] + tiles + [two], masks8, part, range(4, 8))
        put(packs, start, partner_order(blocks, me))

    for pair in range(3):
        each_chunk(tail, 8, lambda start: pack_merid(pl.multiple_of(start + pair * tail, 8), pair))
    for start in range(3 * tail, head, 8):
        pack_merid(start, 2, start)

    gain = jnp.where(lane_ids((1, LANES)) < levels, -0.5 * VERT_COEF, 0.25 * PRESS_COEF * VERT_COEF)
    table = levels_table(levels)
    dot = functools.partial(jnp.dot, preferred_element_type=F32)
    for row in range(rows):
        tile = tile_ref[row]
        high = tile.astype(BF16)
        rest = (tile - high.astype(F32)).astype(BF16)
        vert_ref[row] = tile + gain * (dot(high, table) + dot(rest, table))

    size = chunk_of(width)
    masks = group_masks(size, part)

    def pack(start):
        lines = pl.ds(start, size)
        blocks = transpose_groups([vert_ref[row, lines] for row in range(rows)], masks, part, range(4, 8))
        put(packs, pl.multiple_of(start + head, 8), partner_order(blocks, me))

    each_chunk(width, size, pack)


def turn_groups(value, groups, part):
    shift = groups * part % LANES
    return pltpu.roll(value, shift, 1) if shift else value


def rim_kernel(part, skip, flag_ref, cut_ref, *refs):
    blocks, north_ref, south_ref = natural(refs[:4]), refs[4], refs[5]
    lines = blocks[0].shape[0] - skip
    first = lane_ids((lines, LANES)) // part % 4 < 2
    for half in range(2):
        one, two = blocks[2 * half][skip:], blocks[2 * half + 1][skip:]
        where = slice(half * lines, half * lines + lines)
        south_ref[where] = jnp.where(first, one, turn_groups(two, 2, part))
        north_ref[where] = jnp.where(first, turn_groups(two, -2, part), one)
    last = flag_ref.shape[0] - 1
    nlon = (skip - 8) * 4
    north_ref[2 * lines :] = jnp.full((8, LANES), cut_value(flag_ref, cut_ref, last, nlon), F32)
    south_ref[2 * lines :] = jnp.full((8, LANES), cut_value(flag_ref, cut_ref, 0, nlon), F32)


def edge_spec_kernel(bounds, part, skip, flag_ref, cut_ref, mode_ref, south_ref, north_ref, _, *refs):
    blocks, forward, spec_ref = natural(refs[:4]), refs[4:10], refs[10]
    lines = blocks[0].shape[0] - skip
    width = skip - 8
    half = 0.5 * WIND_COEF
    item = lane_ids((lines, LANES)) // part % 4
    fields = []
    for quarter, block in enumerate(blocks):
        where = slice(quarter // 2 * lines, quarter // 2 * lines + lines)
        own, south, north = block[skip:], south_ref[where], north_ref[where]
        at = 0 if quarter % 2 else 2
        merid_s, press_s = turn_groups(south, 1 - at, part), turn_groups(south, -1 - at, part)
        merid_n, press_n = turn_groups(north, 1 + at, part), turn_groups(north, at - 1, part)
        inner = own + half * jnp.where(item == 0, press_s, -press_n)
        outer = jnp.where(item == 1, merid_s - half * own, merid_n + half * own)
        value = jnp.where(item % 2 == 0, inner, outer)
        fields.append(jnp.concatenate([value, turn_groups(value, -4, part)], 0)[:width])
    rows = flag_ref.shape[0]
    group = lane_ids((1, LANES)) // part
    cut = jnp.where(group == 0, cut_value(flag_ref, cut_ref, 0, 4 * width), cut_value(flag_ref, cut_ref, rows - 1, 4 * width))
    cut = jnp.where(group == 1, south_ref[2 * lines : 2 * lines + 1], cut)
    cut = jnp.where(group == 3, north_ref[2 * lines : 2 * lines + 1], cut)
    damp = damping(cut, mode_ref[:, 0:1])
    for (low, high), value in zip(bounds, forward_dft(fields, forward)):
        spec_ref[low:high] = value * damp[low:high]


def merid_spec_kernel(bounds, part, flag_ref, cut_ref, mode_ref, edge_ref, *refs):
    blocks, forward, inverse, outs, spec_ref = natural(refs[:4]), refs[4:10], refs[10:16], refs[16:20], refs[20]
    rows = flag_ref.shape[0]
    width = outs[0].shape[0]
    head = fold_lines(width)
    tail = width - head
    group = lane_ids((tail, LANES)) // part
    fields = []
    for block in blocks:
        out = None
        for pair in range(3):
            value = block[pair * tail : pair * tail + tail]
            one, two = turn_groups(value, 2 * pair + 1, part), turn_groups(value, 2 * pair + 3, part)
            both = jnp.where(group == 2 * pair + 1, one, two)
            out = both if pair == 0 else jnp.where(group > 2 * pair, both, out)
        fields.append(jnp.concatenate([block[:head], out], 0))
    damp = damping(lane_cut(flag_ref, cut_ref, 4 * width, part), mode_ref[:, 0:1])
    group = lane_ids((1, LANES)) // part
    parts = []
    for (low, high), value in zip(bounds, forward_dft(fields, forward)):
        edge = edge_ref[low:high]
        value = jnp.where(group == 0, edge, value * damp[low:high])
        parts.append(jnp.where(group == rows - 1, turn_groups(edge, rows - 3, part), value))
        spec_ref[low:high] = parts[-1]
    inverse_dft(parts, inverse, outs)


def dot3(table_high, table_low, value):
    high = value.astype(BF16)
    low = (value - high.astype(F32)).astype(BF16)
    width = value.shape[1]
    dot = functools.partial(jnp.dot, preferred_element_type=F32)
    both = dot(table_high[...], jnp.concatenate([high, low], 1))
    return both[:, :width] + both[:, width:] + dot(table_low[...], high)


def by_place(me, dif0, dif1):
    odd = lax.rem(me, 2) == 1
    sign = jnp.where(me >= 2, -1.0, 1.0).astype(F32)
    return jnp.where(odd, dif1, dif0) * sign, jnp.where(odd, dif0, dif1) * sign


def parity_sign(me):
    return jnp.where(lax.rem(me, 2) == 1, -1.0, 1.0).astype(F32)


def forward_dft(quarters, tables):
    me = lax.axis_index("lon")
    own, core, chip, far = quarters
    sum0, sum1 = own + chip, core + far
    dif0, dif1 = by_place(me, own - chip, core - far)
    return (
        dot3(tables[0], tables[1], sum0 + sum1),
        dot3(tables[2], tables[3], (sum0 - sum1) * parity_sign(me)),
        dot3(tables[4], tables[5], jnp.concatenate([dif0, dif1], 0)),
    )


def inverse_dft(parts, tables, outs):
    me = lax.axis_index("lon")
    even = dot3(tables[0], tables[1], parts[0])
    other = dot3(tables[2], tables[3], parts[1]) * parity_sign(me)
    both = dot3(tables[4], tables[5], parts[2])
    quarter = even.shape[0]
    dif0, dif1 = by_place(me, both[:quarter], both[quarter:])
    plus, minus = even + other, even - other
    outs[0][...] = plus + dif0
    outs[1][...] = minus + dif1
    outs[2][...] = plus - dif0
    outs[3][...] = minus - dif1


def lane_rows(pick, rows, part):
    group = lane_ids((1, LANES)) // part
    out = jnp.zeros((1, LANES), F32)
    for row in range(rows):
        out = jnp.where(group == row, pick(row), out)
    return out


def lane_cut(flag_ref, cut_ref, nlon, part):
    rows = flag_ref.shape[0]
    return lane_rows(lambda row: cut_value(flag_ref, cut_ref, row, nlon), rows, part)


def lane_cosine(shift, rows, part):
    row = lane_ids((1, LANES)) // part + lax.axis_index("lat") * rows + shift
    return row_cosine(row, rows * lax.axis_size("lat"))


def damping(cut, inv_wave):
    ratio = cut * inv_wave
    return jnp.minimum(1.0, ratio * ratio)


def zonal_spec_kernel(bounds, part, flag_ref, cut_ref, mode_ref, _, q0, q2, q3, q1, *refs):
    forward, inverse, outs, spec_ref = refs[:6], refs[6:12], refs[12:16], refs[16]
    rows = flag_ref.shape[0]
    width = outs[0].shape[0]
    me = lax.axis_index("lon")
    quarters = (q0, q1, q2, q3)
    scale = WIND_COEF / (2.0 * lane_cosine(0, rows, part))
    line = lax.broadcasted_iota(jnp.int32, (8, LANES), 0)
    sides = partner_order([q[width : width + 8] for q in quarters], me)
    starts = [jnp.where(line == 0, scale * pltpu.roll(sides[(q + 3) % 4], 1, 0), 0.0) for q in range(4)]
    ends = [jnp.where(line == 7, scale * pltpu.roll(sides[(q + 1) % 4], 7, 0), 0.0) for q in range(4)]
    starts, ends = partner_order(starts, me), partner_order(ends, me)
    fields = [
        jnp.concatenate([q[0:8] + start, q[8 : width - 8], q[width - 8 : width] - end], 0)
        for q, start, end in zip(quarters, starts, ends)
    ]
    damp = damping(lane_cut(flag_ref, cut_ref, 4 * width, part), mode_ref[:, 0:1])
    parts = [value * damp[b[0] : b[1]] for b, value in zip(bounds, forward_dft(fields, forward))]
    for (low, high), value in zip(bounds, parts):
        spec_ref[low:high] = value
    inverse_dft(parts, inverse, outs)


def press_back_kernel(bounds, part, flag_ref, cut_ref, mode_ref, zonal_ref, merid_ref, edge_ref, *refs):
    quarters, forward, inverse, outs = natural(refs[:4]), refs[4:10], refs[10:16], refs[16:]
    skip = quarters[0].shape[0] - outs[0].shape[0]
    rows = flag_ref.shape[0]
    nlon = 4 * inverse[0].shape[0]
    band = lax.axis_index("lat")
    mode = mode_ref[...]
    damp = damping(lane_cut(flag_ref, cut_ref, nlon, part), mode[:, 0:1])
    cosine = lane_cosine(0, rows, part)
    below = jnp.where(band == 0, 0.0, lane_cosine(-1, rows, part))
    above = jnp.where(band == lax.axis_size("lat") - 1, 0.0, lane_cosine(1, rows, part))
    half_inv = 0.5 / cosine
    group = lane_ids((1, LANES)) // part
    flux = merid_ref[...] * cosine
    edge = edge_ref[...]
    north = jnp.where(group == rows - 1, turn_groups(edge, rows - 4, part) * above, turn_groups(flux, -1, part))
    south = jnp.where(group == 0, turn_groups(edge, -1, part) * below, turn_groups(flux, 1, part))
    div_y = (north - south) * half_inv
    zonal = zonal_ref[...]
    slope = mode[:, 1:2] / cosine
    parts = []
    for (low, high), press in zip(bounds, forward_dft([q[skip:] for q in quarters], forward)):
        mid = (low + high) // 2
        swapped = jnp.concatenate([zonal[mid:high], zonal[low:mid]], 0)
        div = swapped * slope[low:high] + div_y[low:high]
        parts.append((press - PRESS_COEF * div) * damp[low:high])
    inverse_dft(parts, inverse, outs)


def winds_out_kernel(part, *refs):
    blocks, out_ref = natural(refs[:4]) + natural(refs[4:8]), refs[8]
    rows, width, _ = out_ref.shape
    me = lax.axis_index("lon")
    size = chunk_of(width)
    masks = group_masks(size, part)

    def unpack(start):
        lines = pl.ds(start, size)
        values = [ref[lines] for ref in blocks]
        values = partner_order(values[:4], me) + partner_order(values[4:], me)
        for row, value in enumerate(transpose_groups(values, masks, part, range(rows))):
            out_ref[row, lines] = value

    each_chunk(width, size, unpack)


def press_out_kernel(part, _, tile_ref, *refs):
    blocks, out_hbm, tile_out, sems = natural(refs[:4]), refs[4], refs[5], refs[6]
    rows, width, _ = tile_ref.shape
    me = lax.axis_index("lon")
    size = chunk_of(width)
    masks = group_masks(size, part)
    low = lane_ids((size, LANES)) < LANES // 2
    count = sems.shape[0]
    copies = []
    for piece in range(count):
        begin, end = piece * width // count, (piece + 1) * width // count

        def unpack(start):
            lines = pl.ds(start + begin, size)
            values = partner_order([ref[lines] for ref in blocks], me)
            for row, value in enumerate(gather_groups(values, masks, part)):
                tile_out[row, lines] = jnp.where(low, tile_ref[row, lines], value)

        each_chunk(end - begin, size, unpack)
        copy = pltpu.make_async_copy(tile_out.at[:, begin:end], out_hbm.at[:, begin:end, LANES:], sems.at[piece])
        copy.start()
        copies.append(copy)
    for copy in copies:
        copy.wait()


def whole(shape):
    return pl.BlockSpec(shape, lambda step: (0,) * len(shape))


def tile_of(shape, index):
    return pl.BlockSpec((shape[0], shape[1], LANES), lambda step: (0, 0, index))


SMEM = pl.BlockSpec(memory_space=pltpu.SMEM)
ANY = pl.BlockSpec(memory_space=pl.ANY)


def call(kernel, out_shape, in_specs, out_specs, cost=2, grid=(1,), **more):
    return pl.pallas_call(
        kernel,
        grid=grid,
        out_shape=out_shape,
        in_specs=in_specs,
        out_specs=out_specs,
        compiler_params=pltpu.CompilerParams(vmem_limit_bytes=VMEM_BYTES),
        cost_estimate=pl.CostEstimate(flops=0, bytes_accessed=int(cost * 3.69e6), transcendentals=0),
        **more,
    )


def f32(*shape):
    return jax.ShapeDtypeStruct(shape, F32)


def exchange(blocks):
    pairs = [[(i, i ^ step) for i in range(4)] for step in range(4)]
    return [blocks[0]] + [lax.ppermute(blocks[step], "lon", pairs[step]) for step in (2, 3, 1)]


def packed_body(state, filter_flag, cutoff):
    rows, width, depth = state.shape
    levels = depth // 4
    bands = lax.axis_size("lat")
    nlon = 4 * width
    part = levels // 4
    forward, inverse, mode, sizes = spectral_plan(nlon)
    forward = [jnp.asarray(t) for t in forward]
    inverse = [jnp.asarray(t) for t in inverse]
    mode = jnp.asarray(mode)
    bounds, at = [], 0
    for size in sizes:
        bounds.append((at, at + 2 * size))
        at += 2 * size
    table_specs = [whole(t.shape) for t in forward] + [whole(t.shape) for t in inverse]
    block, spectrum, full = (width, LANES), (at, LANES), (rows, width, LANES)
    skip = width + 8
    first = (skip + rim_lines(width), LANES)
    second = (fold_lines(width) + width, LANES)
    rims = (2 * rim_lines(width) + 8, LANES)
    low_tile, high_tile = tile_of(state.shape, 0), tile_of(state.shape, 1)

    first_circle = exchange(
        call(
            functools.partial(zonal_kernel, part),
            [f32(*first)] * 4,
            [low_tile, high_tile],
            [whole(first)] * 4,
            scratch_shapes=[pltpu.VMEM(full, F32)],
        )(state, state)
    )
    *packs, vert = call(
        functools.partial(press_kernel, part),
        [f32(*second)] * 4 + [f32(*full)],
        [low_tile, high_tile, ANY],
        [whole(second)] * 4 + [whole(full)],
    )(state, state, first_circle[1])
    second_circle = exchange(packs)

    to_north, to_south = call(
        functools.partial(rim_kernel, part, skip),
        [f32(*rims)] * 2,
        [SMEM] * 2 + [whole(first)] * 4,
        [whole(rims)] * 2,
    )(filter_flag, cutoff, *first_circle)
    from_south = lax.ppermute(to_north, "lat", [(i, i + 1) for i in range(bands - 1)])
    from_north = lax.ppermute(to_south, "lat", [(i + 1, i) for i in range(bands - 1)])

    *zonal_parts, zonal_spec = call(
        functools.partial(zonal_spec_kernel, bounds, part),
        [f32(*block)] * 4 + [f32(*spectrum)],
        [SMEM] * 2 + [whole(mode.shape), ANY] + [whole(first)] * 4 + table_specs,
        [whole(block)] * 4 + [whole(spectrum)],
    )(filter_flag, cutoff, mode, second_circle[3], *first_circle, *forward, *inverse)
    zonal_back = exchange(zonal_parts)
    edge_spec = call(
        functools.partial(edge_spec_kernel, bounds, part, skip),
        f32(*spectrum),
        [SMEM] * 2 + [whole(mode.shape)] + [whole(rims)] * 2 + [ANY] + [whole(first)] * 4 + table_specs[:6],
        whole(spectrum),
    )(filter_flag, cutoff, mode, from_south, from_north, zonal_spec, *first_circle, *forward)

    *merid_parts, merid_spec = call(
        functools.partial(merid_spec_kernel, bounds, part),
        [f32(*block)] * 4 + [f32(*spectrum)],
        [SMEM] * 2 + [whole(mode.shape), whole(spectrum)] + [whole(second)] * 4 + table_specs,
        [whole(block)] * 4 + [whole(spectrum)],
    )(filter_flag, cutoff, mode, edge_spec, *second_circle, *forward, *inverse)
    merid_back = exchange(merid_parts)

    press_parts = call(
        functools.partial(press_back_kernel, bounds, part),
        [f32(*block)] * 4,
        [SMEM] * 2 + [whole(mode.shape)] + [whole(spectrum)] * 3 + [whole(second)] * 4 + table_specs,
        [whole(block)] * 4,
    )(filter_flag, cutoff, mode, zonal_spec, merid_spec, edge_spec, *second_circle, *forward, *inverse)
    press_back = exchange(press_parts)

    out = call(
        functools.partial(winds_out_kernel, part),
        f32(*state.shape),
        [whole(block)] * 8,
        low_tile,
    )(*zonal_back, *merid_back)
    pieces = next(n for n in (3, 5, 1) if width % (n * chunk_of(width)) == 0)
    return call(
        functools.partial(press_out_kernel, part),
        f32(*state.shape),
        [ANY, whole(full)] + [whole(block)] * 4,
        ANY,
        scratch_shapes=[pltpu.VMEM(full, F32), pltpu.SemaphoreType.DMA((pieces,))],
        input_output_aliases={0: 0},
    )(out, vert, *press_back)


def padded_2(block, sides, width, periodic):
    for axis, dim in sides:
        count = lax.axis_size(axis)
        forward = [(i, i + 1) for i in range(count - 1)]
        if periodic:
            forward.append((count - 1, 0))
        backward = [(target, source) for source, target in forward]
        low = lax.ppermute(
            lax.slice_in_dim(block, block.shape[dim] - width, None, axis=dim), axis, forward
        )
        high = lax.ppermute(lax.slice_in_dim(block, 0, width, axis=dim), axis, backward)
        block = jnp.concatenate([low, block, high], axis=dim)
    return block


def dft_tables(width):
    points = jnp.arange(width, dtype=jnp.int32)
    waves = jnp.arange(width // 2 + 1, dtype=jnp.int32)
    phase = points[:, None] * waves[None, :] % width
    angle = phase.astype(jnp.float32) * (2.0 * math.pi / width)
    weights = jnp.where((waves == 0) | (waves * 2 == width), 1.0, 2.0).astype(jnp.float32) / width
    return (jnp.cos(angle), jnp.sin(angle), weights)


def rims(stack):
    wide = padded_2(stack, (("lon", 1),), 1, True)
    return padded_2(wide, (("lat", 0),), 1, False)


def level_diff(field):
    padded = jnp.pad(field, ((0, 0), (0, 0), (1, 1)))
    return 0.5 * (padded[:, :, 2:] - padded[:, :, :-2])


def damped(block, cut_vec, tables):
    cos_table, sin_table, weights = tables
    highest = lax.Precision.HIGHEST
    wave_vals = jnp.arange(cos_table.shape[1]).astype(jnp.float32)
    ratio = cut_vec[:, None] / jnp.maximum(wave_vals, 1.0)[None, :]
    damping = (jnp.minimum(1.0, ratio * ratio) * weights[None, :])[:, None, :]
    real_part = jnp.einsum("rnq,nk->rqk", block, cos_table, precision=highest)
    imag_part = jnp.einsum("rnq,nk->rqk", block, sin_table, precision=highest)
    restored = jnp.einsum("rqk,nk->rnq", real_part * damping, cos_table, precision=highest)
    return restored + jnp.einsum("rqk,nk->rnq", imag_part * damping, sin_table, precision=highest)


def circle_local(fields, cut_rows, tables):
    return damped(fields, cut_rows, tables)


def polar(fields, row_flag, cut_rows, tables, apply):
    smooth = apply(fields, cut_rows, tables)
    return jnp.where(row_flag[:, None, None], smooth, fields)


def plain_body(state, filter_flag, cutoff):
    rows, width, depth = state.shape
    levels = depth // 4
    zonal_wind = state[:, :, :levels]
    merid_wind = state[:, :, levels : 2 * levels]
    vert_wind = state[:, :, 2 * levels : 3 * levels]
    pressure = state[:, :, 3 * levels :]
    nlat = rows * lax.axis_size("lat")
    nlon = width * lax.axis_size("lon")
    offset = lax.axis_index("lat") * rows
    row_ids = (offset + jnp.arange(-1, rows + 1)).astype(jnp.float32)
    cos_ext = jnp.cos(-0.5 * math.pi + (row_ids + 0.5) * math.pi / nlat)
    cos_mid = cos_ext[1:-1][:, None, None]
    tables = dft_tables(nlon)
    row_flag = filter_flag == 1
    cut_rows = cutoff.astype(jnp.float32)
    padded = rims(pressure)
    grad_x = (padded[1:-1, 2:] - padded[1:-1, :-2]) / (2.0 * cos_mid)
    grad_y = 0.5 * (padded[2:, 1:-1] - padded[:-2, 1:-1])
    grad_z = level_diff(pressure)
    zonal_pre = zonal_wind - WIND_COEF * grad_x
    merid_pre = merid_wind - WIND_COEF * grad_y
    vert_new = vert_wind - VERT_COEF * grad_z
    div_z = level_diff(vert_new)
    outgoing = jnp.stack([zonal_pre, merid_pre, pressure, div_z], 3).reshape(
        rows, width, 4 * levels
    )
    circles = lax.all_to_all(outgoing, "lon", split_axis=2, concat_axis=1, tiled=True)
    part_levels = circles.shape[2] // 4
    circles = circles.reshape(rows, nlon, part_levels, 4)
    winds_c = jnp.concatenate([circles[:, :, :, 0], circles[:, :, :, 1]], 2)
    press_c = circles[:, :, :, 2]
    div_z_c = circles[:, :, :, 3]
    winds_c = polar(winds_c, row_flag, cut_rows, tables, circle_local)
    zonal_c = winds_c[:, :, :part_levels]
    merid_c = winds_c[:, :, part_levels:]
    div_x = (jnp.roll(zonal_c, -1, 1) - jnp.roll(zonal_c, 1, 1)) / (2.0 * cos_mid)
    flux = padded_2(merid_c * cos_mid, (("lat", 0),), 1, False)
    div_y = (flux[2:] - flux[:-2]) / (2.0 * cos_mid)
    press_mid = press_c - PRESS_COEF * (div_x + div_y + div_z_c)
    press_c = polar(press_mid, row_flag, cut_rows, tables, circle_local)
    back = jnp.stack([zonal_c, merid_c, press_c], 3).reshape(rows, nlon, 3 * part_levels)
    patches = lax.all_to_all(back, "lon", split_axis=1, concat_axis=2, tiled=True).reshape(
        rows, width, levels, 3
    )
    return jnp.concatenate(
        [patches[:, :, :, 0], patches[:, :, :, 1], vert_new, patches[:, :, :, 2]], 2
    )


def body(state, filter_flag, cutoff):
    rows, width, depth = state.shape
    levels = depth // 4
    lanes_fit = rows == 8 and 2 * levels == LANES and width % 8 == 0
    if lax.axis_size("lon") == 4 and lanes_fit:
        return packed_body(state, filter_flag, cutoff)
    return plain_body(state, filter_flag, cutoff)


def solution(mesh):
    return jax.shard_map(
        body,
        mesh=mesh,
        in_specs=(P("lat", "lon", None), P("lat"), P("lat")),
        out_specs=P("lat", "lon", None),
        check_vma=False,
    )
```

```python
import functools
import math

import jax
import jax.numpy as jnp
import numpy as np
from jax import lax
from jax.experimental import pallas as pl
from jax.experimental.pallas import tpu as pltpu
from jax.sharding import PartitionSpec as P

WIND_COEF = 0.03
VERT_COEF = 0.2
PRESS_COEF = 0.03
LANES = 128
VMEM_BYTES = 40 * 1024 * 1024
F32 = jnp.float32
BF16 = jnp.bfloat16


def split_np(table):
    high = table.astype(np.float32).astype(jnp.bfloat16)
    low = (table - high.astype(np.float64)).astype(np.float32).astype(jnp.bfloat16)
    return high, low


def round_up(value, step):
    return -(-value // step) * step


@functools.lru_cache(maxsize=None)
def spectral_plan(nlon):
    quarter = nlon // 4
    points = np.arange(quarter)
    waves0 = np.arange(0, nlon // 2 + 1, 4)
    waves2 = np.arange(2, nlon // 2 + 1, 4)
    waves1 = np.arange(1, nlon // 2 + 1, 2)
    size0 = round_up(len(waves0), 16)
    size2 = round_up(len(waves2), 16)
    size1 = round_up(len(waves1), 8)

    def trig(waves, size):
        angle = 2.0 * np.pi * ((waves[:, None] * points[None, :]) % nlon) / nlon
        cos_t, sin_t = np.zeros((2, size, quarter))
        cos_t[: len(waves)] = np.cos(angle)
        sin_t[: len(waves)] = np.sin(angle)
        return cos_t, sin_t

    def padded(values, size):
        out = np.zeros(size)
        out[: len(values)] = values
        return out

    def weights(waves, size):
        ends = (waves == 0) | (2 * waves == nlon)
        return padded(np.where(ends, 1.0, 2.0) / nlon, size)

    cos0, sin0 = trig(waves0, size0)
    cos2, sin2 = trig(waves2, size2)
    cos1, sin1 = trig(waves1, size1)
    turn = padded(np.where(waves1 % 4 == 1, 1.0, -1.0), size1)[:, None]
    fwd0 = np.concatenate([cos0, sin0], 0)
    fwd2 = np.concatenate([cos2, sin2], 0)
    fwd1 = np.block([[cos1, -turn * sin1], [sin1, turn * cos1]])
    inv0 = (fwd0 * np.tile(weights(waves0, size0), 2)[:, None]).T
    inv2 = (fwd2 * np.tile(weights(waves2, size2), 2)[:, None]).T
    inv1 = (fwd1 * np.tile(weights(waves1, size1), 2)[:, None]).T
    forward = [part for table in (fwd0, fwd2, fwd1) for part in split_np(table)]
    inverse = [part for table in (inv0, inv2, inv1) for part in split_np(table)]

    def columns(waves, size):
        inv_wave = padded(1.0 / np.maximum(waves, 1), size)
        delta = padded(np.sin(2.0 * np.pi * waves / nlon), size)
        return np.concatenate([inv_wave, inv_wave]), np.concatenate([delta, -delta])

    per_wave = [columns(w, s) for w, s in ((waves0, size0), (waves2, size2), (waves1, size1))]
    mode = np.stack([np.concatenate([c[0] for c in per_wave]), np.concatenate([c[1] for c in per_wave])], 1)
    mode = np.pad(mode.astype(np.float32), ((0, 0), (0, LANES - 2)))
    return forward, inverse, mode, (size0, size2, size1)


def lane_ids(shape):
    return lax.broadcasted_iota(jnp.int32, shape, len(shape) - 1)


def select_groups(values, masks):
    out = None
    for mask, value in zip(masks, values):
        if value is not None:
            out = value if out is None else jnp.where(mask, value, out)
    return out


def group_masks(size, part):
    group = lane_ids((size, LANES)) // part
    return [group == g for g in range(LANES // part)]


def transpose_groups(tiles, masks, part, wanted):
    count = len(tiles)
    turned = []
    for shift in range(count):
        mixed = select_groups([tiles[(shift + g) % count] if g in wanted else None for g in range(count)], masks)
        turned.append(pltpu.roll(mixed, shift * part, 1) if shift else mixed)
    return [select_groups([turned[(h - g) % count] for h in range(count)], masks) for g in wanted]


def gather_groups(blocks, masks, part):
    count = len(masks)
    turned = []
    for shift in range(count):
        mixed = [None] * count
        for g, block in enumerate(blocks):
            mixed[(4 + g - shift) % count] = block
        mixed = select_groups(mixed, masks)
        turned.append(pltpu.roll(mixed, shift * part, 1) if shift else mixed)
    return [select_groups([None] * 4 + [turned[(4 + g - row) % count] for g in range(4)], masks) for row in range(count)]


def partner_order(blocks, me):
    odd, far = lax.rem(me, 2) == 1, me >= 2
    a, b, c, d = blocks
    a, b, c, d = jnp.where(odd, b, a), jnp.where(odd, a, b), jnp.where(odd, d, c), jnp.where(odd, c, d)
    return [jnp.where(far, c, a), jnp.where(far, d, b), jnp.where(far, a, c), jnp.where(far, b, d)]


def chunk_of(size):
    return next(c for c in (24, 40, 16, 8) if size % c == 0)


def cut_value(flag_ref, cut_ref, row, nlon):
    return jnp.where(flag_ref[row] == 1, cut_ref[row], nlon).astype(F32)


def row_cosine(row, count):
    return jnp.sin((row.astype(F32) + 0.5) * (math.pi / count))


def levels_table(levels):
    shape = (2 * levels, 2 * levels)
    source = lax.broadcasted_iota(jnp.int32, shape, 0)
    target = lax.broadcasted_iota(jnp.int32, shape, 1)
    step = source % levels - target % levels
    diff = jnp.where(step == 1, 1.0, jnp.where(step == -1, -1.0, 0.0))
    rim = (target % levels == 0) | (target % levels == levels - 1)
    twice = jnp.where(step == 0, jnp.where(rim, -1.0, -2.0), jnp.where(abs(step) == 2, 1.0, 0.0))
    from_press, to_press = source >= levels, target >= levels
    table = jnp.where(from_press, jnp.where(to_press, twice, diff), jnp.where(to_press, -10.0 * diff, 0.0))
    return table.astype(BF16)


def each_chunk(size, step, work):
    def turn(index, carry):
        work(pl.multiple_of(index * step, 8))
        return carry

    lax.fori_loop(0, size // step, turn, 0, unroll=True)


def natural(refs):
    own, chip, far, core = refs
    return [own, core, chip, far]


def put(refs, start, values):
    for ref, value in zip(refs, values):
        ref[pl.ds(start, value.shape[0])] = value


def merid_row(wind_ref, tile_ref, row, lines):
    half = 0.5 * WIND_COEF
    value = wind_ref[row, lines]
    if row < tile_ref.shape[0] - 1:
        value = value - half * tile_ref[row + 1, lines]
    return value + half * tile_ref[row - 1, lines] if row else value


def zonal_kernel(part, wind_ref, tile_ref, *refs):
    packs, zonal_ref = refs[:4], refs[4]
    rows, width, _ = tile_ref.shape
    levels = LANES // 2
    nlat = rows * lax.axis_size("lat")
    me = lax.axis_index("lon")
    first = lax.axis_index("lat") * rows
    place = lax.broadcasted_iota(jnp.int32, (width, LANES), 0)
    for row in range(rows):
        tile = tile_ref[row]
        after = jnp.where(place == width - 1, 0.0, pltpu.roll(tile, width - 1, 0))
        before = jnp.where(place == 0, 0.0, pltpu.roll(tile, 1, 0))
        scale = WIND_COEF / (2.0 * row_cosine(jnp.full((1, LANES), first + row), nlat))
        zonal_ref[row] = wind_ref[row] - pltpu.roll((after - before) * scale, levels, 1)

    size = chunk_of(width)
    masks = group_masks(size, part)

    def pack(start):
        lines = pl.ds(start, size)
        blocks = transpose_groups([zonal_ref[row, lines] for row in range(rows)], masks, part, range(4))
        put(packs, start, partner_order(blocks, me))

    each_chunk(width, size, pack)
    line = lax.broadcasted_iota(jnp.int32, (8, LANES), 0)
    sides = []
    for row in range(rows):
        side = jnp.where(line == 0, tile_ref[row, 0:8], 0.0)
        sides.append(jnp.where(line == 7, tile_ref[row, width - 8 : width], side))
    masks8 = group_masks(8, part)
    put(packs, width, partner_order(transpose_groups(sides, masks8, part, range(4, 8)), me))

def edge_kernel(part, *refs):
    (wind_first, wind_last), (tile_first, tile_last), packs = refs[:2], refs[2:4], refs[4:]
    _, width, _ = tile_first.shape
    me = lax.axis_index("lon")
    half = 0.5 * WIND_COEF
    head = rim_lines(width)
    masks = group_masks(8, part)

    def pack(start):
        tiles = []
        for begin in (start, jnp.minimum(start + head, width - 8)):
            lines = pl.ds(pl.multiple_of(begin, 8), 8)
            tiles += [wind_first[0, lines] - half * tile_first[1, lines], tile_first[0, lines]]
            tiles += [wind_last[1, lines] + half * tile_last[0, lines], tile_last[1, lines]]
        put(packs, start, partner_order(transpose_groups(tiles, masks, part, range(4, 8)), me))

    each_chunk(head, 8, pack)


def rim_lines(width):
    return round_up(-(-width // 2), 8)


def fold_lines(width):
    return round_up(-(-width * 3 // 4), 8)


def press_kernel(part, wind_ref, tile_ref, _, *refs):
    packs, vert_ref = refs[:4], refs[4]
    rows, width, _ = tile_ref.shape
    levels = LANES // 2
    me = lax.axis_index("lon")
    masks8 = group_masks(8, part)
    head = fold_lines(width)
    tail = width - head

    def pack_merid(start, pair, fold=None):
        lines = pl.ds(start, 8)
        folded = pl.ds(start - pair * tail + head if fold is None else fold, 8)
        tiles = [merid_row(wind_ref, tile_ref, row, lines) for row in range(1, rows - 1)]
        one = merid_row(wind_ref, tile_ref, 2 * pair + 1, folded)
        two = merid_row(wind_ref, tile_ref, 2 * pair + 2, folded)
        blocks = transpose_groups([one] + tiles + [two], masks8, part, range(4, 8))
        put(packs, start, partner_order(blocks, me))

    for pair in range(3):
        each_chunk(tail, 8, lambda start: pack_merid(pl.multiple_of(start + pair * tail, 8), pair))
    for start in range(3 * tail, head, 8):
        pack_merid(start, 2, start)

    gain = jnp.where(lane_ids((1, LANES)) < levels, -0.5 * VERT_COEF, 0.25 * PRESS_COEF * VERT_COEF)
    table = levels_table(levels)
    dot = functools.partial(jnp.dot, preferred_element_type=F32)
    for row in range(rows):
        tile = tile_ref[row]
        high = tile.astype(BF16)
        rest = (tile - high.astype(F32)).astype(BF16)
        vert_ref[row] = tile + gain * (dot(high, table) + dot(rest, table))

    size = chunk_of(width)
    masks = group_masks(size, part)

    def pack(start):
        lines = pl.ds(start, size)
        blocks = transpose_groups([vert_ref[row, lines] for row in range(rows)], masks, part, range(4, 8))
        put(packs, pl.multiple_of(start + head, 8), partner_order(blocks, me))

    each_chunk(width, size, pack)


def turn_groups(value, groups, part):
    shift = groups * part % LANES
    return pltpu.roll(value, shift, 1) if shift else value


def rim_kernel(part, skip, flag_ref, cut_ref, *refs):
    blocks, north_ref, south_ref = natural(refs[:4]), refs[-2], refs[-1]
    lines = blocks[0].shape[0]
    first = lane_ids((lines, LANES)) // part % 4 < 2
    for half in range(2):
        one, two = blocks[2 * half][...], blocks[2 * half + 1][...]
        where = slice(half * lines, half * lines + lines)
        south_ref[where] = jnp.where(first, one, turn_groups(two, 2, part))
        north_ref[where] = jnp.where(first, turn_groups(two, -2, part), one)
    last = flag_ref.shape[0] - 1
    nlon = (skip - 8) * 4
    north_ref[2 * lines :] = jnp.full((8, LANES), cut_value(flag_ref, cut_ref, last, nlon), F32)
    south_ref[2 * lines :] = jnp.full((8, LANES), cut_value(flag_ref, cut_ref, 0, nlon), F32)


def edge_spec_kernel(bounds, part, skip, flag_ref, cut_ref, mode_ref, south_ref, north_ref, _, *refs):
    blocks, forward, spec_ref = natural(refs[:4]), refs[4:10], refs[10]
    lines = blocks[0].shape[0]
    width = skip - 8
    half = 0.5 * WIND_COEF
    item = lane_ids((lines, LANES)) // part % 4
    fields = []
    for quarter, block in enumerate(blocks):
        where = slice(quarter // 2 * lines, quarter // 2 * lines + lines)
        own, south, north = block[...], south_ref[where], north_ref[where]
        at = 0 if quarter % 2 else 2
        merid_s, press_s = turn_groups(south, 1 - at, part), turn_groups(south, -1 - at, part)
        merid_n, press_n = turn_groups(north, 1 + at, part), turn_groups(north, at - 1, part)
        inner = own + half * jnp.where(item == 0, press_s, -press_n)
        outer = jnp.where(item == 1, merid_s - half * own, merid_n + half * own)
        value = jnp.where(item % 2 == 0, inner, outer)
        fields.append(jnp.concatenate([value, turn_groups(value, -4, part)], 0)[:width])
    rows = flag_ref.shape[0]
    group = lane_ids((1, LANES)) // part
    cut = jnp.where(group == 0, cut_value(flag_ref, cut_ref, 0, 4 * width), cut_value(flag_ref, cut_ref, rows - 1, 4 * width))
    cut = jnp.where(group == 1, south_ref[2 * lines : 2 * lines + 1], cut)
    cut = jnp.where(group == 3, north_ref[2 * lines : 2 * lines + 1], cut)
    damp = damping(cut, mode_ref[:, 0:1])
    for (low, high), value in zip(bounds, forward_dft(fields, forward)):
        spec_ref[low:high] = value * damp[low:high]


def merid_spec_kernel(bounds, part, flag_ref, cut_ref, mode_ref, edge_ref, *refs):
    blocks, forward, inverse, outs, spec_ref = natural(refs[:4]), refs[4:10], refs[10:16], refs[16:20], refs[20]
    rows = flag_ref.shape[0]
    width = outs[0].shape[0]
    head = fold_lines(width)
    tail = width - head
    group = lane_ids((tail, LANES)) // part
    fields = []
    for block in blocks:
        out = None
        for pair in range(3):
            value = block[pair * tail : pair * tail + tail]
            one, two = turn_groups(value, 2 * pair + 1, part), turn_groups(value, 2 * pair + 3, part)
            both = jnp.where(group == 2 * pair + 1, one, two)
            out = both if pair == 0 else jnp.where(group > 2 * pair, both, out)
        fields.append(jnp.concatenate([block[:head], out], 0))
    damp = damping(lane_cut(flag_ref, cut_ref, 4 * width, part), mode_ref[:, 0:1])
    group = lane_ids((1, LANES)) // part
    parts = []
    for (low, high), value in zip(bounds, forward_dft(fields, forward)):
        edge = edge_ref[low:high]
        value = jnp.where(group == 0, edge, value * damp[low:high])
        parts.append(jnp.where(group == rows - 1, turn_groups(edge, rows - 3, part), value))
        spec_ref[low:high] = parts[-1]
    inverse_dft(parts, inverse, outs)


def dot3(table_high, table_low, value):
    high = value.astype(BF16)
    low = (value - high.astype(F32)).astype(BF16)
    width = value.shape[1]
    dot = functools.partial(jnp.dot, preferred_element_type=F32)
    both = dot(table_high[...], jnp.concatenate([high, low], 1))
    return both[:, :width] + both[:, width:] + dot(table_low[...], high)


def by_place(me, dif0, dif1):
    odd = lax.rem(me, 2) == 1
    sign = jnp.where(me >= 2, -1.0, 1.0).astype(F32)
    return jnp.where(odd, dif1, dif0) * sign, jnp.where(odd, dif0, dif1) * sign


def parity_sign(me):
    return jnp.where(lax.rem(me, 2) == 1, -1.0, 1.0).astype(F32)


def forward_dft(quarters, tables):
    me = lax.axis_index("lon")
    own, core, chip, far = quarters
    sum0, sum1 = own + chip, core + far
    dif0, dif1 = by_place(me, own - chip, core - far)
    return (
        dot3(tables[0], tables[1], sum0 + sum1),
        dot3(tables[2], tables[3], (sum0 - sum1) * parity_sign(me)),
        dot3(tables[4], tables[5], jnp.concatenate([dif0, dif1], 0)),
    )


def inverse_dft(parts, tables, outs):
    me = lax.axis_index("lon")
    even = dot3(tables[0], tables[1], parts[0])
    other = dot3(tables[2], tables[3], parts[1]) * parity_sign(me)
    both = dot3(tables[4], tables[5], parts[2])
    quarter = even.shape[0]
    dif0, dif1 = by_place(me, both[:quarter], both[quarter:])
    plus, minus = even + other, even - other
    outs[0][...] = plus + dif0
    outs[1][...] = minus + dif1
    outs[2][...] = plus - dif0
    outs[3][...] = minus - dif1


def lane_rows(pick, rows, part):
    group = lane_ids((1, LANES)) // part
    out = jnp.zeros((1, LANES), F32)
    for row in range(rows):
        out = jnp.where(group == row, pick(row), out)
    return out


def lane_cut(flag_ref, cut_ref, nlon, part):
    rows = flag_ref.shape[0]
    return lane_rows(lambda row: cut_value(flag_ref, cut_ref, row, nlon), rows, part)


def lane_cosine(shift, rows, part):
    row = lane_ids((1, LANES)) // part + lax.axis_index("lat") * rows + shift
    return row_cosine(row, rows * lax.axis_size("lat"))


def damping(cut, inv_wave):
    ratio = cut * inv_wave
    return jnp.minimum(1.0, ratio * ratio)


def zonal_spec_kernel(bounds, part, flag_ref, cut_ref, mode_ref, _, q0, q2, q3, q1, *refs):
    forward, inverse, outs, spec_ref = refs[:6], refs[6:12], refs[12:16], refs[16]
    rows = flag_ref.shape[0]
    width = outs[0].shape[0]
    me = lax.axis_index("lon")
    quarters = (q0, q1, q2, q3)
    scale = WIND_COEF / (2.0 * lane_cosine(0, rows, part))
    line = lax.broadcasted_iota(jnp.int32, (8, LANES), 0)
    sides = partner_order([q[width : width + 8] for q in quarters], me)
    starts = [jnp.where(line == 0, scale * pltpu.roll(sides[(q + 3) % 4], 1, 0), 0.0) for q in range(4)]
    ends = [jnp.where(line == 7, scale * pltpu.roll(sides[(q + 1) % 4], 7, 0), 0.0) for q in range(4)]
    starts, ends = partner_order(starts, me), partner_order(ends, me)
    fields = [
        jnp.concatenate([q[0:8] + start, q[8 : width - 8], q[width - 8 : width] - end], 0)
        for q, start, end in zip(quarters, starts, ends)
    ]
    damp = damping(lane_cut(flag_ref, cut_ref, 4 * width, part), mode_ref[:, 0:1])
    parts = [value * damp[b[0] : b[1]] for b, value in zip(bounds, forward_dft(fields, forward))]
    for (low, high), value in zip(bounds, parts):
        spec_ref[low:high] = value
    inverse_dft(parts, inverse, outs)


def press_back_kernel(bounds, part, flag_ref, cut_ref, mode_ref, zonal_ref, merid_ref, edge_ref, *refs):
    quarters, forward, inverse, outs = natural(refs[:4]), refs[4:10], refs[10:16], refs[16:]
    skip = quarters[0].shape[0] - outs[0].shape[0]
    rows = flag_ref.shape[0]
    nlon = 4 * inverse[0].shape[0]
    band = lax.axis_index("lat")
    mode = mode_ref[...]
    damp = damping(lane_cut(flag_ref, cut_ref, nlon, part), mode[:, 0:1])
    cosine = lane_cosine(0, rows, part)
    below = jnp.where(band == 0, 0.0, lane_cosine(-1, rows, part))
    above = jnp.where(band == lax.axis_size("lat") - 1, 0.0, lane_cosine(1, rows, part))
    half_inv = 0.5 / cosine
    group = lane_ids((1, LANES)) // part
    flux = merid_ref[...] * cosine
    edge = edge_ref[...]
    north = jnp.where(group == rows - 1, turn_groups(edge, rows - 4, part) * above, turn_groups(flux, -1, part))
    south = jnp.where(group == 0, turn_groups(edge, -1, part) * below, turn_groups(flux, 1, part))
    div_y = (north - south) * half_inv
    zonal = zonal_ref[...]
    slope = mode[:, 1:2] / cosine
    parts = []
    for (low, high), press in zip(bounds, forward_dft([q[skip:] for q in quarters], forward)):
        mid = (low + high) // 2
        swapped = jnp.concatenate([zonal[mid:high], zonal[low:mid]], 0)
        div = swapped * slope[low:high] + div_y[low:high]
        parts.append((press - PRESS_COEF * div) * damp[low:high])
    inverse_dft(parts, inverse, outs)


def winds_out_kernel(part, *refs):
    blocks, out_ref = natural(refs[:4]) + natural(refs[4:8]), refs[8]
    rows, width, _ = out_ref.shape
    me = lax.axis_index("lon")
    size = chunk_of(width)
    masks = group_masks(size, part)

    def unpack(start):
        lines = pl.ds(start, size)
        values = [ref[lines] for ref in blocks]
        values = partner_order(values[:4], me) + partner_order(values[4:], me)
        for row, value in enumerate(transpose_groups(values, masks, part, range(rows))):
            out_ref[row, lines] = value

    each_chunk(width, size, unpack)


def press_out_kernel(part, _, tile_ref, *refs):
    blocks, out_hbm, tile_out, sems = natural(refs[:4]), refs[4], refs[5], refs[6]
    rows, width, _ = tile_ref.shape
    me = lax.axis_index("lon")
    size = chunk_of(width)
    masks = group_masks(size, part)
    low = lane_ids((size, LANES)) < LANES // 2
    count = sems.shape[0]
    copies = []
    for piece in range(count):
        begin, end = piece * width // count, (piece + 1) * width // count

        def unpack(start):
            lines = pl.ds(start + begin, size)
            values = partner_order([ref[lines] for ref in blocks], me)
            for row, value in enumerate(gather_groups(values, masks, part)):
                tile_out[row, lines] = jnp.where(low, tile_ref[row, lines], value)

        each_chunk(end - begin, size, unpack)
        copy = pltpu.make_async_copy(tile_out.at[:, begin:end], out_hbm.at[:, begin:end, LANES:], sems.at[piece])
        copy.start()
        copies.append(copy)
    for copy in copies:
        copy.wait()


def whole(shape):
    return pl.BlockSpec(shape, lambda step: (0,) * len(shape))


def tile_of(shape, index):
    return pl.BlockSpec((shape[0], shape[1], LANES), lambda step: (0, 0, index))


SMEM = pl.BlockSpec(memory_space=pltpu.SMEM)
ANY = pl.BlockSpec(memory_space=pl.ANY)


def call(kernel, out_shape, in_specs, out_specs, cost=2, grid=(1,), **more):
    return pl.pallas_call(
        kernel,
        grid=grid,
        out_shape=out_shape,
        in_specs=in_specs,
        out_specs=out_specs,
        compiler_params=pltpu.CompilerParams(vmem_limit_bytes=VMEM_BYTES),
        cost_estimate=pl.CostEstimate(flops=0, bytes_accessed=int(cost * 3.69e6), transcendentals=0),
        **more,
    )


def f32(*shape):
    return jax.ShapeDtypeStruct(shape, F32)


def send(block, step):
    return lax.ppermute(block, "lon", [(i, i ^ step) for i in range(4)])


def exchange(blocks):
    return [blocks[0]] + [send(blocks[step], step) for step in (2, 3, 1)]


def packed_body(state, filter_flag, cutoff):
    rows, width, depth = state.shape
    levels = depth // 4
    bands = lax.axis_size("lat")
    nlon = 4 * width
    part = levels // 4
    forward, inverse, mode, sizes = spectral_plan(nlon)
    forward = [jnp.asarray(t) for t in forward]
    inverse = [jnp.asarray(t) for t in inverse]
    mode = jnp.asarray(mode)
    bounds, at = [], 0
    for size in sizes:
        bounds.append((at, at + 2 * size))
        at += 2 * size
    table_specs = [whole(t.shape) for t in forward] + [whole(t.shape) for t in inverse]
    block, spectrum, full = (width, LANES), (at, LANES), (rows, width, LANES)
    skip = width + 8
    second = (fold_lines(width) + width, LANES)
    rims = (2 * rim_lines(width) + 8, LANES)
    low_tile, high_tile = tile_of(state.shape, 0), tile_of(state.shape, 1)

    edges = (rim_lines(width), LANES)
    sided = (skip, LANES)

    def two_rows(row, index):
        return pl.BlockSpec((2, width, LANES), lambda step: (row, 0, index))

    edge_packs = call(
        functools.partial(edge_kernel, part),
        [f32(*edges)] * 4,
        [two_rows(0, 0), two_rows(rows // 2 - 1, 0), two_rows(0, 1), two_rows(rows // 2 - 1, 1)],
        [whole(edges)] * 4,
    )(state, state, state, state)
    zonal_packs = call(
        functools.partial(zonal_kernel, part),
        [f32(*sided)] * 4,
        [low_tile, high_tile],
        [whole(sided)] * 4,
        scratch_shapes=[pltpu.VMEM(full, F32)],
    )(state, state)
    edge_circle = exchange(edge_packs)
    first_circle = exchange(zonal_packs)
    *packs, vert = call(
        functools.partial(press_kernel, part),
        [f32(*second)] * 4 + [f32(*full)],
        [low_tile, high_tile, ANY],
        [whole(second)] * 4 + [whole(full)],
    )(state, state, edge_circle[1])
    second_circle = exchange(packs)

    edge_specs = [whole(edges)] * 4
    to_north, to_south = call(
        functools.partial(rim_kernel, part, skip),
        [f32(*rims)] * 2,
        [SMEM] * 2 + edge_specs + [ANY],
        [whole(rims)] * 2,
    )(filter_flag, cutoff, *edge_circle, vert)
    from_south = lax.ppermute(to_north, "lat", [(i, i + 1) for i in range(bands - 1)])
    from_north = lax.ppermute(to_south, "lat", [(i + 1, i) for i in range(bands - 1)])

    *zonal_parts, zonal_spec = call(
        functools.partial(zonal_spec_kernel, bounds, part),
        [f32(*block)] * 4 + [f32(*spectrum)],
        [SMEM] * 2 + [whole(mode.shape), ANY] + [whole(sided)] * 4 + table_specs,
        [whole(block)] * 4 + [whole(spectrum)],
    )(filter_flag, cutoff, mode, second_circle[3], *first_circle, *forward, *inverse)
    zonal_back = exchange(zonal_parts)
    edge_spec = call(
        functools.partial(edge_spec_kernel, bounds, part, skip),
        f32(*spectrum),
        [SMEM] * 2 + [whole(mode.shape)] + [whole(rims)] * 2 + [ANY] + edge_specs + table_specs[:6],
        whole(spectrum),
    )(filter_flag, cutoff, mode, from_south, from_north, zonal_spec, *edge_circle, *forward)

    *merid_parts, merid_spec = call(
        functools.partial(merid_spec_kernel, bounds, part),
        [f32(*block)] * 4 + [f32(*spectrum)],
        [SMEM] * 2 + [whole(mode.shape), whole(spectrum)] + [whole(second)] * 4 + table_specs,
        [whole(block)] * 4 + [whole(spectrum)],
    )(filter_flag, cutoff, mode, edge_spec, *second_circle, *forward, *inverse)
    merid_back = exchange(merid_parts)

    press_parts = call(
        functools.partial(press_back_kernel, bounds, part),
        [f32(*block)] * 4,
        [SMEM] * 2 + [whole(mode.shape)] + [whole(spectrum)] * 3 + [whole(second)] * 4 + table_specs,
        [whole(block)] * 4,
    )(filter_flag, cutoff, mode, zonal_spec, merid_spec, edge_spec, *second_circle, *forward, *inverse)
    press_back = exchange(press_parts)

    out = call(
        functools.partial(winds_out_kernel, part),
        f32(*state.shape),
        [whole(block)] * 8,
        low_tile,
    )(*zonal_back, *merid_back)
    pieces = next(n for n in (3, 5, 1) if width % (n * chunk_of(width)) == 0)
    return call(
        functools.partial(press_out_kernel, part),
        f32(*state.shape),
        [ANY, whole(full)] + [whole(block)] * 4,
        ANY,
        scratch_shapes=[pltpu.VMEM(full, F32), pltpu.SemaphoreType.DMA((pieces,))],
        input_output_aliases={0: 0},
    )(out, vert, *press_back)


def padded_2(block, sides, width, periodic):
    for axis, dim in sides:
        count = lax.axis_size(axis)
        forward = [(i, i + 1) for i in range(count - 1)]
        if periodic:
            forward.append((count - 1, 0))
        backward = [(target, source) for source, target in forward]
        low = lax.ppermute(
            lax.slice_in_dim(block, block.shape[dim] - width, None, axis=dim), axis, forward
        )
        high = lax.ppermute(lax.slice_in_dim(block, 0, width, axis=dim), axis, backward)
        block = jnp.concatenate([low, block, high], axis=dim)
    return block


def dft_tables(width):
    points = jnp.arange(width, dtype=jnp.int32)
    waves = jnp.arange(width // 2 + 1, dtype=jnp.int32)
    phase = points[:, None] * waves[None, :] % width
    angle = phase.astype(jnp.float32) * (2.0 * math.pi / width)
    weights = jnp.where((waves == 0) | (waves * 2 == width), 1.0, 2.0).astype(jnp.float32) / width
    return (jnp.cos(angle), jnp.sin(angle), weights)


def rims(stack):
    wide = padded_2(stack, (("lon", 1),), 1, True)
    return padded_2(wide, (("lat", 0),), 1, False)


def level_diff(field):
    padded = jnp.pad(field, ((0, 0), (0, 0), (1, 1)))
    return 0.5 * (padded[:, :, 2:] - padded[:, :, :-2])


def damped(block, cut_vec, tables):
    cos_table, sin_table, weights = tables
    highest = lax.Precision.HIGHEST
    wave_vals = jnp.arange(cos_table.shape[1]).astype(jnp.float32)
    ratio = cut_vec[:, None] / jnp.maximum(wave_vals, 1.0)[None, :]
    damping = (jnp.minimum(1.0, ratio * ratio) * weights[None, :])[:, None, :]
    real_part = jnp.einsum("rnq,nk->rqk", block, cos_table, precision=highest)
    imag_part = jnp.einsum("rnq,nk->rqk", block, sin_table, precision=highest)
    restored = jnp.einsum("rqk,nk->rnq", real_part * damping, cos_table, precision=highest)
    return restored + jnp.einsum("rqk,nk->rnq", imag_part * damping, sin_table, precision=highest)


def circle_local(fields, cut_rows, tables):
    return damped(fields, cut_rows, tables)


def polar(fields, row_flag, cut_rows, tables, apply):
    smooth = apply(fields, cut_rows, tables)
    return jnp.where(row_flag[:, None, None], smooth, fields)


def plain_body(state, filter_flag, cutoff):
    rows, width, depth = state.shape
    levels = depth // 4
    zonal_wind = state[:, :, :levels]
    merid_wind = state[:, :, levels : 2 * levels]
    vert_wind = state[:, :, 2 * levels : 3 * levels]
    pressure = state[:, :, 3 * levels :]
    nlat = rows * lax.axis_size("lat")
    nlon = width * lax.axis_size("lon")
    offset = lax.axis_index("lat") * rows
    row_ids = (offset + jnp.arange(-1, rows + 1)).astype(jnp.float32)
    cos_ext = jnp.cos(-0.5 * math.pi + (row_ids + 0.5) * math.pi / nlat)
    cos_mid = cos_ext[1:-1][:, None, None]
    tables = dft_tables(nlon)
    row_flag = filter_flag == 1
    cut_rows = cutoff.astype(jnp.float32)
    padded = rims(pressure)
    grad_x = (padded[1:-1, 2:] - padded[1:-1, :-2]) / (2.0 * cos_mid)
    grad_y = 0.5 * (padded[2:, 1:-1] - padded[:-2, 1:-1])
    grad_z = level_diff(pressure)
    zonal_pre = zonal_wind - WIND_COEF * grad_x
    merid_pre = merid_wind - WIND_COEF * grad_y
    vert_new = vert_wind - VERT_COEF * grad_z
    div_z = level_diff(vert_new)
    outgoing = jnp.stack([zonal_pre, merid_pre, pressure, div_z], 3).reshape(
        rows, width, 4 * levels
    )
    circles = lax.all_to_all(outgoing, "lon", split_axis=2, concat_axis=1, tiled=True)
    part_levels = circles.shape[2] // 4
    circles = circles.reshape(rows, nlon, part_levels, 4)
    winds_c = jnp.concatenate([circles[:, :, :, 0], circles[:, :, :, 1]], 2)
    press_c = circles[:, :, :, 2]
    div_z_c = circles[:, :, :, 3]
    winds_c = polar(winds_c, row_flag, cut_rows, tables, circle_local)
    zonal_c = winds_c[:, :, :part_levels]
    merid_c = winds_c[:, :, part_levels:]
    div_x = (jnp.roll(zonal_c, -1, 1) - jnp.roll(zonal_c, 1, 1)) / (2.0 * cos_mid)
    flux = padded_2(merid_c * cos_mid, (("lat", 0),), 1, False)
    div_y = (flux[2:] - flux[:-2]) / (2.0 * cos_mid)
    press_mid = press_c - PRESS_COEF * (div_x + div_y + div_z_c)
    press_c = polar(press_mid, row_flag, cut_rows, tables, circle_local)
    back = jnp.stack([zonal_c, merid_c, press_c], 3).reshape(rows, nlon, 3 * part_levels)
    patches = lax.all_to_all(back, "lon", split_axis=1, concat_axis=2, tiled=True).reshape(
        rows, width, levels, 3
    )
    return jnp.concatenate(
        [patches[:, :, :, 0], patches[:, :, :, 1], vert_new, patches[:, :, :, 2]], 2
    )


def body(state, filter_flag, cutoff):
    rows, width, depth = state.shape
    levels = depth // 4
    lanes_fit = rows == 8 and 2 * levels == LANES and width % 8 == 0
    if lax.axis_size("lon") == 4 and lanes_fit:
        return packed_body(state, filter_flag, cutoff)
    return plain_body(state, filter_flag, cutoff)


def solution(mesh):
    return jax.shard_map(
        body,
        mesh=mesh,
        in_specs=(P("lat", "lon", None), P("lat"), P("lat")),
        out_specs=P("lat", "lon", None),
        check_vma=False,
    )
```

```python
import functools
import math

import jax
import jax.numpy as jnp
import numpy as np
from jax import lax
from jax.experimental import pallas as pl
from jax.experimental.pallas import tpu as pltpu
from jax.sharding import PartitionSpec as P

WIND_COEF = 0.03
VERT_COEF = 0.2
PRESS_COEF = 0.03
LANES = 128
VMEM_BYTES = 40 * 1024 * 1024
F32 = jnp.float32
BF16 = jnp.bfloat16


def split_np(table):
    high = table.astype(np.float32).astype(jnp.bfloat16)
    low = (table - high.astype(np.float64)).astype(np.float32).astype(jnp.bfloat16)
    return high, low


def round_up(value, step):
    return -(-value // step) * step


@functools.lru_cache(maxsize=None)
def spectral_plan(nlon):
    quarter = nlon // 4
    points = np.arange(quarter)
    waves0 = np.arange(0, nlon // 2 + 1, 4)
    waves2 = np.arange(2, nlon // 2 + 1, 4)
    waves1 = np.arange(1, nlon // 2 + 1, 2)
    size0 = round_up(len(waves0), 16)
    size2 = round_up(len(waves2), 16)
    size1 = round_up(len(waves1), 8)

    def trig(waves, size):
        angle = 2.0 * np.pi * ((waves[:, None] * points[None, :]) % nlon) / nlon
        cos_t, sin_t = np.zeros((2, size, quarter))
        cos_t[: len(waves)] = np.cos(angle)
        sin_t[: len(waves)] = np.sin(angle)
        return cos_t, sin_t

    def padded(values, size):
        out = np.zeros(size)
        out[: len(values)] = values
        return out

    def weights(waves, size):
        ends = (waves == 0) | (2 * waves == nlon)
        return padded(np.where(ends, 1.0, 2.0) / nlon, size)

    cos0, sin0 = trig(waves0, size0)
    cos2, sin2 = trig(waves2, size2)
    cos1, sin1 = trig(waves1, size1)
    turn = padded(np.where(waves1 % 4 == 1, 1.0, -1.0), size1)[:, None]
    fwd0 = np.concatenate([cos0, sin0], 0)
    fwd2 = np.concatenate([cos2, sin2], 0)
    fwd1 = np.block([[cos1, -turn * sin1], [sin1, turn * cos1]])
    inv0 = (fwd0 * np.tile(weights(waves0, size0), 2)[:, None]).T
    inv2 = (fwd2 * np.tile(weights(waves2, size2), 2)[:, None]).T
    inv1 = (fwd1 * np.tile(weights(waves1, size1), 2)[:, None]).T
    forward = [part for table in (fwd0, fwd2, fwd1) for part in split_np(table)]
    inverse = [part for table in (inv0, inv2, inv1) for part in split_np(table)]

    def columns(waves, size):
        inv_wave = padded(1.0 / np.maximum(waves, 1), size)
        delta = padded(np.sin(2.0 * np.pi * waves / nlon), size)
        return np.concatenate([inv_wave, inv_wave]), np.concatenate([delta, -delta])

    per_wave = [columns(w, s) for w, s in ((waves0, size0), (waves2, size2), (waves1, size1))]
    mode = np.stack([np.concatenate([c[0] for c in per_wave]), np.concatenate([c[1] for c in per_wave])], 1)
    mode = np.pad(mode.astype(np.float32), ((0, 0), (0, LANES - 2)))
    return forward, inverse, mode, (size0, size2, size1)


def lane_ids(shape):
    return lax.broadcasted_iota(jnp.int32, shape, len(shape) - 1)


def select_groups(values, masks):
    out = None
    for mask, value in zip(masks, values):
        if value is not None:
            out = value if out is None else jnp.where(mask, value, out)
    return out


def group_masks(size, part):
    group = lane_ids((size, LANES)) // part
    return [group == g for g in range(LANES // part)]


def transpose_groups(tiles, masks, part, wanted):
    count = len(tiles)
    turned = []
    for shift in range(count):
        mixed = select_groups([tiles[(shift + g) % count] if g in wanted else None for g in range(count)], masks)
        turned.append(pltpu.roll(mixed, shift * part, 1) if shift else mixed)
    return [select_groups([turned[(h - g) % count] for h in range(count)], masks) for g in wanted]


def gather_groups(blocks, masks, part):
    count = len(masks)
    turned = []
    for shift in range(count):
        mixed = [None] * count
        for g, block in enumerate(blocks):
            mixed[(4 + g - shift) % count] = block
        mixed = select_groups(mixed, masks)
        turned.append(pltpu.roll(mixed, shift * part, 1) if shift else mixed)
    return [select_groups([None] * 4 + [turned[(4 + g - row) % count] for g in range(4)], masks) for row in range(count)]


def partner_order(blocks, me):
    odd, far = lax.rem(me, 2) == 1, me >= 2
    a, b, c, d = blocks
    a, b, c, d = jnp.where(odd, b, a), jnp.where(odd, a, b), jnp.where(odd, d, c), jnp.where(odd, c, d)
    return [jnp.where(far, c, a), jnp.where(far, d, b), jnp.where(far, a, c), jnp.where(far, b, d)]


def chunk_of(size):
    return next(c for c in (24, 40, 16, 8) if size % c == 0)


def cut_value(flag_ref, cut_ref, row, nlon):
    return jnp.where(flag_ref[row] == 1, cut_ref[row], nlon).astype(F32)


def row_cosine(row, count):
    return jnp.sin((row.astype(F32) + 0.5) * (math.pi / count))


def levels_table(levels):
    shape = (2 * levels, 2 * levels)
    source = lax.broadcasted_iota(jnp.int32, shape, 0)
    target = lax.broadcasted_iota(jnp.int32, shape, 1)
    step = source % levels - target % levels
    diff = jnp.where(step == 1, 1.0, jnp.where(step == -1, -1.0, 0.0))
    rim = (target % levels == 0) | (target % levels == levels - 1)
    twice = jnp.where(step == 0, jnp.where(rim, -1.0, -2.0), jnp.where(abs(step) == 2, 1.0, 0.0))
    from_press, to_press = source >= levels, target >= levels
    table = jnp.where(from_press, jnp.where(to_press, twice, diff), jnp.where(to_press, -10.0 * diff, 0.0))
    return table.astype(BF16)


def each_chunk(size, step, work):
    def turn(index, carry):
        work(pl.multiple_of(index * step, 8))
        return carry

    lax.fori_loop(0, size // step, turn, 0, unroll=True)


def natural(refs):
    own, chip, far, core = refs
    return [own, core, chip, far]


def put(refs, start, values):
    for ref, value in zip(refs, values):
        ref[pl.ds(start, value.shape[0])] = value


def merid_row(wind_ref, tile_ref, row, lines):
    half = 0.5 * WIND_COEF
    value = wind_ref[row, lines]
    if row < tile_ref.shape[0] - 1:
        value = value - half * tile_ref[row + 1, lines]
    return value + half * tile_ref[row - 1, lines] if row else value


def zonal_kernel(part, wind_ref, tile_ref, *refs):
    packs, zonal_ref = refs[:4], refs[4]
    rows, width, _ = tile_ref.shape
    levels = LANES // 2
    nlat = rows * lax.axis_size("lat")
    me = lax.axis_index("lon")
    first = lax.axis_index("lat") * rows
    place = lax.broadcasted_iota(jnp.int32, (width, LANES), 0)
    for row in range(rows):
        tile = tile_ref[row]
        after = jnp.where(place == width - 1, 0.0, pltpu.roll(tile, width - 1, 0))
        before = jnp.where(place == 0, 0.0, pltpu.roll(tile, 1, 0))
        scale = WIND_COEF / (2.0 * row_cosine(jnp.full((1, LANES), first + row), nlat))
        zonal_ref[row] = wind_ref[row] - pltpu.roll((after - before) * scale, levels, 1)

    size = chunk_of(width)
    masks = group_masks(size, part)

    def pack(start):
        lines = pl.ds(start, size)
        blocks = transpose_groups([zonal_ref[row, lines] for row in range(rows)], masks, part, range(4))
        put(packs, start, partner_order(blocks, me))

    each_chunk(width, size, pack)
    line = lax.broadcasted_iota(jnp.int32, (8, LANES), 0)
    sides = []
    for row in range(rows):
        side = jnp.where(line == 0, tile_ref[row, 0:8], 0.0)
        sides.append(jnp.where(line == 7, tile_ref[row, width - 8 : width], side))
    masks8 = group_masks(8, part)
    put(packs, width, partner_order(transpose_groups(sides, masks8, part, range(4, 8)), me))

def edge_kernel(part, *refs):
    (wind_first, wind_last), (tile_first, tile_last), packs = refs[:2], refs[2:4], refs[4:]
    _, width, _ = tile_first.shape
    me = lax.axis_index("lon")
    half = 0.5 * WIND_COEF
    head = rim_lines(width)
    masks = group_masks(8, part)

    def pack(start):
        tiles = []
        for begin in (start, jnp.minimum(start + head, width - 8)):
            lines = pl.ds(pl.multiple_of(begin, 8), 8)
            tiles += [wind_first[0, lines] - half * tile_first[1, lines], tile_first[0, lines]]
            tiles += [wind_last[1, lines] + half * tile_last[0, lines], tile_last[1, lines]]
        put(packs, start, partner_order(transpose_groups(tiles, masks, part, range(4, 8)), me))

    each_chunk(head, 8, pack)


def rim_lines(width):
    return round_up(-(-width // 2), 8)


def fold_lines(width):
    return round_up(-(-width * 3 // 4), 8)


def press_kernel(part, wind_ref, tile_ref, _, *refs):
    packs, vert_ref = refs[:4], refs[4]
    rows, width, _ = tile_ref.shape
    levels = LANES // 2
    me = lax.axis_index("lon")
    masks8 = group_masks(8, part)
    head = fold_lines(width)
    tail = width - head

    def pack_merid(start, pair, fold=None):
        lines = pl.ds(start, 8)
        folded = pl.ds(start - pair * tail + head if fold is None else fold, 8)
        tiles = [merid_row(wind_ref, tile_ref, row, lines) for row in range(1, rows - 1)]
        one = merid_row(wind_ref, tile_ref, 2 * pair + 1, folded)
        two = merid_row(wind_ref, tile_ref, 2 * pair + 2, folded)
        blocks = transpose_groups([one] + tiles + [two], masks8, part, range(4, 8))
        put(packs, start, partner_order(blocks, me))

    for pair in range(3):
        each_chunk(tail, 8, lambda start: pack_merid(pl.multiple_of(start + pair * tail, 8), pair))
    for start in range(3 * tail, head, 8):
        pack_merid(start, 2, start)

    gain = jnp.where(lane_ids((1, LANES)) < levels, -0.5 * VERT_COEF, 0.25 * PRESS_COEF * VERT_COEF)
    table = levels_table(levels)
    dot = functools.partial(jnp.dot, preferred_element_type=F32)
    for row in range(rows):
        tile = tile_ref[row]
        high = tile.astype(BF16)
        rest = (tile - high.astype(F32)).astype(BF16)
        vert_ref[row] = tile + gain * (dot(high, table) + dot(rest, table))

    size = chunk_of(width)
    masks = group_masks(size, part)

    def pack(start):
        lines = pl.ds(start, size)
        blocks = transpose_groups([vert_ref[row, lines] for row in range(rows)], masks, part, range(4, 8))
        put(packs, pl.multiple_of(start + head, 8), partner_order(blocks, me))

    each_chunk(width, size, pack)


def turn_groups(value, groups, part):
    shift = groups * part % LANES
    return pltpu.roll(value, shift, 1) if shift else value


def rim_kernel(part, skip, flag_ref, cut_ref, *refs):
    blocks, north_ref, south_ref = natural(refs[:4]), refs[-2], refs[-1]
    lines = blocks[0].shape[0]
    first = lane_ids((lines, LANES)) // part % 4 < 2
    for half in range(2):
        one, two = blocks[2 * half][...], blocks[2 * half + 1][...]
        where = slice(half * lines, half * lines + lines)
        south_ref[where] = jnp.where(first, one, turn_groups(two, 2, part))
        north_ref[where] = jnp.where(first, turn_groups(two, -2, part), one)
    last = flag_ref.shape[0] - 1
    nlon = (skip - 8) * 4
    north_ref[2 * lines :] = jnp.full((8, LANES), cut_value(flag_ref, cut_ref, last, nlon), F32)
    south_ref[2 * lines :] = jnp.full((8, LANES), cut_value(flag_ref, cut_ref, 0, nlon), F32)


def edge_spec_kernel(bounds, part, skip, flag_ref, cut_ref, mode_ref, south_ref, north_ref, _, *refs):
    blocks, forward, spec_ref = natural(refs[:4]), refs[4:10], refs[10]
    lines = blocks[0].shape[0]
    width = skip - 8
    half = 0.5 * WIND_COEF
    item = lane_ids((lines, LANES)) // part % 4
    fields = []
    for quarter, block in enumerate(blocks):
        where = slice(quarter // 2 * lines, quarter // 2 * lines + lines)
        own, south, north = block[...], south_ref[where], north_ref[where]
        at = 0 if quarter % 2 else 2
        merid_s, press_s = turn_groups(south, 1 - at, part), turn_groups(south, -1 - at, part)
        merid_n, press_n = turn_groups(north, 1 + at, part), turn_groups(north, at - 1, part)
        inner = own + half * jnp.where(item == 0, press_s, -press_n)
        outer = jnp.where(item == 1, merid_s - half * own, merid_n + half * own)
        value = jnp.where(item % 2 == 0, inner, outer)
        fields.append(jnp.concatenate([value, turn_groups(value, -4, part)], 0)[:width])
    rows = flag_ref.shape[0]
    group = lane_ids((1, LANES)) // part
    cut = jnp.where(group == 0, cut_value(flag_ref, cut_ref, 0, 4 * width), cut_value(flag_ref, cut_ref, rows - 1, 4 * width))
    cut = jnp.where(group == 1, south_ref[2 * lines : 2 * lines + 1], cut)
    cut = jnp.where(group == 3, north_ref[2 * lines : 2 * lines + 1], cut)
    damp = damping(cut, mode_ref[:, 0:1])
    for (low, high), value in zip(bounds, forward_dft(fields, forward)):
        spec_ref[low:high] = value * damp[low:high]


def merid_spec_kernel(bounds, part, flag_ref, cut_ref, mode_ref, edge_ref, *refs):
    blocks, forward, inverse, outs, spec_ref = natural(refs[:4]), refs[4:10], refs[10:16], refs[16:20], refs[20]
    rows = flag_ref.shape[0]
    width = outs[0].shape[0]
    head = fold_lines(width)
    tail = width - head
    group = lane_ids((tail, LANES)) // part
    fields = []
    for block in blocks:
        out = None
        for pair in range(3):
            value = block[pair * tail : pair * tail + tail]
            one, two = turn_groups(value, 2 * pair + 1, part), turn_groups(value, 2 * pair + 3, part)
            both = jnp.where(group == 2 * pair + 1, one, two)
            out = both if pair == 0 else jnp.where(group > 2 * pair, both, out)
        fields.append(jnp.concatenate([block[:head], out], 0))
    damp = damping(lane_cut(flag_ref, cut_ref, 4 * width, part), mode_ref[:, 0:1])
    group = lane_ids((1, LANES)) // part
    parts = []
    for (low, high), value in zip(bounds, forward_dft(fields, forward)):
        edge = edge_ref[low:high]
        value = jnp.where(group == 0, edge, value * damp[low:high])
        parts.append(jnp.where(group == rows - 1, turn_groups(edge, rows - 3, part), value))
        spec_ref[low:high] = parts[-1]
    inverse_dft(parts, inverse, outs)


def dot3(table_high, table_low, value):
    high = value.astype(BF16)
    low = (value - high.astype(F32)).astype(BF16)
    width = value.shape[1]
    dot = functools.partial(jnp.dot, preferred_element_type=F32)
    both = dot(table_high[...], jnp.concatenate([high, low], 1))
    return both[:, :width] + both[:, width:] + dot(table_low[...], high)


def by_place(me, dif0, dif1):
    odd = lax.rem(me, 2) == 1
    sign = jnp.where(me >= 2, -1.0, 1.0).astype(F32)
    return jnp.where(odd, dif1, dif0) * sign, jnp.where(odd, dif0, dif1) * sign


def parity_sign(me):
    return jnp.where(lax.rem(me, 2) == 1, -1.0, 1.0).astype(F32)


def forward_dft(quarters, tables):
    me = lax.axis_index("lon")
    own, core, chip, far = quarters
    sum0, sum1 = own + chip, core + far
    dif0, dif1 = by_place(me, own - chip, core - far)
    return (
        dot3(tables[0], tables[1], sum0 + sum1),
        dot3(tables[2], tables[3], (sum0 - sum1) * parity_sign(me)),
        dot3(tables[4], tables[5], jnp.concatenate([dif0, dif1], 0)),
    )


def inverse_dft(parts, tables, outs):
    me = lax.axis_index("lon")
    even = dot3(tables[0], tables[1], parts[0])
    other = dot3(tables[2], tables[3], parts[1]) * parity_sign(me)
    both = dot3(tables[4], tables[5], parts[2])
    quarter = even.shape[0]
    dif0, dif1 = by_place(me, both[:quarter], both[quarter:])
    plus, minus = even + other, even - other
    outs[0][...] = plus + dif0
    outs[1][...] = minus + dif1
    outs[2][...] = plus - dif0
    outs[3][...] = minus - dif1


def lane_rows(pick, rows, part):
    group = lane_ids((1, LANES)) // part
    out = jnp.zeros((1, LANES), F32)
    for row in range(rows):
        out = jnp.where(group == row, pick(row), out)
    return out


def lane_cut(flag_ref, cut_ref, nlon, part):
    rows = flag_ref.shape[0]
    return lane_rows(lambda row: cut_value(flag_ref, cut_ref, row, nlon), rows, part)


def lane_cosine(shift, rows, part):
    row = lane_ids((1, LANES)) // part + lax.axis_index("lat") * rows + shift
    return row_cosine(row, rows * lax.axis_size("lat"))


def damping(cut, inv_wave):
    ratio = cut * inv_wave
    return jnp.minimum(1.0, ratio * ratio)


def zonal_spec_kernel(bounds, part, flag_ref, cut_ref, mode_ref, _, q0, q2, q3, q1, *refs):
    forward, inverse, outs, spec_ref = refs[:6], refs[6:12], refs[12:16], refs[16]
    rows = flag_ref.shape[0]
    width = outs[0].shape[0]
    me = lax.axis_index("lon")
    quarters = (q0, q1, q2, q3)
    scale = WIND_COEF / (2.0 * lane_cosine(0, rows, part))
    line = lax.broadcasted_iota(jnp.int32, (8, LANES), 0)
    sides = partner_order([q[width : width + 8] for q in quarters], me)
    starts = [jnp.where(line == 0, scale * pltpu.roll(sides[(q + 3) % 4], 1, 0), 0.0) for q in range(4)]
    ends = [jnp.where(line == 7, scale * pltpu.roll(sides[(q + 1) % 4], 7, 0), 0.0) for q in range(4)]
    starts, ends = partner_order(starts, me), partner_order(ends, me)
    fields = [
        jnp.concatenate([q[0:8] + start, q[8 : width - 8], q[width - 8 : width] - end], 0)
        for q, start, end in zip(quarters, starts, ends)
    ]
    damp = damping(lane_cut(flag_ref, cut_ref, 4 * width, part), mode_ref[:, 0:1])
    parts = [value * damp[b[0] : b[1]] for b, value in zip(bounds, forward_dft(fields, forward))]
    for (low, high), value in zip(bounds, parts):
        spec_ref[low:high] = value
    inverse_dft(parts, inverse, outs)


def press_back_kernel(bounds, part, flag_ref, cut_ref, mode_ref, zonal_ref, merid_ref, edge_ref, *refs):
    quarters, forward, inverse, outs = natural(refs[:4]), refs[4:10], refs[10:16], refs[16:]
    skip = quarters[0].shape[0] - outs[0].shape[0]
    rows = flag_ref.shape[0]
    nlon = 4 * inverse[0].shape[0]
    band = lax.axis_index("lat")
    mode = mode_ref[...]
    damp = damping(lane_cut(flag_ref, cut_ref, nlon, part), mode[:, 0:1])
    cosine = lane_cosine(0, rows, part)
    below = jnp.where(band == 0, 0.0, lane_cosine(-1, rows, part))
    above = jnp.where(band == lax.axis_size("lat") - 1, 0.0, lane_cosine(1, rows, part))
    half_inv = 0.5 / cosine
    group = lane_ids((1, LANES)) // part
    flux = merid_ref[...] * cosine
    edge = edge_ref[...]
    north = jnp.where(group == rows - 1, turn_groups(edge, rows - 4, part) * above, turn_groups(flux, -1, part))
    south = jnp.where(group == 0, turn_groups(edge, -1, part) * below, turn_groups(flux, 1, part))
    div_y = (north - south) * half_inv
    zonal = zonal_ref[...]
    slope = mode[:, 1:2] / cosine
    parts = []
    for (low, high), press in zip(bounds, forward_dft([q[skip:] for q in quarters], forward)):
        mid = (low + high) // 2
        swapped = jnp.concatenate([zonal[mid:high], zonal[low:mid]], 0)
        div = swapped * slope[low:high] + div_y[low:high]
        parts.append((press - PRESS_COEF * div) * damp[low:high])
    inverse_dft(parts, inverse, outs)


def winds_out_kernel(part, *refs):
    blocks, out_ref = natural(refs[:4]) + natural(refs[4:8]), refs[8]
    rows, width, _ = out_ref.shape
    me = lax.axis_index("lon")
    size = chunk_of(width)
    masks = group_masks(size, part)

    def unpack(start):
        lines = pl.ds(start, size)
        values = [ref[lines] for ref in blocks]
        values = partner_order(values[:4], me) + partner_order(values[4:], me)
        for row, value in enumerate(transpose_groups(values, masks, part, range(rows))):
            out_ref[row, lines] = value

    each_chunk(width, size, unpack)


def press_out_kernel(part, _, tile_ref, *refs):
    blocks, out_hbm, tile_out, sems = natural(refs[:4]), refs[4], refs[5], refs[6]
    rows, width, _ = tile_ref.shape
    me = lax.axis_index("lon")
    size = chunk_of(width)
    masks = group_masks(size, part)
    low = lane_ids((size, LANES)) < LANES // 2
    count = sems.shape[0]
    copies = []
    for piece in range(count):
        begin, end = piece * width // count, (piece + 1) * width // count

        def unpack(start):
            lines = pl.ds(start + begin, size)
            values = partner_order([ref[lines] for ref in blocks], me)
            for row, value in enumerate(gather_groups(values, masks, part)):
                tile_out[row, lines] = jnp.where(low, tile_ref[row, lines], value)

        each_chunk(end - begin, size, unpack)
        copy = pltpu.make_async_copy(tile_out.at[:, begin:end], out_hbm.at[:, begin:end, LANES:], sems.at[piece])
        copy.start()
        copies.append(copy)
    for copy in copies:
        copy.wait()


def whole(shape):
    return pl.BlockSpec(shape, lambda step: (0,) * len(shape))


def tile_of(shape, index):
    return pl.BlockSpec((shape[0], shape[1], LANES), lambda step: (0, 0, index))


SMEM = pl.BlockSpec(memory_space=pltpu.SMEM)
ANY = pl.BlockSpec(memory_space=pl.ANY)


def call(kernel, out_shape, in_specs, out_specs, cost=2, grid=(1,), **more):
    return pl.pallas_call(
        kernel,
        grid=grid,
        out_shape=out_shape,
        in_specs=in_specs,
        out_specs=out_specs,
        compiler_params=pltpu.CompilerParams(vmem_limit_bytes=VMEM_BYTES),
        cost_estimate=pl.CostEstimate(flops=int(cost * 1.15e9), bytes_accessed=int(cost * 3.69e6), transcendentals=0),
        **more,
    )


def f32(*shape):
    return jax.ShapeDtypeStruct(shape, F32)


def send(block, step):
    return lax.ppermute(block, "lon", [(i, i ^ step) for i in range(4)])


def exchange(blocks):
    return [blocks[0]] + [send(blocks[step], step) for step in (2, 3, 1)]


def packed_body(state, filter_flag, cutoff):
    rows, width, depth = state.shape
    levels = depth // 4
    bands = lax.axis_size("lat")
    nlon = 4 * width
    part = levels // 4
    forward, inverse, mode, sizes = spectral_plan(nlon)
    forward = [jnp.asarray(t) for t in forward]
    inverse = [jnp.asarray(t) for t in inverse]
    mode = jnp.asarray(mode)
    bounds, at = [], 0
    for size in sizes:
        bounds.append((at, at + 2 * size))
        at += 2 * size
    table_specs = [whole(t.shape) for t in forward] + [whole(t.shape) for t in inverse]
    block, spectrum, full = (width, LANES), (at, LANES), (rows, width, LANES)
    skip = width + 8
    second = (fold_lines(width) + width, LANES)
    rims = (2 * rim_lines(width) + 8, LANES)
    low_tile, high_tile = tile_of(state.shape, 0), tile_of(state.shape, 1)

    edges = (rim_lines(width), LANES)
    sided = (skip, LANES)

    def two_rows(row, index):
        return pl.BlockSpec((2, width, LANES), lambda step: (row, 0, index))

    edge_packs = call(
        functools.partial(edge_kernel, part),
        [f32(*edges)] * 4,
        [two_rows(0, 0), two_rows(rows // 2 - 1, 0), two_rows(0, 1), two_rows(rows // 2 - 1, 1)],
        [whole(edges)] * 4,
    )(state, state, state, state)
    zonal_packs = call(
        functools.partial(zonal_kernel, part),
        [f32(*sided)] * 4,
        [low_tile, high_tile],
        [whole(sided)] * 4,
        scratch_shapes=[pltpu.VMEM(full, F32)],
    )(state, state)
    edge_circle = exchange(edge_packs)
    first_circle = exchange(zonal_packs)
    *packs, vert = call(
        functools.partial(press_kernel, part),
        [f32(*second)] * 4 + [f32(*full)],
        [low_tile, high_tile, ANY],
        [whole(second)] * 4 + [whole(full)],
    )(state, state, edge_circle[1])
    second_circle = exchange(packs)

    edge_specs = [whole(edges)] * 4
    to_north, to_south = call(
        functools.partial(rim_kernel, part, skip),
        [f32(*rims)] * 2,
        [SMEM] * 2 + edge_specs + [ANY],
        [whole(rims)] * 2,
        cost=8,
    )(filter_flag, cutoff, *edge_circle, vert)
    from_south = lax.ppermute(to_north, "lat", [(i, i + 1) for i in range(bands - 1)])
    from_north = lax.ppermute(to_south, "lat", [(i + 1, i) for i in range(bands - 1)])

    *zonal_parts, zonal_spec = call(
        functools.partial(zonal_spec_kernel, bounds, part),
        [f32(*block)] * 4 + [f32(*spectrum)],
        [SMEM] * 2 + [whole(mode.shape), ANY] + [whole(sided)] * 4 + table_specs,
        [whole(block)] * 4 + [whole(spectrum)],
    )(filter_flag, cutoff, mode, second_circle[3], *first_circle, *forward, *inverse)
    zonal_back = exchange(zonal_parts)
    edge_spec = call(
        functools.partial(edge_spec_kernel, bounds, part, skip),
        f32(*spectrum),
        [SMEM] * 2 + [whole(mode.shape)] + [whole(rims)] * 2 + [ANY] + edge_specs + table_specs[:6],
        whole(spectrum),
    )(filter_flag, cutoff, mode, from_south, from_north, zonal_spec, *edge_circle, *forward)

    *merid_parts, merid_spec = call(
        functools.partial(merid_spec_kernel, bounds, part),
        [f32(*block)] * 4 + [f32(*spectrum)],
        [SMEM] * 2 + [whole(mode.shape), whole(spectrum)] + [whole(second)] * 4 + table_specs,
        [whole(block)] * 4 + [whole(spectrum)],
    )(filter_flag, cutoff, mode, edge_spec, *second_circle, *forward, *inverse)
    merid_back = exchange(merid_parts)

    press_parts = call(
        functools.partial(press_back_kernel, bounds, part),
        [f32(*block)] * 4,
        [SMEM] * 2 + [whole(mode.shape)] + [whole(spectrum)] * 3 + [whole(second)] * 4 + table_specs,
        [whole(block)] * 4,
    )(filter_flag, cutoff, mode, zonal_spec, merid_spec, edge_spec, *second_circle, *forward, *inverse)
    press_back = exchange(press_parts)

    out = call(
        functools.partial(winds_out_kernel, part),
        f32(*state.shape),
        [whole(block)] * 8,
        low_tile,
    )(*zonal_back, *merid_back)
    pieces = next(n for n in (3, 5, 1) if width % (n * chunk_of(width)) == 0)
    return call(
        functools.partial(press_out_kernel, part),
        f32(*state.shape),
        [ANY, whole(full)] + [whole(block)] * 4,
        ANY,
        scratch_shapes=[pltpu.VMEM(full, F32), pltpu.SemaphoreType.DMA((pieces,))],
        input_output_aliases={0: 0},
    )(out, vert, *press_back)


def padded_2(block, sides, width, periodic):
    for axis, dim in sides:
        count = lax.axis_size(axis)
        forward = [(i, i + 1) for i in range(count - 1)]
        if periodic:
            forward.append((count - 1, 0))
        backward = [(target, source) for source, target in forward]
        low = lax.ppermute(
            lax.slice_in_dim(block, block.shape[dim] - width, None, axis=dim), axis, forward
        )
        high = lax.ppermute(lax.slice_in_dim(block, 0, width, axis=dim), axis, backward)
        block = jnp.concatenate([low, block, high], axis=dim)
    return block


def dft_tables(width):
    points = jnp.arange(width, dtype=jnp.int32)
    waves = jnp.arange(width // 2 + 1, dtype=jnp.int32)
    phase = points[:, None] * waves[None, :] % width
    angle = phase.astype(jnp.float32) * (2.0 * math.pi / width)
    weights = jnp.where((waves == 0) | (waves * 2 == width), 1.0, 2.0).astype(jnp.float32) / width
    return (jnp.cos(angle), jnp.sin(angle), weights)


def rims(stack):
    wide = padded_2(stack, (("lon", 1),), 1, True)
    return padded_2(wide, (("lat", 0),), 1, False)


def level_diff(field):
    padded = jnp.pad(field, ((0, 0), (0, 0), (1, 1)))
    return 0.5 * (padded[:, :, 2:] - padded[:, :, :-2])


def damped(block, cut_vec, tables):
    cos_table, sin_table, weights = tables
    highest = lax.Precision.HIGHEST
    wave_vals = jnp.arange(cos_table.shape[1]).astype(jnp.float32)
    ratio = cut_vec[:, None] / jnp.maximum(wave_vals, 1.0)[None, :]
    damping = (jnp.minimum(1.0, ratio * ratio) * weights[None, :])[:, None, :]
    real_part = jnp.einsum("rnq,nk->rqk", block, cos_table, precision=highest)
    imag_part = jnp.einsum("rnq,nk->rqk", block, sin_table, precision=highest)
    restored = jnp.einsum("rqk,nk->rnq", real_part * damping, cos_table, precision=highest)
    return restored + jnp.einsum("rqk,nk->rnq", imag_part * damping, sin_table, precision=highest)


def circle_local(fields, cut_rows, tables):
    return damped(fields, cut_rows, tables)


def polar(fields, row_flag, cut_rows, tables, apply):
    smooth = apply(fields, cut_rows, tables)
    return jnp.where(row_flag[:, None, None], smooth, fields)


def plain_body(state, filter_flag, cutoff):
    rows, width, depth = state.shape
    levels = depth // 4
    zonal_wind = state[:, :, :levels]
    merid_wind = state[:, :, levels : 2 * levels]
    vert_wind = state[:, :, 2 * levels : 3 * levels]
    pressure = state[:, :, 3 * levels :]
    nlat = rows * lax.axis_size("lat")
    nlon = width * lax.axis_size("lon")
    offset = lax.axis_index("lat") * rows
    row_ids = (offset + jnp.arange(-1, rows + 1)).astype(jnp.float32)
    cos_ext = jnp.cos(-0.5 * math.pi + (row_ids + 0.5) * math.pi / nlat)
    cos_mid = cos_ext[1:-1][:, None, None]
    tables = dft_tables(nlon)
    row_flag = filter_flag == 1
    cut_rows = cutoff.astype(jnp.float32)
    padded = rims(pressure)
    grad_x = (padded[1:-1, 2:] - padded[1:-1, :-2]) / (2.0 * cos_mid)
    grad_y = 0.5 * (padded[2:, 1:-1] - padded[:-2, 1:-1])
    grad_z = level_diff(pressure)
    zonal_pre = zonal_wind - WIND_COEF * grad_x
    merid_pre = merid_wind - WIND_COEF * grad_y
    vert_new = vert_wind - VERT_COEF * grad_z
    div_z = level_diff(vert_new)
    outgoing = jnp.stack([zonal_pre, merid_pre, pressure, div_z], 3).reshape(
        rows, width, 4 * levels
    )
    circles = lax.all_to_all(outgoing, "lon", split_axis=2, concat_axis=1, tiled=True)
    part_levels = circles.shape[2] // 4
    circles = circles.reshape(rows, nlon, part_levels, 4)
    winds_c = jnp.concatenate([circles[:, :, :, 0], circles[:, :, :, 1]], 2)
    press_c = circles[:, :, :, 2]
    div_z_c = circles[:, :, :, 3]
    winds_c = polar(winds_c, row_flag, cut_rows, tables, circle_local)
    zonal_c = winds_c[:, :, :part_levels]
    merid_c = winds_c[:, :, part_levels:]
    div_x = (jnp.roll(zonal_c, -1, 1) - jnp.roll(zonal_c, 1, 1)) / (2.0 * cos_mid)
    flux = padded_2(merid_c * cos_mid, (("lat", 0),), 1, False)
    div_y = (flux[2:] - flux[:-2]) / (2.0 * cos_mid)
    press_mid = press_c - PRESS_COEF * (div_x + div_y + div_z_c)
    press_c = polar(press_mid, row_flag, cut_rows, tables, circle_local)
    back = jnp.stack([zonal_c, merid_c, press_c], 3).reshape(rows, nlon, 3 * part_levels)
    patches = lax.all_to_all(back, "lon", split_axis=1, concat_axis=2, tiled=True).reshape(
        rows, width, levels, 3
    )
    return jnp.concatenate(
        [patches[:, :, :, 0], patches[:, :, :, 1], vert_new, patches[:, :, :, 2]], 2
    )


def body(state, filter_flag, cutoff):
    rows, width, depth = state.shape
    levels = depth // 4
    lanes_fit = rows == 8 and 2 * levels == LANES and width % 8 == 0
    if lax.axis_size("lon") == 4 and lanes_fit:
        return packed_body(state, filter_flag, cutoff)
    return plain_body(state, filter_flag, cutoff)


def solution(mesh):
    return jax.shard_map(
        body,
        mesh=mesh,
        in_specs=(P("lat", "lon", None), P("lat"), P("lat")),
        out_specs=P("lat", "lon", None),
        check_vma=False,
    )
```

```python
import functools
import math

import jax
import jax.numpy as jnp
import numpy as np
from jax import lax
from jax.experimental import pallas as pl
from jax.experimental.pallas import tpu as pltpu
from jax.sharding import PartitionSpec as P

WIND_COEF = 0.03
VERT_COEF = 0.2
PRESS_COEF = 0.03
LANES = 128
VMEM_BYTES = 40 * 1024 * 1024
F32 = jnp.float32
BF16 = jnp.bfloat16


def split_np(table):
    high = table.astype(np.float32).astype(jnp.bfloat16)
    low = (table - high.astype(np.float64)).astype(np.float32).astype(jnp.bfloat16)
    return high, low


def round_up(value, step):
    return -(-value // step) * step


@functools.lru_cache(maxsize=None)
def spectral_plan(nlon):
    quarter = nlon // 4
    points = np.arange(quarter)
    waves0 = np.arange(0, nlon // 2 + 1, 4)
    waves2 = np.arange(2, nlon // 2 + 1, 4)
    waves1 = np.arange(1, nlon // 2 + 1, 2)
    size0 = round_up(len(waves0), 16)
    size2 = round_up(len(waves2), 16)
    size1 = round_up(len(waves1), 8)

    def trig(waves, size):
        angle = 2.0 * np.pi * ((waves[:, None] * points[None, :]) % nlon) / nlon
        cos_t, sin_t = np.zeros((2, size, quarter))
        cos_t[: len(waves)] = np.cos(angle)
        sin_t[: len(waves)] = np.sin(angle)
        return cos_t, sin_t

    def padded(values, size):
        out = np.zeros(size)
        out[: len(values)] = values
        return out

    def weights(waves, size):
        ends = (waves == 0) | (2 * waves == nlon)
        return padded(np.where(ends, 1.0, 2.0) / nlon, size)

    cos0, sin0 = trig(waves0, size0)
    cos2, sin2 = trig(waves2, size2)
    cos1, sin1 = trig(waves1, size1)
    turn = padded(np.where(waves1 % 4 == 1, 1.0, -1.0), size1)[:, None]
    fwd0 = np.concatenate([cos0, sin0], 0)
    fwd2 = np.concatenate([cos2, sin2], 0)
    fwd1 = np.block([[cos1, -turn * sin1], [sin1, turn * cos1]])
    inv0 = (fwd0 * np.tile(weights(waves0, size0), 2)[:, None]).T
    inv2 = (fwd2 * np.tile(weights(waves2, size2), 2)[:, None]).T
    inv1 = (fwd1 * np.tile(weights(waves1, size1), 2)[:, None]).T
    forward = [part for table in (fwd0, fwd2, fwd1) for part in split_np(table)]
    inverse = [part for table in (inv0, inv2, inv1) for part in split_np(table)]

    def columns(waves, size):
        inv_wave = padded(1.0 / np.maximum(waves, 1), size)
        delta = padded(np.sin(2.0 * np.pi * waves / nlon), size)
        return np.concatenate([inv_wave, inv_wave]), np.concatenate([delta, -delta])

    per_wave = [columns(w, s) for w, s in ((waves0, size0), (waves2, size2), (waves1, size1))]
    mode = np.stack([np.concatenate([c[0] for c in per_wave]), np.concatenate([c[1] for c in per_wave])], 1)
    mode = np.pad(mode.astype(np.float32), ((0, 0), (0, LANES - 2)))
    return forward, inverse, mode, (size0, size2, size1)


def lane_ids(shape):
    return lax.broadcasted_iota(jnp.int32, shape, len(shape) - 1)


def select_groups(values, masks):
    out = None
    for mask, value in zip(masks, values):
        if value is not None:
            out = value if out is None else jnp.where(mask, value, out)
    return out


def group_masks(size, part):
    group = lane_ids((size, LANES)) // part
    return [group == g for g in range(LANES // part)]


def transpose_groups(tiles, masks, part, wanted):
    count = len(tiles)
    turned = []
    for shift in range(count):
        mixed = select_groups([tiles[(shift + g) % count] if g in wanted else None for g in range(count)], masks)
        turned.append(pltpu.roll(mixed, shift * part, 1) if shift else mixed)
    return [select_groups([turned[(h - g) % count] for h in range(count)], masks) for g in wanted]


def gather_groups(blocks, masks, part):
    count = len(masks)
    turned = []
    for shift in range(count):
        mixed = [None] * count
        for g, block in enumerate(blocks):
            mixed[(4 + g - shift) % count] = block
        mixed = select_groups(mixed, masks)
        turned.append(pltpu.roll(mixed, shift * part, 1) if shift else mixed)
    return [select_groups([None] * 4 + [turned[(4 + g - row) % count] for g in range(4)], masks) for row in range(count)]


def partner_order(blocks, me):
    odd, far = lax.rem(me, 2) == 1, me >= 2
    a, b, c, d = blocks
    a, b, c, d = jnp.where(odd, b, a), jnp.where(odd, a, b), jnp.where(odd, d, c), jnp.where(odd, c, d)
    return [jnp.where(far, c, a), jnp.where(far, d, b), jnp.where(far, a, c), jnp.where(far, b, d)]


def chunk_of(size):
    return next(c for c in (24, 40, 16, 8) if size % c == 0)


def cut_value(flag_ref, cut_ref, row, nlon):
    return jnp.where(flag_ref[row] == 1, cut_ref[row], nlon).astype(F32)


def row_cosine(row, count):
    return jnp.sin((row.astype(F32) + 0.5) * (math.pi / count))


def levels_table(levels):
    shape = (2 * levels, 2 * levels)
    source = lax.broadcasted_iota(jnp.int32, shape, 0)
    target = lax.broadcasted_iota(jnp.int32, shape, 1)
    step = source % levels - target % levels
    diff = jnp.where(step == 1, 1.0, jnp.where(step == -1, -1.0, 0.0))
    rim = (target % levels == 0) | (target % levels == levels - 1)
    twice = jnp.where(step == 0, jnp.where(rim, -1.0, -2.0), jnp.where(abs(step) == 2, 1.0, 0.0))
    from_press, to_press = source >= levels, target >= levels
    table = jnp.where(from_press, jnp.where(to_press, twice, diff), jnp.where(to_press, -10.0 * diff, 0.0))
    return table.astype(BF16)


def each_chunk(size, step, work):
    def turn(index, carry):
        work(pl.multiple_of(index * step, 8))
        return carry

    lax.fori_loop(0, size // step, turn, 0, unroll=True)


def natural(refs):
    own, chip, far, core = refs
    return [own, core, chip, far]


def put(refs, start, values):
    for ref, value in zip(refs, values):
        ref[pl.ds(start, value.shape[0])] = value


def merid_row(wind_ref, tile_ref, row, lines):
    half = 0.5 * WIND_COEF
    value = wind_ref[row, lines]
    if row < tile_ref.shape[0] - 1:
        value = value - half * tile_ref[row + 1, lines]
    return value + half * tile_ref[row - 1, lines] if row else value


def zonal_kernel(part, wind_ref, tile_ref, *refs):
    packs, zonal_ref = refs[:4], refs[4]
    rows, width, _ = tile_ref.shape
    levels = LANES // 2
    nlat = rows * lax.axis_size("lat")
    me = lax.axis_index("lon")
    first = lax.axis_index("lat") * rows
    place = lax.broadcasted_iota(jnp.int32, (width, LANES), 0)
    for row in range(rows):
        tile = tile_ref[row]
        after = jnp.where(place == width - 1, 0.0, pltpu.roll(tile, width - 1, 0))
        before = jnp.where(place == 0, 0.0, pltpu.roll(tile, 1, 0))
        scale = WIND_COEF / (2.0 * row_cosine(jnp.full((1, LANES), first + row), nlat))
        zonal_ref[row] = wind_ref[row] - pltpu.roll((after - before) * scale, levels, 1)

    size = chunk_of(width)
    masks = group_masks(size, part)

    def pack(start):
        lines = pl.ds(start, size)
        blocks = transpose_groups([zonal_ref[row, lines] for row in range(rows)], masks, part, range(4))
        put(packs, start, partner_order(blocks, me))

    each_chunk(width, size, pack)


def edge_kernel(part, *refs):
    (wind_first, wind_last), (tile_first, tile_last), (begin_ref, end_ref), packs = refs[:2], refs[2:4], refs[4:6], refs[6:]
    _, width, _ = tile_first.shape
    me = lax.axis_index("lon")
    half = 0.5 * WIND_COEF
    head = rim_lines(width)
    masks = group_masks(8, part)

    def pack(start):
        tiles = []
        for begin in (start, jnp.minimum(start + head, width - 8)):
            lines = pl.ds(pl.multiple_of(begin, 8), 8)
            tiles += [wind_first[0, lines] - half * tile_first[1, lines], tile_first[0, lines]]
            tiles += [wind_last[1, lines] + half * tile_last[0, lines], tile_last[1, lines]]
        return tiles

    def send_out(start, tiles):
        put(packs, start, partner_order(transpose_groups(tiles, masks, part, range(4, 8)), me))

    each_chunk(head - 8, 8, lambda start: send_out(start, pack(start)))
    line = lax.broadcasted_iota(jnp.int32, (8, LANES), 0)
    ends = []
    for row in range(4):
        inner = jnp.where(line == 1, pltpu.roll(begin_ref[row + 4], 1, 0), pltpu.roll(end_ref[row + 4], 7, 0))
        ends.append(jnp.where(line == 0, begin_ref[row], jnp.where(line == 7, end_ref[row], inner)))
    send_out(head - 8, pack(head - 8)[:4] + ends)


def rim_lines(width):
    return round_up(-(-width // 2), 8)


def fold_lines(width):
    return round_up(-(-width * 3 // 4), 8)


def press_kernel(part, wind_ref, tile_ref, _, *refs):
    packs, vert_ref = refs[:4], refs[4]
    rows, width, _ = tile_ref.shape
    levels = LANES // 2
    me = lax.axis_index("lon")
    masks8 = group_masks(8, part)
    head = fold_lines(width)
    tail = width - head

    def pack_merid(start, pair, fold=None):
        lines = pl.ds(start, 8)
        folded = pl.ds(start - pair * tail + head if fold is None else fold, 8)
        tiles = [merid_row(wind_ref, tile_ref, row, lines) for row in range(1, rows - 1)]
        one = merid_row(wind_ref, tile_ref, 2 * pair + 1, folded)
        two = merid_row(wind_ref, tile_ref, 2 * pair + 2, folded)
        blocks = transpose_groups([one] + tiles + [two], masks8, part, range(4, 8))
        put(packs, start, partner_order(blocks, me))

    for pair in range(3):
        each_chunk(tail, 8, lambda start: pack_merid(pl.multiple_of(start + pair * tail, 8), pair))
    for start in range(3 * tail, head, 8):
        pack_merid(start, 2, start)

    gain = jnp.where(lane_ids((1, LANES)) < levels, -0.5 * VERT_COEF, 0.25 * PRESS_COEF * VERT_COEF)
    table = levels_table(levels)
    dot = functools.partial(jnp.dot, preferred_element_type=F32)
    for row in range(rows):
        tile = tile_ref[row]
        high = tile.astype(BF16)
        rest = (tile - high.astype(F32)).astype(BF16)
        vert_ref[row] = tile + gain * (dot(high, table) + dot(rest, table))

    size = chunk_of(width)
    masks = group_masks(size, part)

    def pack(start):
        lines = pl.ds(start, size)
        blocks = transpose_groups([vert_ref[row, lines] for row in range(rows)], masks, part, range(4, 8))
        put(packs, pl.multiple_of(start + head, 8), partner_order(blocks, me))

    each_chunk(width, size, pack)


def turn_groups(value, groups, part):
    shift = groups * part % LANES
    return pltpu.roll(value, shift, 1) if shift else value


def rim_kernel(part, skip, flag_ref, cut_ref, *refs):
    blocks, north_ref, south_ref = natural(refs[:4]), refs[-2], refs[-1]
    lines = blocks[0].shape[0]
    first = lane_ids((lines, LANES)) // part % 4 < 2
    for half in range(2):
        one, two = blocks[2 * half][...], blocks[2 * half + 1][...]
        where = slice(half * lines, half * lines + lines)
        south_ref[where] = jnp.where(first, one, turn_groups(two, 2, part))
        north_ref[where] = jnp.where(first, turn_groups(two, -2, part), one)
    last = flag_ref.shape[0] - 1
    nlon = (skip - 8) * 4
    north_ref[2 * lines :] = jnp.full((8, LANES), cut_value(flag_ref, cut_ref, last, nlon), F32)
    south_ref[2 * lines :] = jnp.full((8, LANES), cut_value(flag_ref, cut_ref, 0, nlon), F32)


def edge_spec_kernel(bounds, part, skip, flag_ref, cut_ref, mode_ref, south_ref, north_ref, _, *refs):
    blocks, forward, spec_ref = natural(refs[:4]), refs[4:10], refs[10]
    lines = blocks[0].shape[0]
    width = skip - 8
    half = 0.5 * WIND_COEF
    item = lane_ids((lines, LANES)) // part % 4
    fields = []
    for quarter, block in enumerate(blocks):
        where = slice(quarter // 2 * lines, quarter // 2 * lines + lines)
        own, south, north = block[...], south_ref[where], north_ref[where]
        at = 0 if quarter % 2 else 2
        merid_s, press_s = turn_groups(south, 1 - at, part), turn_groups(south, -1 - at, part)
        merid_n, press_n = turn_groups(north, 1 + at, part), turn_groups(north, at - 1, part)
        inner = own + half * jnp.where(item == 0, press_s, -press_n)
        outer = jnp.where(item == 1, merid_s - half * own, merid_n + half * own)
        value = jnp.where(item % 2 == 0, inner, outer)
        fields.append(jnp.concatenate([value, turn_groups(value, -4, part)], 0)[:width])
    rows = flag_ref.shape[0]
    group = lane_ids((1, LANES)) // part
    cut = jnp.where(group == 0, cut_value(flag_ref, cut_ref, 0, 4 * width), cut_value(flag_ref, cut_ref, rows - 1, 4 * width))
    cut = jnp.where(group == 1, south_ref[2 * lines : 2 * lines + 1], cut)
    cut = jnp.where(group == 3, north_ref[2 * lines : 2 * lines + 1], cut)
    damp = damping(cut, mode_ref[:, 0:1])
    for (low, high), value in zip(bounds, forward_dft(fields, forward)):
        spec_ref[low:high] = value * damp[low:high]


def merid_spec_kernel(bounds, part, flag_ref, cut_ref, mode_ref, edge_ref, *refs):
    blocks, forward, inverse, outs, spec_ref = natural(refs[:4]), refs[4:10], refs[10:16], refs[16:20], refs[20]
    rows = flag_ref.shape[0]
    width = outs[0].shape[0]
    head = fold_lines(width)
    tail = width - head
    group = lane_ids((tail, LANES)) // part
    fields = []
    for block in blocks:
        out = None
        for pair in range(3):
            value = block[pair * tail : pair * tail + tail]
            one, two = turn_groups(value, 2 * pair + 1, part), turn_groups(value, 2 * pair + 3, part)
            both = jnp.where(group == 2 * pair + 1, one, two)
            out = both if pair == 0 else jnp.where(group > 2 * pair, both, out)
        fields.append(jnp.concatenate([block[:head], out], 0))
    damp = damping(lane_cut(flag_ref, cut_ref, 4 * width, part), mode_ref[:, 0:1])
    group = lane_ids((1, LANES)) // part
    parts = []
    for (low, high), value in zip(bounds, forward_dft(fields, forward)):
        edge = edge_ref[low:high]
        value = jnp.where(group == 0, edge, value * damp[low:high])
        parts.append(jnp.where(group == rows - 1, turn_groups(edge, rows - 3, part), value))
        spec_ref[low:high] = parts[-1]
    inverse_dft(parts, inverse, outs)


def dot3(table_high, table_low, value):
    high = value.astype(BF16)
    low = (value - high.astype(F32)).astype(BF16)
    width = value.shape[1]
    dot = functools.partial(jnp.dot, preferred_element_type=F32)
    both = dot(table_high[...], jnp.concatenate([high, low], 1))
    return both[:, :width] + both[:, width:] + dot(table_low[...], high)


def by_place(me, dif0, dif1):
    odd = lax.rem(me, 2) == 1
    sign = jnp.where(me >= 2, -1.0, 1.0).astype(F32)
    return jnp.where(odd, dif1, dif0) * sign, jnp.where(odd, dif0, dif1) * sign


def parity_sign(me):
    return jnp.where(lax.rem(me, 2) == 1, -1.0, 1.0).astype(F32)


def forward_dft(quarters, tables):
    me = lax.axis_index("lon")
    own, core, chip, far = quarters
    sum0, sum1 = own + chip, core + far
    dif0, dif1 = by_place(me, own - chip, core - far)
    return (
        dot3(tables[0], tables[1], sum0 + sum1),
        dot3(tables[2], tables[3], (sum0 - sum1) * parity_sign(me)),
        dot3(tables[4], tables[5], jnp.concatenate([dif0, dif1], 0)),
    )


def inverse_dft(parts, tables, outs):
    me = lax.axis_index("lon")
    even = dot3(tables[0], tables[1], parts[0])
    other = dot3(tables[2], tables[3], parts[1]) * parity_sign(me)
    both = dot3(tables[4], tables[5], parts[2])
    quarter = even.shape[0]
    dif0, dif1 = by_place(me, both[:quarter], both[quarter:])
    plus, minus = even + other, even - other
    outs[0][...] = plus + dif0
    outs[1][...] = minus + dif1
    outs[2][...] = plus - dif0
    outs[3][...] = minus - dif1


def lane_rows(pick, rows, part):
    group = lane_ids((1, LANES)) // part
    out = jnp.zeros((1, LANES), F32)
    for row in range(rows):
        out = jnp.where(group == row, pick(row), out)
    return out


def lane_cut(flag_ref, cut_ref, nlon, part):
    rows = flag_ref.shape[0]
    return lane_rows(lambda row: cut_value(flag_ref, cut_ref, row, nlon), rows, part)


def lane_cosine(shift, rows, part):
    row = lane_ids((1, LANES)) // part + lax.axis_index("lat") * rows + shift
    return row_cosine(row, rows * lax.axis_size("lat"))


def damping(cut, inv_wave):
    ratio = cut * inv_wave
    return jnp.minimum(1.0, ratio * ratio)


def zonal_spec_kernel(bounds, part, flag_ref, cut_ref, mode_ref, _, e0, e2, e3, e1, q0, q2, q3, q1, *refs):
    forward, inverse, outs, spec_ref = refs[:6], refs[6:12], refs[12:16], refs[16]
    rows = flag_ref.shape[0]
    width = outs[0].shape[0]
    me = lax.axis_index("lon")
    quarters = (q0, q1, q2, q3)
    scale = WIND_COEF / (2.0 * lane_cosine(0, rows, part))
    line = lax.broadcasted_iota(jnp.int32, (8, LANES), 0)
    low = lane_ids((8, LANES)) < LANES // 2
    sides = []
    for edge in (e0, e1, e2, e3):
        value = edge[edge.shape[0] - 8 :]
        inner = jnp.where(line == 0, pltpu.roll(value, 7, 0), pltpu.roll(value, 1, 0))
        sides.append(jnp.where(low, turn_groups(value, -4, part), inner))
    sides = partner_order(sides, me)
    starts = [jnp.where(line == 0, scale * pltpu.roll(sides[(q + 3) % 4], 1, 0), 0.0) for q in range(4)]
    ends = [jnp.where(line == 7, scale * pltpu.roll(sides[(q + 1) % 4], 7, 0), 0.0) for q in range(4)]
    starts, ends = partner_order(starts, me), partner_order(ends, me)
    fields = [
        jnp.concatenate([q[0:8] + start, q[8 : width - 8], q[width - 8 : width] - end], 0)
        for q, start, end in zip(quarters, starts, ends)
    ]
    damp = damping(lane_cut(flag_ref, cut_ref, 4 * width, part), mode_ref[:, 0:1])
    parts = [value * damp[b[0] : b[1]] for b, value in zip(bounds, forward_dft(fields, forward))]
    for (low, high), value in zip(bounds, parts):
        spec_ref[low:high] = value
    inverse_dft(parts, inverse, outs)


def press_back_kernel(bounds, part, flag_ref, cut_ref, mode_ref, zonal_ref, merid_ref, edge_ref, *refs):
    quarters, forward, inverse, outs = natural(refs[:4]), refs[4:10], refs[10:16], refs[16:]
    skip = quarters[0].shape[0] - outs[0].shape[0]
    rows = flag_ref.shape[0]
    nlon = 4 * inverse[0].shape[0]
    band = lax.axis_index("lat")
    mode = mode_ref[...]
    damp = damping(lane_cut(flag_ref, cut_ref, nlon, part), mode[:, 0:1])
    cosine = lane_cosine(0, rows, part)
    below = jnp.where(band == 0, 0.0, lane_cosine(-1, rows, part))
    above = jnp.where(band == lax.axis_size("lat") - 1, 0.0, lane_cosine(1, rows, part))
    half_inv = 0.5 / cosine
    group = lane_ids((1, LANES)) // part
    flux = merid_ref[...] * cosine
    edge = edge_ref[...]
    north = jnp.where(group == rows - 1, turn_groups(edge, rows - 4, part) * above, turn_groups(flux, -1, part))
    south = jnp.where(group == 0, turn_groups(edge, -1, part) * below, turn_groups(flux, 1, part))
    div_y = (north - south) * half_inv
    zonal = zonal_ref[...]
    slope = mode[:, 1:2] / cosine
    parts = []
    for (low, high), press in zip(bounds, forward_dft([q[skip:] for q in quarters], forward)):
        mid = (low + high) // 2
        swapped = jnp.concatenate([zonal[mid:high], zonal[low:mid]], 0)
        div = swapped * slope[low:high] + div_y[low:high]
        parts.append((press - PRESS_COEF * div) * damp[low:high])
    inverse_dft(parts, inverse, outs)


def winds_out_kernel(part, *refs):
    blocks, out_ref = natural(refs[:4]) + natural(refs[4:8]), refs[8]
    rows, width, _ = out_ref.shape
    me = lax.axis_index("lon")
    size = chunk_of(width)
    masks = group_masks(size, part)

    def unpack(start):
        lines = pl.ds(start, size)
        values = [ref[lines] for ref in blocks]
        values = partner_order(values[:4], me) + partner_order(values[4:], me)
        for row, value in enumerate(transpose_groups(values, masks, part, range(rows))):
            out_ref[row, lines] = value

    each_chunk(width, size, unpack)


def press_out_kernel(part, _, tile_ref, *refs):
    blocks, out_hbm, tile_out, sems = natural(refs[:4]), refs[4], refs[5], refs[6]
    rows, width, _ = tile_ref.shape
    me = lax.axis_index("lon")
    size = chunk_of(width)
    masks = group_masks(size, part)
    low = lane_ids((size, LANES)) < LANES // 2
    count = sems.shape[0]
    copies = []
    for piece in range(count):
        begin, end = piece * width // count, (piece + 1) * width // count

        def unpack(start):
            lines = pl.ds(start + begin, size)
            values = partner_order([ref[lines] for ref in blocks], me)
            for row, value in enumerate(gather_groups(values, masks, part)):
                tile_out[row, lines] = jnp.where(low, tile_ref[row, lines], value)

        each_chunk(end - begin, size, unpack)
        copy = pltpu.make_async_copy(tile_out.at[:, begin:end], out_hbm.at[:, begin:end, LANES:], sems.at[piece])
        copy.start()
        copies.append(copy)
    for copy in copies:
        copy.wait()


def whole(shape):
    return pl.BlockSpec(shape, lambda step: (0,) * len(shape))


def tile_of(shape, index):
    return pl.BlockSpec((shape[0], shape[1], LANES), lambda step: (0, 0, index))


SMEM = pl.BlockSpec(memory_space=pltpu.SMEM)
ANY = pl.BlockSpec(memory_space=pl.ANY)


def call(kernel, out_shape, in_specs, out_specs, cost=2, grid=(1,), **more):
    return pl.pallas_call(
        kernel,
        grid=grid,
        out_shape=out_shape,
        in_specs=in_specs,
        out_specs=out_specs,
        compiler_params=pltpu.CompilerParams(vmem_limit_bytes=VMEM_BYTES),
        cost_estimate=pl.CostEstimate(flops=int(cost * 1.15e9), bytes_accessed=int(cost * 3.69e6), transcendentals=0),
        **more,
    )


def f32(*shape):
    return jax.ShapeDtypeStruct(shape, F32)


def send(block, step):
    return lax.ppermute(block, "lon", [(i, i ^ step) for i in range(4)])


def exchange(blocks):
    return [blocks[0]] + [send(blocks[step], step) for step in (2, 3, 1)]


def packed_body(state, filter_flag, cutoff):
    rows, width, depth = state.shape
    levels = depth // 4
    bands = lax.axis_size("lat")
    nlon = 4 * width
    part = levels // 4
    forward, inverse, mode, sizes = spectral_plan(nlon)
    forward = [jnp.asarray(t) for t in forward]
    inverse = [jnp.asarray(t) for t in inverse]
    mode = jnp.asarray(mode)
    bounds, at = [], 0
    for size in sizes:
        bounds.append((at, at + 2 * size))
        at += 2 * size
    table_specs = [whole(t.shape) for t in forward] + [whole(t.shape) for t in inverse]
    block, spectrum, full = (width, LANES), (at, LANES), (rows, width, LANES)
    skip = width + 8
    second = (fold_lines(width) + width, LANES)
    rims = (2 * rim_lines(width) + 8, LANES)
    low_tile, high_tile = tile_of(state.shape, 0), tile_of(state.shape, 1)

    edges = (rim_lines(width), LANES)

    def two_rows(row, index):
        return pl.BlockSpec((2, width, LANES), lambda step: (row, 0, index))

    def end_lines(index):
        return pl.BlockSpec((rows, 8, LANES), lambda step: (0, index, 1))

    edge_packs = call(
        functools.partial(edge_kernel, part),
        [f32(*edges)] * 4,
        [two_rows(0, 0), two_rows(rows // 2 - 1, 0), two_rows(0, 1), two_rows(rows // 2 - 1, 1)] + [end_lines(0), end_lines(width // 8 - 1)],
        [whole(edges)] * 4,
    )(*[state] * 6)
    zonal_packs = call(
        functools.partial(zonal_kernel, part),
        [f32(*block)] * 4,
        [low_tile, high_tile],
        [whole(block)] * 4,
        scratch_shapes=[pltpu.VMEM(full, F32)],
    )(state, state)
    edge_circle = exchange(edge_packs)
    first_circle = exchange(zonal_packs)
    *packs, vert = call(
        functools.partial(press_kernel, part),
        [f32(*second)] * 4 + [f32(*full)],
        [low_tile, high_tile, ANY],
        [whole(second)] * 4 + [whole(full)],
    )(state, state, edge_circle[1])
    second_circle = exchange(packs)

    edge_specs = [whole(edges)] * 4
    to_north, to_south = call(
        functools.partial(rim_kernel, part, skip),
        [f32(*rims)] * 2,
        [SMEM] * 2 + edge_specs + [ANY],
        [whole(rims)] * 2,
        cost=8,
    )(filter_flag, cutoff, *edge_circle, vert)
    from_south = lax.ppermute(to_north, "lat", [(i, i + 1) for i in range(bands - 1)])
    from_north = lax.ppermute(to_south, "lat", [(i + 1, i) for i in range(bands - 1)])

    *zonal_parts, zonal_spec = call(
        functools.partial(zonal_spec_kernel, bounds, part),
        [f32(*block)] * 4 + [f32(*spectrum)],
        [SMEM] * 2 + [whole(mode.shape), ANY] + [whole(edges)] * 4 + [whole(block)] * 4 + table_specs,
        [whole(block)] * 4 + [whole(spectrum)],
    )(filter_flag, cutoff, mode, second_circle[3], *edge_circle, *first_circle, *forward, *inverse)
    zonal_back = exchange(zonal_parts)
    edge_spec = call(
        functools.partial(edge_spec_kernel, bounds, part, skip),
        f32(*spectrum),
        [SMEM] * 2 + [whole(mode.shape)] + [whole(rims)] * 2 + [ANY] + edge_specs + table_specs[:6],
        whole(spectrum),
    )(filter_flag, cutoff, mode, from_south, from_north, zonal_spec, *edge_circle, *forward)

    *merid_parts, merid_spec = call(
        functools.partial(merid_spec_kernel, bounds, part),
        [f32(*block)] * 4 + [f32(*spectrum)],
        [SMEM] * 2 + [whole(mode.shape), whole(spectrum)] + [whole(second)] * 4 + table_specs,
        [whole(block)] * 4 + [whole(spectrum)],
    )(filter_flag, cutoff, mode, edge_spec, *second_circle, *forward, *inverse)
    merid_back = exchange(merid_parts)

    press_parts = call(
        functools.partial(press_back_kernel, bounds, part),
        [f32(*block)] * 4,
        [SMEM] * 2 + [whole(mode.shape)] + [whole(spectrum)] * 3 + [whole(second)] * 4 + table_specs,
        [whole(block)] * 4,
    )(filter_flag, cutoff, mode, zonal_spec, merid_spec, edge_spec, *second_circle, *forward, *inverse)
    press_back = exchange(press_parts)

    out = call(
        functools.partial(winds_out_kernel, part),
        f32(*state.shape),
        [whole(block)] * 8,
        low_tile,
    )(*zonal_back, *merid_back)
    pieces = next(n for n in (3, 5, 1) if width % (n * chunk_of(width)) == 0)
    return call(
        functools.partial(press_out_kernel, part),
        f32(*state.shape),
        [ANY, whole(full)] + [whole(block)] * 4,
        ANY,
        scratch_shapes=[pltpu.VMEM(full, F32), pltpu.SemaphoreType.DMA((pieces,))],
        input_output_aliases={0: 0},
    )(out, vert, *press_back)


def padded_2(block, sides, width, periodic):
    for axis, dim in sides:
        count = lax.axis_size(axis)
        forward = [(i, i + 1) for i in range(count - 1)]
        if periodic:
            forward.append((count - 1, 0))
        backward = [(target, source) for source, target in forward]
        low = lax.ppermute(
            lax.slice_in_dim(block, block.shape[dim] - width, None, axis=dim), axis, forward
        )
        high = lax.ppermute(lax.slice_in_dim(block, 0, width, axis=dim), axis, backward)
        block = jnp.concatenate([low, block, high], axis=dim)
    return block


def dft_tables(width):
    points = jnp.arange(width, dtype=jnp.int32)
    waves = jnp.arange(width // 2 + 1, dtype=jnp.int32)
    phase = points[:, None] * waves[None, :] % width
    angle = phase.astype(jnp.float32) * (2.0 * math.pi / width)
    weights = jnp.where((waves == 0) | (waves * 2 == width), 1.0, 2.0).astype(jnp.float32) / width
    return (jnp.cos(angle), jnp.sin(angle), weights)


def rims(stack):
    wide = padded_2(stack, (("lon", 1),), 1, True)
    return padded_2(wide, (("lat", 0),), 1, False)


def level_diff(field):
    padded = jnp.pad(field, ((0, 0), (0, 0), (1, 1)))
    return 0.5 * (padded[:, :, 2:] - padded[:, :, :-2])


def damped(block, cut_vec, tables):
    cos_table, sin_table, weights = tables
    highest = lax.Precision.HIGHEST
    wave_vals = jnp.arange(cos_table.shape[1]).astype(jnp.float32)
    ratio = cut_vec[:, None] / jnp.maximum(wave_vals, 1.0)[None, :]
    damping = (jnp.minimum(1.0, ratio * ratio) * weights[None, :])[:, None, :]
    real_part = jnp.einsum("rnq,nk->rqk", block, cos_table, precision=highest)
    imag_part = jnp.einsum("rnq,nk->rqk", block, sin_table, precision=highest)
    restored = jnp.einsum("rqk,nk->rnq", real_part * damping, cos_table, precision=highest)
    return restored + jnp.einsum("rqk,nk->rnq", imag_part * damping, sin_table, precision=highest)


def circle_local(fields, cut_rows, tables):
    return damped(fields, cut_rows, tables)


def polar(fields, row_flag, cut_rows, tables, apply):
    smooth = apply(fields, cut_rows, tables)
    return jnp.where(row_flag[:, None, None], smooth, fields)


def plain_body(state, filter_flag, cutoff):
    rows, width, depth = state.shape
    levels = depth // 4
    zonal_wind = state[:, :, :levels]
    merid_wind = state[:, :, levels : 2 * levels]
    vert_wind = state[:, :, 2 * levels : 3 * levels]
    pressure = state[:, :, 3 * levels :]
    nlat = rows * lax.axis_size("lat")
    nlon = width * lax.axis_size("lon")
    offset = lax.axis_index("lat") * rows
    row_ids = (offset + jnp.arange(-1, rows + 1)).astype(jnp.float32)
    cos_ext = jnp.cos(-0.5 * math.pi + (row_ids + 0.5) * math.pi / nlat)
    cos_mid = cos_ext[1:-1][:, None, None]
    tables = dft_tables(nlon)
    row_flag = filter_flag == 1
    cut_rows = cutoff.astype(jnp.float32)
    padded = rims(pressure)
    grad_x = (padded[1:-1, 2:] - padded[1:-1, :-2]) / (2.0 * cos_mid)
    grad_y = 0.5 * (padded[2:, 1:-1] - padded[:-2, 1:-1])
    grad_z = level_diff(pressure)
    zonal_pre = zonal_wind - WIND_COEF * grad_x
    merid_pre = merid_wind - WIND_COEF * grad_y
    vert_new = vert_wind - VERT_COEF * grad_z
    div_z = level_diff(vert_new)
    outgoing = jnp.stack([zonal_pre, merid_pre, pressure, div_z], 3).reshape(
        rows, width, 4 * levels
    )
    circles = lax.all_to_all(outgoing, "lon", split_axis=2, concat_axis=1, tiled=True)
    part_levels = circles.shape[2] // 4
    circles = circles.reshape(rows, nlon, part_levels, 4)
    winds_c = jnp.concatenate([circles[:, :, :, 0], circles[:, :, :, 1]], 2)
    press_c = circles[:, :, :, 2]
    div_z_c = circles[:, :, :, 3]
    winds_c = polar(winds_c, row_flag, cut_rows, tables, circle_local)
    zonal_c = winds_c[:, :, :part_levels]
    merid_c = winds_c[:, :, part_levels:]
    div_x = (jnp.roll(zonal_c, -1, 1) - jnp.roll(zonal_c, 1, 1)) / (2.0 * cos_mid)
    flux = padded_2(merid_c * cos_mid, (("lat", 0),), 1, False)
    div_y = (flux[2:] - flux[:-2]) / (2.0 * cos_mid)
    press_mid = press_c - PRESS_COEF * (div_x + div_y + div_z_c)
    press_c = polar(press_mid, row_flag, cut_rows, tables, circle_local)
    back = jnp.stack([zonal_c, merid_c, press_c], 3).reshape(rows, nlon, 3 * part_levels)
    patches = lax.all_to_all(back, "lon", split_axis=1, concat_axis=2, tiled=True).reshape(
        rows, width, levels, 3
    )
    return jnp.concatenate(
        [patches[:, :, :, 0], patches[:, :, :, 1], vert_new, patches[:, :, :, 2]], 2
    )


def body(state, filter_flag, cutoff):
    rows, width, depth = state.shape
    levels = depth // 4
    lanes_fit = rows == 8 and 2 * levels == LANES and width % 16 == 8
    if lax.axis_size("lon") == 4 and lanes_fit:
        return packed_body(state, filter_flag, cutoff)
    return plain_body(state, filter_flag, cutoff)


def solution(mesh):
    return jax.shard_map(
        body,
        mesh=mesh,
        in_specs=(P("lat", "lon", None), P("lat"), P("lat")),
        out_specs=P("lat", "lon", None),
        check_vma=False,
    )
```

```python
import functools
import math

import jax
import jax.numpy as jnp
import numpy as np
from jax import lax
from jax.experimental import pallas as pl
from jax.experimental.pallas import tpu as pltpu
from jax.sharding import PartitionSpec as P

WIND_COEF = 0.03
VERT_COEF = 0.2
PRESS_COEF = 0.03
LANES = 128
VMEM_BYTES = 40 * 1024 * 1024
F32 = jnp.float32
BF16 = jnp.bfloat16


def split_np(table):
    high = table.astype(np.float32).astype(jnp.bfloat16)
    low = (table - high.astype(np.float64)).astype(np.float32).astype(jnp.bfloat16)
    return high, low


def round_up(value, step):
    return -(-value // step) * step


@functools.lru_cache(maxsize=None)
def spectral_plan(nlon):
    quarter = nlon // 4
    points = np.arange(quarter)
    waves0 = np.arange(0, nlon // 2 + 1, 4)
    waves2 = np.arange(2, nlon // 2 + 1, 4)
    waves1 = np.arange(1, nlon // 2 + 1, 2)
    size0 = round_up(len(waves0), 16)
    size2 = round_up(len(waves2), 16)
    size1 = round_up(len(waves1), 8)

    def trig(waves, size):
        angle = 2.0 * np.pi * ((waves[:, None] * points[None, :]) % nlon) / nlon
        cos_t, sin_t = np.zeros((2, size, quarter))
        cos_t[: len(waves)] = np.cos(angle)
        sin_t[: len(waves)] = np.sin(angle)
        return cos_t, sin_t

    def padded(values, size):
        out = np.zeros(size)
        out[: len(values)] = values
        return out

    def weights(waves, size):
        ends = (waves == 0) | (2 * waves == nlon)
        return padded(np.where(ends, 1.0, 2.0) / nlon, size)

    cos0, sin0 = trig(waves0, size0)
    cos2, sin2 = trig(waves2, size2)
    cos1, sin1 = trig(waves1, size1)
    turn = padded(np.where(waves1 % 4 == 1, 1.0, -1.0), size1)[:, None]
    fwd0 = np.concatenate([cos0, sin0], 0)
    fwd2 = np.concatenate([cos2, sin2], 0)
    fwd1 = np.block([[cos1, -turn * sin1], [sin1, turn * cos1]])
    inv0 = (fwd0 * np.tile(weights(waves0, size0), 2)[:, None]).T
    inv2 = (fwd2 * np.tile(weights(waves2, size2), 2)[:, None]).T
    inv1 = (fwd1 * np.tile(weights(waves1, size1), 2)[:, None]).T
    forward = [part for table in (fwd0, fwd2, fwd1) for part in split_np(table)]
    inverse = [part for table in (inv0, inv2, inv1) for part in split_np(table)]

    def columns(waves, size):
        inv_wave = padded(1.0 / np.maximum(waves, 1), size)
        delta = padded(np.sin(2.0 * np.pi * waves / nlon), size)
        return np.concatenate([inv_wave, inv_wave]), np.concatenate([delta, -delta])

    per_wave = [columns(w, s) for w, s in ((waves0, size0), (waves2, size2), (waves1, size1))]
    mode = np.stack([np.concatenate([c[0] for c in per_wave]), np.concatenate([c[1] for c in per_wave])], 1)
    mode = np.pad(mode.astype(np.float32), ((0, 0), (0, LANES - 2)))
    return forward, inverse, mode, (size0, size2, size1)


def lane_ids(shape):
    return lax.broadcasted_iota(jnp.int32, shape, len(shape) - 1)


def select_groups(values, masks):
    out = None
    for mask, value in zip(masks, values):
        if value is not None:
            out = value if out is None else jnp.where(mask, value, out)
    return out


def group_masks(size, part):
    group = lane_ids((size, LANES)) // part
    return [group == g for g in range(LANES // part)]


def transpose_groups(tiles, masks, part, wanted):
    count = len(tiles)
    turned = []
    for shift in range(count):
        mixed = select_groups([tiles[(shift + g) % count] if g in wanted else None for g in range(count)], masks)
        turned.append(pltpu.roll(mixed, shift * part, 1) if shift else mixed)
    return [select_groups([turned[(h - g) % count] for h in range(count)], masks) for g in wanted]


def gather_groups(blocks, masks, part):
    count = len(masks)
    turned = []
    for shift in range(count):
        mixed = [None] * count
        for g, block in enumerate(blocks):
            mixed[(4 + g - shift) % count] = block
        mixed = select_groups(mixed, masks)
        turned.append(pltpu.roll(mixed, shift * part, 1) if shift else mixed)
    return [select_groups([None] * 4 + [turned[(4 + g - row) % count] for g in range(4)], masks) for row in range(count)]


def partner_order(blocks, me):
    odd, far = lax.rem(me, 2) == 1, me >= 2
    a, b, c, d = blocks
    a, b, c, d = jnp.where(odd, b, a), jnp.where(odd, a, b), jnp.where(odd, d, c), jnp.where(odd, c, d)
    return [jnp.where(far, c, a), jnp.where(far, d, b), jnp.where(far, a, c), jnp.where(far, b, d)]


def chunk_of(size):
    return next(c for c in (24, 40, 16, 8) if size % c == 0)


def cut_value(flag_ref, cut_ref, row, nlon):
    return jnp.where(flag_ref[row] == 1, cut_ref[row], nlon).astype(F32)


def row_cosine(row, count):
    return jnp.sin((row.astype(F32) + 0.5) * (math.pi / count))


def levels_table(levels):
    shape = (2 * levels, 2 * levels)
    source = lax.broadcasted_iota(jnp.int32, shape, 0)
    target = lax.broadcasted_iota(jnp.int32, shape, 1)
    step = source % levels - target % levels
    diff = jnp.where(step == 1, 1.0, jnp.where(step == -1, -1.0, 0.0))
    rim = (target % levels == 0) | (target % levels == levels - 1)
    twice = jnp.where(step == 0, jnp.where(rim, -1.0, -2.0), jnp.where(abs(step) == 2, 1.0, 0.0))
    from_press, to_press = source >= levels, target >= levels
    table = jnp.where(from_press, jnp.where(to_press, twice, diff), jnp.where(to_press, -10.0 * diff, 0.0))
    return table.astype(BF16)


def each_chunk(size, step, work):
    def turn(index, carry):
        work(pl.multiple_of(index * step, 8))
        return carry

    lax.fori_loop(0, size // step, turn, 0, unroll=True)


def natural(refs):
    own, chip, far, core = refs
    return [own, core, chip, far]


def put(refs, start, values):
    for ref, value in zip(refs, values):
        ref[pl.ds(start, value.shape[0])] = value


def merid_row(wind_ref, tile_ref, row, lines):
    half = 0.5 * WIND_COEF
    value = wind_ref[row, lines]
    if row < tile_ref.shape[0] - 1:
        value = value - half * tile_ref[row + 1, lines]
    return value + half * tile_ref[row - 1, lines] if row else value


def zonal_kernel(part, wind_ref, tile_ref, *refs):
    packs, zonal_ref = refs[:4], refs[4]
    rows, width, _ = tile_ref.shape
    levels = LANES // 2
    nlat = rows * lax.axis_size("lat")
    me = lax.axis_index("lon")
    first = lax.axis_index("lat") * rows
    place = lax.broadcasted_iota(jnp.int32, (width, LANES), 0)
    for row in range(rows):
        tile = tile_ref[row]
        after = jnp.where(place == width - 1, 0.0, pltpu.roll(tile, width - 1, 0))
        before = jnp.where(place == 0, 0.0, pltpu.roll(tile, 1, 0))
        scale = WIND_COEF / (2.0 * row_cosine(jnp.full((1, LANES), first + row), nlat))
        zonal_ref[row] = wind_ref[row] - pltpu.roll((after - before) * scale, levels, 1)

    size = chunk_of(width)
    masks = group_masks(size, part)

    def pack(start):
        lines = pl.ds(start, size)
        blocks = transpose_groups([zonal_ref[row, lines] for row in range(rows)], masks, part, range(4))
        put(packs, start, partner_order(blocks, me))

    each_chunk(width, size, pack)


def edge_kernel(part, *refs):
    (wind_first, wind_last), (tile_first, tile_last), (begin_ref, end_ref), packs = refs[:2], refs[2:4], refs[4:6], refs[6:]
    _, width, _ = tile_first.shape
    me = lax.axis_index("lon")
    half = 0.5 * WIND_COEF
    head = rim_lines(width)
    masks = group_masks(8, part)

    def pack(start):
        tiles = []
        for begin in (start, jnp.minimum(start + head, width - 8)):
            lines = pl.ds(pl.multiple_of(begin, 8), 8)
            tiles += [wind_first[0, lines] - half * tile_first[1, lines], tile_first[0, lines]]
            tiles += [wind_last[1, lines] + half * tile_last[0, lines], tile_last[1, lines]]
        return tiles

    def send_out(start, tiles):
        put(packs, start, partner_order(transpose_groups(tiles, masks, part, range(4, 8)), me))

    each_chunk(head - 8, 8, lambda start: send_out(start, pack(start)))
    line = lax.broadcasted_iota(jnp.int32, (8, LANES), 0)
    ends = []
    for row in range(4):
        inner = jnp.where(line == 1, pltpu.roll(begin_ref[row + 4], 1, 0), pltpu.roll(end_ref[row + 4], 7, 0))
        ends.append(jnp.where(line == 0, begin_ref[row], jnp.where(line == 7, end_ref[row], inner)))
    send_out(head - 8, pack(head - 8)[:4] + ends)


def rim_lines(width):
    return round_up(-(-width // 2), 8)


def fold_lines(width):
    return round_up(-(-width * 3 // 4), 8)


def press_kernel(part, wind_ref, tile_ref, _, *refs):
    packs, vert_ref = refs[:4], refs[4]
    rows, width, _ = tile_ref.shape
    levels = LANES // 2
    me = lax.axis_index("lon")
    masks8 = group_masks(8, part)
    head = fold_lines(width)
    tail = width - head

    def pack_merid(start, pair, fold=None):
        lines = pl.ds(start, 8)
        folded = pl.ds(start - pair * tail + head if fold is None else fold, 8)
        tiles = [merid_row(wind_ref, tile_ref, row, lines) for row in range(1, rows - 1)]
        one = merid_row(wind_ref, tile_ref, 2 * pair + 1, folded)
        two = merid_row(wind_ref, tile_ref, 2 * pair + 2, folded)
        blocks = transpose_groups([one] + tiles + [two], masks8, part, range(4, 8))
        put(packs, start, partner_order(blocks, me))

    for pair in range(3):
        each_chunk(tail, 8, lambda start: pack_merid(pl.multiple_of(start + pair * tail, 8), pair))
    for start in range(3 * tail, head, 8):
        pack_merid(start, 2, start)

    gain = jnp.where(lane_ids((1, LANES)) < levels, -0.5 * VERT_COEF, 0.25 * PRESS_COEF * VERT_COEF)
    table = levels_table(levels)
    dot = functools.partial(jnp.dot, preferred_element_type=F32)
    for row in range(rows):
        tile = tile_ref[row]
        high = tile.astype(BF16)
        rest = (tile - high.astype(F32)).astype(BF16)
        vert_ref[row] = tile + gain * (dot(high, table) + dot(rest, table))

    size = chunk_of(width)
    masks = group_masks(size, part)

    def pack(start):
        lines = pl.ds(start, size)
        blocks = transpose_groups([vert_ref[row, lines] for row in range(rows)], masks, part, range(4, 8))
        put(packs, pl.multiple_of(start + head, 8), partner_order(blocks, me))

    each_chunk(width, size, pack)


def turn_groups(value, groups, part):
    shift = groups * part % LANES
    return pltpu.roll(value, shift, 1) if shift else value


def rim_kernel(part, skip, flag_ref, cut_ref, *refs):
    blocks, north_ref, south_ref = natural(refs[:4]), refs[-2], refs[-1]
    lines = blocks[0].shape[0]
    first = lane_ids((lines, LANES)) // part % 4 < 2
    for half in range(2):
        one, two = blocks[2 * half][...], blocks[2 * half + 1][...]
        where = slice(half * lines, half * lines + lines)
        south_ref[where] = jnp.where(first, one, turn_groups(two, 2, part))
        north_ref[where] = jnp.where(first, turn_groups(two, -2, part), one)
    last = flag_ref.shape[0] - 1
    nlon = (skip - 8) * 4
    north_ref[2 * lines :] = jnp.full((8, LANES), cut_value(flag_ref, cut_ref, last, nlon), F32)
    south_ref[2 * lines :] = jnp.full((8, LANES), cut_value(flag_ref, cut_ref, 0, nlon), F32)


def edge_spec_kernel(bounds, part, skip, flag_ref, cut_ref, mode_ref, south_ref, north_ref, _, *refs):
    blocks, forward, spec_ref = natural(refs[:4]), refs[4:10], refs[10]
    lines = blocks[0].shape[0]
    width = skip - 8
    half = 0.5 * WIND_COEF
    item = lane_ids((lines, LANES)) // part % 4
    fields = []
    for quarter, block in enumerate(blocks):
        where = slice(quarter // 2 * lines, quarter // 2 * lines + lines)
        own, south, north = block[...], south_ref[where], north_ref[where]
        at = 0 if quarter % 2 else 2
        merid_s, press_s = turn_groups(south, 1 - at, part), turn_groups(south, -1 - at, part)
        merid_n, press_n = turn_groups(north, 1 + at, part), turn_groups(north, at - 1, part)
        inner = own + half * jnp.where(item == 0, press_s, -press_n)
        outer = jnp.where(item == 1, merid_s - half * own, merid_n + half * own)
        value = jnp.where(item % 2 == 0, inner, outer)
        fields.append(jnp.concatenate([value, turn_groups(value, -4, part)], 0)[:width])
    rows = flag_ref.shape[0]
    group = lane_ids((1, LANES)) // part
    cut = jnp.where(group == 0, cut_value(flag_ref, cut_ref, 0, 4 * width), cut_value(flag_ref, cut_ref, rows - 1, 4 * width))
    cut = jnp.where(group == 1, south_ref[2 * lines : 2 * lines + 1], cut)
    cut = jnp.where(group == 3, north_ref[2 * lines : 2 * lines + 1], cut)
    damp = damping(cut, mode_ref[:, 0:1])
    for (low, high), value in zip(bounds, forward_dft(fields, forward)):
        spec_ref[low:high] = value * damp[low:high]


def merid_spec_kernel(bounds, part, flag_ref, cut_ref, mode_ref, edge_ref, *refs):
    blocks, forward, inverse, outs, spec_ref = natural(refs[:4]), refs[4:10], refs[10:16], refs[16:20], refs[20]
    rows = flag_ref.shape[0]
    width = outs[0].shape[0]
    head = fold_lines(width)
    tail = width - head
    group = lane_ids((tail, LANES)) // part
    fields = []
    for block in blocks:
        out = None
        for pair in range(3):
            value = block[pair * tail : pair * tail + tail]
            one, two = turn_groups(value, 2 * pair + 1, part), turn_groups(value, 2 * pair + 3, part)
            both = jnp.where(group == 2 * pair + 1, one, two)
            out = both if pair == 0 else jnp.where(group > 2 * pair, both, out)
        fields.append(jnp.concatenate([block[:head], out], 0))
    damp = damping(lane_cut(flag_ref, cut_ref, 4 * width, part), mode_ref[:, 0:1])
    group = lane_ids((1, LANES)) // part
    parts = []
    for (low, high), value in zip(bounds, forward_dft(fields, forward)):
        edge = edge_ref[low:high]
        value = jnp.where(group == 0, edge, value * damp[low:high])
        parts.append(jnp.where(group == rows - 1, turn_groups(edge, rows - 3, part), value))
        spec_ref[low:high] = parts[-1]
    inverse_dft(parts, inverse, outs)


def dot3(table_high, table_low, value):
    high = value.astype(BF16)
    low = (value - high.astype(F32)).astype(BF16)
    width = value.shape[1]
    dot = functools.partial(jnp.dot, preferred_element_type=F32)
    both = dot(table_high[...], jnp.concatenate([high, low], 1))
    return both[:, :width] + both[:, width:] + dot(table_low[...], high)


def by_place(me, dif0, dif1):
    odd = lax.rem(me, 2) == 1
    sign = jnp.where(me >= 2, -1.0, 1.0).astype(F32)
    return jnp.where(odd, dif1, dif0) * sign, jnp.where(odd, dif0, dif1) * sign


def parity_sign(me):
    return jnp.where(lax.rem(me, 2) == 1, -1.0, 1.0).astype(F32)


def forward_dft(quarters, tables):
    me = lax.axis_index("lon")
    own, core, chip, far = quarters
    sum0, sum1 = own + chip, core + far
    dif0, dif1 = by_place(me, own - chip, core - far)
    return (
        dot3(tables[0], tables[1], sum0 + sum1),
        dot3(tables[2], tables[3], (sum0 - sum1) * parity_sign(me)),
        dot3(tables[4], tables[5], jnp.concatenate([dif0, dif1], 0)),
    )


def inverse_dft(parts, tables, outs):
    me = lax.axis_index("lon")
    even = dot3(tables[0], tables[1], parts[0])
    other = dot3(tables[2], tables[3], parts[1]) * parity_sign(me)
    both = dot3(tables[4], tables[5], parts[2])
    quarter = even.shape[0]
    dif0, dif1 = by_place(me, both[:quarter], both[quarter:])
    plus, minus = even + other, even - other
    outs[0][...] = plus + dif0
    outs[1][...] = minus + dif1
    outs[2][...] = plus - dif0
    outs[3][...] = minus - dif1


def lane_rows(pick, rows, part):
    group = lane_ids((1, LANES)) // part
    out = jnp.zeros((1, LANES), F32)
    for row in range(rows):
        out = jnp.where(group == row, pick(row), out)
    return out


def lane_cut(flag_ref, cut_ref, nlon, part):
    rows = flag_ref.shape[0]
    return lane_rows(lambda row: cut_value(flag_ref, cut_ref, row, nlon), rows, part)


def lane_cosine(shift, rows, part):
    row = lane_ids((1, LANES)) // part + lax.axis_index("lat") * rows + shift
    return row_cosine(row, rows * lax.axis_size("lat"))


def damping(cut, inv_wave):
    ratio = cut * inv_wave
    return jnp.minimum(1.0, ratio * ratio)


def zonal_spec_kernel(bounds, part, flag_ref, cut_ref, mode_ref, _, e0, e2, e3, e1, q0, q2, q3, q1, *refs):
    forward, inverse, outs, spec_ref = refs[:6], refs[6:12], refs[12:16], refs[16]
    rows = flag_ref.shape[0]
    width = outs[0].shape[0]
    me = lax.axis_index("lon")
    quarters = (q0, q1, q2, q3)
    scale = WIND_COEF / (2.0 * lane_cosine(0, rows, part))
    line = lax.broadcasted_iota(jnp.int32, (8, LANES), 0)
    low = lane_ids((8, LANES)) < LANES // 2
    sides = []
    for edge in (e0, e1, e2, e3):
        value = edge[edge.shape[0] - 8 :]
        inner = jnp.where(line == 0, pltpu.roll(value, 7, 0), pltpu.roll(value, 1, 0))
        sides.append(jnp.where(low, turn_groups(value, -4, part), inner))
    sides = partner_order(sides, me)
    starts = [jnp.where(line == 0, scale * pltpu.roll(sides[(q + 3) % 4], 1, 0), 0.0) for q in range(4)]
    ends = [jnp.where(line == 7, scale * pltpu.roll(sides[(q + 1) % 4], 7, 0), 0.0) for q in range(4)]
    starts, ends = partner_order(starts, me), partner_order(ends, me)
    fields = [
        jnp.concatenate([q[0:8] + start, q[8 : width - 8], q[width - 8 : width] - end], 0)
        for q, start, end in zip(quarters, starts, ends)
    ]
    damp = damping(lane_cut(flag_ref, cut_ref, 4 * width, part), mode_ref[:, 0:1])
    parts = [value * damp[b[0] : b[1]] for b, value in zip(bounds, forward_dft(fields, forward))]
    for (low, high), value in zip(bounds, parts):
        spec_ref[low:high] = value
    inverse_dft(parts, inverse, outs)


def press_back_kernel(bounds, part, flag_ref, cut_ref, mode_ref, zonal_ref, merid_ref, edge_ref, *refs):
    quarters, forward, inverse, outs = natural(refs[:4]), refs[4:10], refs[10:16], refs[16:]
    skip = quarters[0].shape[0] - outs[0].shape[0]
    rows = flag_ref.shape[0]
    nlon = 4 * inverse[0].shape[0]
    band = lax.axis_index("lat")
    mode = mode_ref[...]
    damp = damping(lane_cut(flag_ref, cut_ref, nlon, part), mode[:, 0:1])
    cosine = lane_cosine(0, rows, part)
    below = jnp.where(band == 0, 0.0, lane_cosine(-1, rows, part))
    above = jnp.where(band == lax.axis_size("lat") - 1, 0.0, lane_cosine(1, rows, part))
    half_inv = 0.5 / cosine
    group = lane_ids((1, LANES)) // part
    flux = merid_ref[...] * cosine
    edge = edge_ref[...]
    north = jnp.where(group == rows - 1, turn_groups(edge, rows - 4, part) * above, turn_groups(flux, -1, part))
    south = jnp.where(group == 0, turn_groups(edge, -1, part) * below, turn_groups(flux, 1, part))
    div_y = (north - south) * half_inv
    zonal = zonal_ref[...]
    slope = mode[:, 1:2] / cosine
    parts = []
    for (low, high), press in zip(bounds, forward_dft([q[skip:] for q in quarters], forward)):
        mid = (low + high) // 2
        swapped = jnp.concatenate([zonal[mid:high], zonal[low:mid]], 0)
        div = swapped * slope[low:high] + div_y[low:high]
        parts.append((press - PRESS_COEF * div) * damp[low:high])
    inverse_dft(parts, inverse, outs)


def winds_out_kernel(part, *refs):
    blocks, out_ref = natural(refs[:4]) + natural(refs[4:8]), refs[8]
    rows, width, _ = out_ref.shape
    me = lax.axis_index("lon")
    size = chunk_of(width)
    masks = group_masks(size, part)

    def unpack(start):
        lines = pl.ds(start, size)
        values = [ref[lines] for ref in blocks]
        values = partner_order(values[:4], me) + partner_order(values[4:], me)
        for row, value in enumerate(transpose_groups(values, masks, part, range(rows))):
            out_ref[row, lines] = value

    each_chunk(width, size, unpack)


def out_cuts(width):
    size = chunk_of(width)
    chunks = width // size
    return sorted({size * (chunks * part // 15) for part in (0, 6, 10, 13, 15)})


def press_out_kernel(part, _, tile_ref, *refs):
    blocks, out_hbm, tile_out, sems = natural(refs[:4]), refs[4], refs[5], refs[6]
    rows, width, _ = tile_ref.shape
    me = lax.axis_index("lon")
    size = chunk_of(width)
    masks = group_masks(size, part)
    low = lane_ids((size, LANES)) < LANES // 2
    cuts = out_cuts(width)
    copies = []
    for piece in range(len(cuts) - 1):
        begin, end = cuts[piece], cuts[piece + 1]

        def unpack(start):
            lines = pl.ds(start + begin, size)
            values = partner_order([ref[lines] for ref in blocks], me)
            for row, value in enumerate(gather_groups(values, masks, part)):
                tile_out[row, lines] = jnp.where(low, tile_ref[row, lines], value)

        each_chunk(end - begin, size, unpack)
        copy = pltpu.make_async_copy(tile_out.at[:, begin:end], out_hbm.at[:, begin:end, LANES:], sems.at[piece])
        copy.start()
        copies.append(copy)
    for copy in copies:
        copy.wait()


def whole(shape):
    return pl.BlockSpec(shape, lambda step: (0,) * len(shape))


def tile_of(shape, index):
    return pl.BlockSpec((shape[0], shape[1], LANES), lambda step: (0, 0, index))


SMEM = pl.BlockSpec(memory_space=pltpu.SMEM)
ANY = pl.BlockSpec(memory_space=pl.ANY)


def call(kernel, out_shape, in_specs, out_specs, cost=2, grid=(1,), **more):
    return pl.pallas_call(
        kernel,
        grid=grid,
        out_shape=out_shape,
        in_specs=in_specs,
        out_specs=out_specs,
        compiler_params=pltpu.CompilerParams(vmem_limit_bytes=VMEM_BYTES),
        cost_estimate=pl.CostEstimate(flops=int(cost * 1.15e9), bytes_accessed=int(cost * 3.69e6), transcendentals=0),
        **more,
    )


def f32(*shape):
    return jax.ShapeDtypeStruct(shape, F32)


def send(block, step):
    return lax.ppermute(block, "lon", [(i, i ^ step) for i in range(4)])


def exchange(blocks):
    return [blocks[0]] + [send(blocks[step], step) for step in (2, 3, 1)]


def packed_body(state, filter_flag, cutoff):
    rows, width, depth = state.shape
    levels = depth // 4
    bands = lax.axis_size("lat")
    nlon = 4 * width
    part = levels // 4
    forward, inverse, mode, sizes = spectral_plan(nlon)
    forward = [jnp.asarray(t) for t in forward]
    inverse = [jnp.asarray(t) for t in inverse]
    mode = jnp.asarray(mode)
    bounds, at = [], 0
    for size in sizes:
        bounds.append((at, at + 2 * size))
        at += 2 * size
    table_specs = [whole(t.shape) for t in forward] + [whole(t.shape) for t in inverse]
    block, spectrum, full = (width, LANES), (at, LANES), (rows, width, LANES)
    skip = width + 8
    second = (fold_lines(width) + width, LANES)
    rims = (2 * rim_lines(width) + 8, LANES)
    low_tile, high_tile = tile_of(state.shape, 0), tile_of(state.shape, 1)

    edges = (rim_lines(width), LANES)

    def two_rows(row, index):
        return pl.BlockSpec((2, width, LANES), lambda step: (row, 0, index))

    def end_lines(index):
        return pl.BlockSpec((rows, 8, LANES), lambda step: (0, index, 1))

    edge_packs = call(
        functools.partial(edge_kernel, part),
        [f32(*edges)] * 4,
        [two_rows(0, 0), two_rows(rows // 2 - 1, 0), two_rows(0, 1), two_rows(rows // 2 - 1, 1)] + [end_lines(0), end_lines(width // 8 - 1)],
        [whole(edges)] * 4,
    )(*[state] * 6)
    zonal_packs = call(
        functools.partial(zonal_kernel, part),
        [f32(*block)] * 4,
        [low_tile, high_tile],
        [whole(block)] * 4,
        scratch_shapes=[pltpu.VMEM(full, F32)],
    )(state, state)
    edge_circle = exchange(edge_packs)
    first_circle = exchange(zonal_packs)
    *packs, vert = call(
        functools.partial(press_kernel, part),
        [f32(*second)] * 4 + [f32(*full)],
        [low_tile, high_tile, ANY],
        [whole(second)] * 4 + [whole(full)],
    )(state, state, edge_circle[1])
    second_circle = exchange(packs)

    edge_specs = [whole(edges)] * 4
    to_north, to_south = call(
        functools.partial(rim_kernel, part, skip),
        [f32(*rims)] * 2,
        [SMEM] * 2 + edge_specs + [ANY],
        [whole(rims)] * 2,
        cost=8,
    )(filter_flag, cutoff, *edge_circle, vert)
    from_south = lax.ppermute(to_north, "lat", [(i, i + 1) for i in range(bands - 1)])
    from_north = lax.ppermute(to_south, "lat", [(i + 1, i) for i in range(bands - 1)])

    *zonal_parts, zonal_spec = call(
        functools.partial(zonal_spec_kernel, bounds, part),
        [f32(*block)] * 4 + [f32(*spectrum)],
        [SMEM] * 2 + [whole(mode.shape), ANY] + [whole(edges)] * 4 + [whole(block)] * 4 + table_specs,
        [whole(block)] * 4 + [whole(spectrum)],
    )(filter_flag, cutoff, mode, second_circle[3], *edge_circle, *first_circle, *forward, *inverse)
    zonal_back = exchange(zonal_parts)
    edge_spec = call(
        functools.partial(edge_spec_kernel, bounds, part, skip),
        f32(*spectrum),
        [SMEM] * 2 + [whole(mode.shape)] + [whole(rims)] * 2 + [ANY] + edge_specs + table_specs[:6],
        whole(spectrum),
    )(filter_flag, cutoff, mode, from_south, from_north, zonal_spec, *edge_circle, *forward)

    *merid_parts, merid_spec = call(
        functools.partial(merid_spec_kernel, bounds, part),
        [f32(*block)] * 4 + [f32(*spectrum)],
        [SMEM] * 2 + [whole(mode.shape), whole(spectrum)] + [whole(second)] * 4 + table_specs,
        [whole(block)] * 4 + [whole(spectrum)],
    )(filter_flag, cutoff, mode, edge_spec, *second_circle, *forward, *inverse)
    merid_back = exchange(merid_parts)

    press_parts = call(
        functools.partial(press_back_kernel, bounds, part),
        [f32(*block)] * 4,
        [SMEM] * 2 + [whole(mode.shape)] + [whole(spectrum)] * 3 + [whole(second)] * 4 + table_specs,
        [whole(block)] * 4,
    )(filter_flag, cutoff, mode, zonal_spec, merid_spec, edge_spec, *second_circle, *forward, *inverse)
    press_back = exchange(press_parts)

    out = call(
        functools.partial(winds_out_kernel, part),
        f32(*state.shape),
        [whole(block)] * 8,
        low_tile,
    )(*zonal_back, *merid_back)
    pieces = len(out_cuts(width)) - 1
    return call(
        functools.partial(press_out_kernel, part),
        f32(*state.shape),
        [ANY, whole(full)] + [whole(block)] * 4,
        ANY,
        scratch_shapes=[pltpu.VMEM(full, F32), pltpu.SemaphoreType.DMA((pieces,))],
        input_output_aliases={0: 0},
    )(out, vert, *press_back)


def padded_2(block, sides, width, periodic):
    for axis, dim in sides:
        count = lax.axis_size(axis)
        forward = [(i, i + 1) for i in range(count - 1)]
        if periodic:
            forward.append((count - 1, 0))
        backward = [(target, source) for source, target in forward]
        low = lax.ppermute(
            lax.slice_in_dim(block, block.shape[dim] - width, None, axis=dim), axis, forward
        )
        high = lax.ppermute(lax.slice_in_dim(block, 0, width, axis=dim), axis, backward)
        block = jnp.concatenate([low, block, high], axis=dim)
    return block


def dft_tables(width):
    points = jnp.arange(width, dtype=jnp.int32)
    waves = jnp.arange(width // 2 + 1, dtype=jnp.int32)
    phase = points[:, None] * waves[None, :] % width
    angle = phase.astype(jnp.float32) * (2.0 * math.pi / width)
    weights = jnp.where((waves == 0) | (waves * 2 == width), 1.0, 2.0).astype(jnp.float32) / width
    return (jnp.cos(angle), jnp.sin(angle), weights)


def rims(stack):
    wide = padded_2(stack, (("lon", 1),), 1, True)
    return padded_2(wide, (("lat", 0),), 1, False)


def level_diff(field):
    padded = jnp.pad(field, ((0, 0), (0, 0), (1, 1)))
    return 0.5 * (padded[:, :, 2:] - padded[:, :, :-2])


def damped(block, cut_vec, tables):
    cos_table, sin_table, weights = tables
    highest = lax.Precision.HIGHEST
    wave_vals = jnp.arange(cos_table.shape[1]).astype(jnp.float32)
    ratio = cut_vec[:, None] / jnp.maximum(wave_vals, 1.0)[None, :]
    damping = (jnp.minimum(1.0, ratio * ratio) * weights[None, :])[:, None, :]
    real_part = jnp.einsum("rnq,nk->rqk", block, cos_table, precision=highest)
    imag_part = jnp.einsum("rnq,nk->rqk", block, sin_table, precision=highest)
    restored = jnp.einsum("rqk,nk->rnq", real_part * damping, cos_table, precision=highest)
    return restored + jnp.einsum("rqk,nk->rnq", imag_part * damping, sin_table, precision=highest)


def circle_local(fields, cut_rows, tables):
    return damped(fields, cut_rows, tables)


def polar(fields, row_flag, cut_rows, tables, apply):
    smooth = apply(fields, cut_rows, tables)
    return jnp.where(row_flag[:, None, None], smooth, fields)


def plain_body(state, filter_flag, cutoff):
    rows, width, depth = state.shape
    levels = depth // 4
    zonal_wind = state[:, :, :levels]
    merid_wind = state[:, :, levels : 2 * levels]
    vert_wind = state[:, :, 2 * levels : 3 * levels]
    pressure = state[:, :, 3 * levels :]
    nlat = rows * lax.axis_size("lat")
    nlon = width * lax.axis_size("lon")
    offset = lax.axis_index("lat") * rows
    row_ids = (offset + jnp.arange(-1, rows + 1)).astype(jnp.float32)
    cos_ext = jnp.cos(-0.5 * math.pi + (row_ids + 0.5) * math.pi / nlat)
    cos_mid = cos_ext[1:-1][:, None, None]
    tables = dft_tables(nlon)
    row_flag = filter_flag == 1
    cut_rows = cutoff.astype(jnp.float32)
    padded = rims(pressure)
    grad_x = (padded[1:-1, 2:] - padded[1:-1, :-2]) / (2.0 * cos_mid)
    grad_y = 0.5 * (padded[2:, 1:-1] - padded[:-2, 1:-1])
    grad_z = level_diff(pressure)
    zonal_pre = zonal_wind - WIND_COEF * grad_x
    merid_pre = merid_wind - WIND_COEF * grad_y
    vert_new = vert_wind - VERT_COEF * grad_z
    div_z = level_diff(vert_new)
    outgoing = jnp.stack([zonal_pre, merid_pre, pressure, div_z], 3).reshape(
        rows, width, 4 * levels
    )
    circles = lax.all_to_all(outgoing, "lon", split_axis=2, concat_axis=1, tiled=True)
    part_levels = circles.shape[2] // 4
    circles = circles.reshape(rows, nlon, part_levels, 4)
    winds_c = jnp.concatenate([circles[:, :, :, 0], circles[:, :, :, 1]], 2)
    press_c = circles[:, :, :, 2]
    div_z_c = circles[:, :, :, 3]
    winds_c = polar(winds_c, row_flag, cut_rows, tables, circle_local)
    zonal_c = winds_c[:, :, :part_levels]
    merid_c = winds_c[:, :, part_levels:]
    div_x = (jnp.roll(zonal_c, -1, 1) - jnp.roll(zonal_c, 1, 1)) / (2.0 * cos_mid)
    flux = padded_2(merid_c * cos_mid, (("lat", 0),), 1, False)
    div_y = (flux[2:] - flux[:-2]) / (2.0 * cos_mid)
    press_mid = press_c - PRESS_COEF * (div_x + div_y + div_z_c)
    press_c = polar(press_mid, row_flag, cut_rows, tables, circle_local)
    back = jnp.stack([zonal_c, merid_c, press_c], 3).reshape(rows, nlon, 3 * part_levels)
    patches = lax.all_to_all(back, "lon", split_axis=1, concat_axis=2, tiled=True).reshape(
        rows, width, levels, 3
    )
    return jnp.concatenate(
        [patches[:, :, :, 0], patches[:, :, :, 1], vert_new, patches[:, :, :, 2]], 2
    )


def body(state, filter_flag, cutoff):
    rows, width, depth = state.shape
    levels = depth // 4
    lanes_fit = rows == 8 and 2 * levels == LANES and width % 16 == 8
    if lax.axis_size("lon") == 4 and lanes_fit:
        return packed_body(state, filter_flag, cutoff)
    return plain_body(state, filter_flag, cutoff)


def solution(mesh):
    return jax.shard_map(
        body,
        mesh=mesh,
        in_specs=(P("lat", "lon", None), P("lat"), P("lat")),
        out_specs=P("lat", "lon", None),
        check_vma=False,
    )
```
